32 devices in a mesh: dp: 2 (over y), fsdp: 16 (over z, x, core).
Axes of the slice: x: 2, y: 2, z: 4, core: 2. Of those that a mesh axis runs over, the one named last changes fastest.
Arguments:
- patches: bfloat16 [2, 32, 529, 768], P(None, ('dp', 'fsdp')), may hold values from -6 to 6
- visible_index: int32 [2, 32, 400], P(None, ('dp', 'fsdp')), may hold values from 0 to 528, as said below
- visible_count: int32 [2, 32], P(None, ('dp', 'fsdp')), may hold values from 389 to 400, as said below
- qkv_weight: bfloat16 [768, 2304], P(('dp', 'fsdp')), may hold values from -0.21875 to 0.21875
- out_weight: bfloat16 [768, 768], P(('dp', 'fsdp')), may hold values from -3.5 to 3.5
- up_weight: bfloat16 [768, 3072], P(('dp', 'fsdp')), may hold values from -0.21875 to 0.21875
- down_weight: bfloat16 [3072, 768], P(('dp', 'fsdp')), may hold values from -0.109375 to 0.109375
- attention_gain: bfloat16 [768], P(('dp', 'fsdp')), may hold values from 0.5 to 1.5
- attention_shift: bfloat16 [768], P(('dp', 'fsdp')), may hold values from -3 to 3
- feedforward_gain: bfloat16 [768], P(('dp', 'fsdp')), may hold values from 0.5 to 1.5
- feedforward_shift: bfloat16 [768], P(('dp', 'fsdp')), may hold values from -3 to 3
- cotangent: bfloat16 [2, 32, 400, 768], P(None, ('dp', 'fsdp')), may hold values from -6 to 6
Outputs:
- layer_output: float32 [2, 32, 400, 768], P(None, ('dp', 'fsdp'))
- patch_gradient: float32 [2, 32, 529, 768], P(None, ('dp', 'fsdp'))
- qkv_gradient: float32 [768, 2304], P(('dp', 'fsdp'))
- out_gradient: float32 [768, 768], P(('dp', 'fsdp'))
- up_gradient: float32 [768, 3072], P(('dp', 'fsdp'))
- down_gradient: float32 [3072, 768], P(('dp', 'fsdp'))
- attention_gain_gradient: float32 [768], P(('dp', 'fsdp'))
- attention_shift_gradient: float32 [768], P(('dp', 'fsdp'))
- feedforward_gain_gradient: float32 [768], P(('dp', 'fsdp'))
- feedforward_shift_gradient: float32 [768], P(('dp', 'fsdp'))
The draws below stay inside these ranges and needn't reach their ends.
Inputs may be any that keep to these rules, and one draw needn't show every extreme that they name: `visible_index`: in each strip the first visible_count entries are the numbers of the visible patches in increasing order, each once; the other entries are numbers of masked patches. Masked patches gather near the start of the strip. `visible_count`: in each micro-batch some strip has exactly 400 visible patches.
All inputs are finite; a program needn't handle non-finite values.
Results may differ from the reference program's by a relative error of at most 0.012.
Values may be sent and summed in bfloat16 or wider, within the bound.
A program may use at most 192 MiB of HBM per device.

```python
import jax
import jax.numpy as jnp
from jax import lax

D = 768
HEADS = 12
HEAD = 64
FF = 3072
PATCHES = 529
VIS = 400
MICRO = 2
STRIPS = 32


def masked_layout(key):
    draw_keys = jax.random.split(key, 4)
    shortfall = jax.random.randint(draw_keys[0], (MICRO, STRIPS), 0, 12)
    chosen = jax.random.randint(draw_keys[1], (MICRO,), 0, STRIPS)
    shortfall = jnp.where(jnp.arange(STRIPS)[None, :] == chosen[:, None], 0, shortfall)
    counts = (VIS - shortfall).astype(jnp.int32)
    span_length = jax.random.randint(draw_keys[2], (MICRO, STRIPS), 1, 7)
    positions = jnp.arange(PATCHES)
    group_ids = positions[None, None, :] // span_length[:, :, None]
    noise = jax.random.randint(draw_keys[3], (MICRO, STRIPS, PATCHES), 0, 4096)
    group_noise = jnp.take_along_axis(noise, group_ids, axis=2)
    rising = max(8192 // PATCHES, 1)
    priority = (group_noise + group_ids * span_length[:, :, None] * rising) * PATCHES + positions[None, None, :]
    ranking = jnp.argsort(jnp.argsort(priority, axis=2), axis=2)
    masked = (ranking < (PATCHES - counts)[:, :, None]).astype(jnp.int32)
    ordering = jnp.argsort(masked * PATCHES + positions[None, None, :], axis=2)
    return (ordering[:, :, :VIS].astype(jnp.int32), counts)


def draw_visible_index(key, part):
    layout = masked_layout(key)
    return layout[0]


def draw_visible_count(key, part):
    layout = masked_layout(key)
    return layout[1]


def levels(key, shape, shards, smallest, largest):
    factor_of, own = 1.0, jax.random.fold_in(key, 6)
    for dim, shards_of in shards:
        draws = jnp.exp(jax.random.uniform(jax.random.fold_in(own, dim), (shards_of,), jnp.float32, smallest / len(shards), largest / len(shards)))
        factor_of = factor_of * jnp.repeat(draws, shape[dim] // shards_of).reshape([-1 if axis == dim else 1 for axis in range(len(shape))])
    return factor_of


def gaussian(stream_key, extent, spread, reach, shards=(), held_as=jnp.bfloat16):
    array = spread * jax.random.normal(stream_key, extent, jnp.float32)
    if shards:
        array = array * levels(stream_key, extent, shards, -0.22, 0.18)
    return jnp.clip(array, -reach, reach).astype(held_as)


def setup_inputs(seed: int = 0) -> dict:
    arg_keys = jax.random.split(jax.random.key(seed), 13)
    return {
        "patches": gaussian(arg_keys[0], (MICRO, STRIPS, PATCHES, D), 1.0, 6.0, ((1, 32),)),
        "visible_index": draw_visible_index(jax.random.fold_in(arg_keys[12], 71), 0),
        "visible_count": draw_visible_count(jax.random.fold_in(arg_keys[12], 71), 0),
        "qkv_weight": gaussian(arg_keys[3], (D, 3 * D), D ** -0.5, 0.21875, ((0, 32),)),
        "out_weight": gaussian(arg_keys[4], (D, D), (max(2 * D // VIS, 1)) ** -0.5, 3.5, ((0, 32),)),
        "up_weight": gaussian(arg_keys[5], (D, FF), D ** -0.5, 0.21875, ((0, 32),)),
        "down_weight": gaussian(arg_keys[6], (FF, D), FF ** -0.5, 0.109375, ((0, 32),)),
        "attention_gain": jnp.clip(1.0 + 0.1 * jax.random.normal(arg_keys[7], (D,), jnp.float32), 0.5, 1.5).astype(jnp.bfloat16),
        "attention_shift": gaussian(arg_keys[8], (D,), 0.3, 3.0, ((0, 32),)),
        "feedforward_gain": jnp.clip(1.0 + 0.1 * jax.random.normal(arg_keys[9], (D,), jnp.float32), 0.5, 1.5).astype(jnp.bfloat16),
        "feedforward_shift": gaussian(arg_keys[10], (D,), 0.3, 3.0, ((0, 32),)),
        "cotangent": gaussian(arg_keys[11], (MICRO, STRIPS, VIS, D), 1.0, 6.0, ((1, 32),)),
    }


@jax.custom_vjp
def low(v):
    return lax.optimization_barrier(v.astype(jnp.bfloat16)).astype(jnp.float32)

@jax.custom_vjp
def low_back(v):
    return v

def low_keep(v):
    return (low(v), None)

def low_pass(kept, grad):
    return (grad,)

def back_keep(v):
    return (v, None)

def back_low(kept, grad):
    return (low(grad),)
low.defvjp(low_keep, low_pass)
low_back.defvjp(back_keep, back_low)
highest = lax.Precision.HIGHEST
masked_score = -1000000000.0
norm_epsilon = 1e-06

def norm_rows(features, scaling, offset):
    center = features - lax.optimization_barrier(jnp.mean(features, axis=-1, keepdims=True))
    inverse = lax.rsqrt(lax.optimization_barrier(jnp.mean(center * center, axis=-1, keepdims=True)) + norm_epsilon)
    return center * inverse * scaling + offset

def strip_layer(params, patch_rows, indices, counts):
    qkv_full, out_full, up_full, down_full, first_gain, first_shift, second_gain, second_shift = params
    present = jnp.arange(VIS) < counts
    onehot = ((indices[:, None] == jnp.arange(PATCHES)[None, :]) & present[:, None]).astype(patch_rows.dtype)
    inputs = low_back(jnp.dot(onehot, patch_rows, precision=highest))
    first_low = low(norm_rows(inputs, first_gain, first_shift))
    projected = low_back(low(jnp.dot(first_low, qkv_full, precision=highest)))
    queries = projected[:, :D].reshape(VIS, HEADS, HEAD)
    keys_all = projected[:, D:2 * D].reshape(VIS, HEADS, HEAD)
    values_all = projected[:, 2 * D:].reshape(VIS, HEADS, HEAD)
    scores = jnp.einsum('qhe,khe->hqk', queries, keys_all, precision=highest) * HEAD ** (-0.5)
    scores = low_back(jnp.where(present[None, None, :], scores, masked_score))
    attention = jax.nn.softmax(scores, axis=-1)
    mixed_heads = jnp.einsum('hqk,khe->qhe', low(attention), values_all, precision=highest).reshape(VIS, D)
    mixed_heads = low_back(low(mixed_heads))
    middle = inputs + low_back(jnp.dot(mixed_heads, out_full, precision=highest))
    second_low = low(norm_rows(middle, second_gain, second_shift))
    hidden_pre = low_back(jnp.dot(second_low, up_full, precision=highest))
    hidden_low = low(jax.nn.gelu(hidden_pre, approximate=False))
    branch = low_back(jnp.dot(hidden_low, down_full, precision=highest))
    return (middle + branch) * present[:, None].astype(middle.dtype)

def forward(params, patches, visible_index, visible_count):
    strip_step = jax.checkpoint(strip_layer)

    def advance(state_none, item):
        return (state_none, strip_step(params, item[0], item[1], item[2]))
    items = (patches.reshape(MICRO * STRIPS, PATCHES, D), visible_index.reshape(MICRO * STRIPS, VIS), visible_count.reshape(MICRO * STRIPS))
    state_none, outputs = lax.scan(advance, jnp.zeros((), patches.dtype), items)
    return outputs.reshape(MICRO, STRIPS, VIS, D)

def reference(patches, visible_index, visible_count, qkv_weight, out_weight, up_weight, down_weight, attention_gain, attention_shift, feedforward_gain, feedforward_shift, cotangent):
    params = tuple((weight.astype(jnp.float32) for weight in (qkv_weight, out_weight, up_weight, down_weight, attention_gain, attention_shift, feedforward_gain, feedforward_shift)))

    def whole(values_in, patch_values):
        return forward(values_in, patch_values, visible_index, visible_count)
    layer_output, pullback = jax.vjp(whole, params, patches.astype(jnp.float32))
    grads_all, patch_gradient = pullback(cotangent.astype(jnp.float32))
    return (layer_output, patch_gradient, grads_all[0], grads_all[1], grads_all[2], grads_all[3], grads_all[4], grads_all[5], grads_all[6], grads_all[7])
```

```python
import jax
import jax.numpy as jnp
from jax import lax
from jax.experimental import pallas as pl
from jax.experimental.pallas import tpu as pltpu
from jax.sharding import PartitionSpec as P

HEADS = 12
AXES = ("dp", "fsdp")
MASKED = -1000000000.0
EPSILON = 1e-06
F32 = jnp.float32
BF16 = jnp.bfloat16


def norm_forward(features, scaling, offset):
    center = features - jnp.mean(features, axis=-1, keepdims=True)
    inverse = lax.rsqrt(jnp.mean(center * center, axis=-1, keepdims=True) + EPSILON)
    normed = center * inverse
    return (normed * scaling.astype(F32) + offset.astype(F32), normed, inverse)


def norm_backward(upstream, normed, inverse, scaling):
    through = upstream * scaling.astype(F32)
    inward = inverse * (
        through
        - jnp.mean(through, axis=-1, keepdims=True)
        - normed * jnp.mean(through * normed, axis=-1, keepdims=True)
    )
    return (inward, jnp.sum(upstream * normed, axis=0), jnp.sum(upstream, axis=0))


def sums(equation, left, right):
    return jnp.einsum(equation, left, right, preferred_element_type=F32)


def layer(weights, patches, indices, counts, cotangent):
    qkv_full, out_full, up_full, down_full, first_gain, first_shift, second_gain, second_shift = weights
    strips, visible, patch_count = (indices.shape[0], indices.shape[1], patches.shape[1])
    width = out_full.shape[1]
    rows = strips * visible
    heads = (strips, visible, HEADS, width // HEADS)
    scale = (width // HEADS) ** (-0.5)
    present = jnp.arange(visible)[None, :] < counts[:, None]
    onehot = ((indices[:, :, None] == jnp.arange(patch_count)[None, None, :]) & present[:, :, None]).astype(BF16)
    inputs = sums("bvp,bpd->bvd", onehot, patches).reshape(rows, width)
    first_norm, first_normed, first_inverse = norm_forward(inputs, first_gain, first_shift)
    first_low = first_norm.astype(BF16)
    projected = jnp.dot(first_low, qkv_full, preferred_element_type=F32).astype(BF16)
    queries = projected[:, :width].reshape(heads)
    keys = projected[:, width : 2 * width].reshape(heads)
    values = projected[:, 2 * width :].reshape(heads)
    scores = sums("bqhe,bkhe->bhqk", queries, keys) * scale
    scores = jnp.where(present[:, None, None, :], scores, MASKED)
    attention = jax.nn.softmax(scores, axis=-1)
    attention_low = attention.astype(BF16)
    mixed = sums("bhqk,bkhe->bqhe", attention_low, values).astype(BF16).reshape(rows, width)
    middle = inputs + jnp.dot(mixed, out_full, preferred_element_type=F32)
    second_norm, second_normed, second_inverse = norm_forward(middle, second_gain, second_shift)
    second_low = second_norm.astype(BF16)
    hidden_pre = jnp.dot(second_low, up_full, preferred_element_type=F32)
    hidden, gelu_pull = jax.vjp(lambda v: jax.nn.gelu(v, approximate=False), hidden_pre)
    hidden_low = hidden.astype(BF16)
    branch = jnp.dot(hidden_low, down_full, preferred_element_type=F32)
    live = present.reshape(rows, 1)
    output = ((middle + branch) * live.astype(F32)).reshape(strips, visible, width)

    upstream = cotangent.reshape(rows, width) * live.astype(BF16)
    down_grad = sums("rf,rd->fd", hidden_low, upstream)
    pre_low = gelu_pull(sums("rd,fd->rf", upstream, down_full))[0].astype(BF16)
    up_grad = sums("rf,rd->fd", second_low, pre_low)
    second_back = sums("rd,fd->rf", pre_low, up_full)
    inward, second_gain_grad, second_shift_grad = norm_backward(second_back, second_normed, second_inverse, second_gain)
    middle_grad = upstream.astype(F32) + inward
    middle_low = middle_grad.astype(BF16)
    out_grad = sums("rf,rd->fd", mixed, middle_low)
    mixed_grad = sums("rd,fd->rf", middle_low, out_full).astype(BF16).reshape(heads)
    prob_grad = sums("bqhe,bkhe->bhqk", mixed_grad, values)
    value_grad = sums("bhqk,bqhe->bkhe", attention_low, mixed_grad)
    score_low = (attention * (prob_grad - jnp.sum(attention * prob_grad, axis=-1, keepdims=True))).astype(BF16)
    query_grad = sums("bhqk,bkhe->bqhe", score_low, keys) * scale
    key_grad = sums("bhqk,bqhe->bkhe", score_low, queries) * scale
    projected_grad = jnp.concatenate([g.reshape(rows, width) for g in (query_grad, key_grad, value_grad)], axis=1).astype(BF16)
    qkv_grad = sums("rf,rd->fd", first_low, projected_grad)
    first_back = sums("rd,fd->rf", projected_grad, qkv_full)
    inward, first_gain_grad, first_shift_grad = norm_backward(first_back, first_normed, first_inverse, first_gain)
    input_low = (middle_grad + inward).astype(BF16).reshape(strips, visible, width)
    patch_part = sums("bvp,bvd->bpd", onehot, input_low)
    gradients = (qkv_grad, out_grad, up_grad, down_grad, first_gain_grad, first_shift_grad, second_gain_grad, second_shift_grad)
    return (output, gradients, patch_part)


def any_slice(patches, visible_index, visible_count, *rest):
    weights, cotangent = rest[:-1], rest[-1]
    whole = [lax.all_gather(w, AXES, axis=0, tiled=True) for w in weights]
    micro, strips = patches.shape[:2]
    flat = lambda a: a.reshape((micro * strips,) + a.shape[2:])
    output, gradients, patch_part = layer(whole, flat(patches), flat(visible_index), flat(visible_count), flat(cotangent))
    shares = [lax.psum_scatter(g, AXES, scatter_dimension=0, tiled=True) for g in gradients]
    back = lambda a: a.reshape((micro, strips) + a.shape[1:])
    return (back(output), back(patch_part), *shares)


MESH = pl.DeviceIdType.MESH
EXT = 128
ROUNDS = 6


def coords():
    y = lax.axis_index("dp")
    f = lax.axis_index("fsdp")
    return y, f // 4, (f // 2) % 2, f % 2


def device(y, z, x, c):
    return (y, z * 4 + x * 2 + c)


def blocks(refs, rnd, par):
    first, second, third = refs
    if rnd == 0:
        return lambda *at: first.at[(par,) + at]
    if rnd < 4:
        return lambda *at: second.at[(2 * (rnd - 1) + par,) + at]
    return lambda yy, zz, xx, *at: third.at[(yy, zz, xx, 2 * par + (rnd - 4)) + at]


def cut(rnd):
    return 384, (512 if rnd == 0 else 384)


ALL = slice(None)


def other(z, dz):
    if dz == 0:
        return z
    if dz == 1:
        return z + 1 - 2 * (z % 2)
    if dz == 2:
        return (z + 2) % 4
    return 3 - z


class Gather:
    def __init__(self, place, weights, sems):
        self.place = place
        self.weights = weights
        self.sems = sems

    def copy(self, kind, i, src, dst, to):
        send, recv = self.sems[kind]
        return pltpu.make_async_remote_copy(src_ref=src, dst_ref=dst, send_sem=send.at[i], recv_sem=recv.at[i], device_id=to, device_id_type=MESH)

    def z(self, j, dz):
        y, z, x, c = self.place
        at = blocks(self.weights, j, c)
        return self.copy("z", (j, dz - 1), at(y, z, x), at(y, z, x), device(y, other(z, dz), x, c))

    def z_in(self, j, dz):
        y, z, x, c = self.place
        at = blocks(self.weights, j, c)
        there = at(y, other(z, dz), x)
        return self.copy("z", (j, dz - 1), there, there, device(y, other(z, dz), x, c))

    def side(self, j, dz, axis):
        y, z, x, c = self.place
        at = blocks(self.weights, j, c)
        src = at(y, other(z, dz), x)
        to = device(y, z, 1 - x, c) if axis == "x" else device(1 - y, z, x, c)
        return self.copy(axis, (j, dz), src, src, to)

    def side_in(self, j, dz, axis):
        y, z, x, c = self.place
        at = blocks(self.weights, j, c)
        there = at(y, other(z, dz), 1 - x) if axis == "x" else at(1 - y, other(z, dz), x)
        to = device(y, z, 1 - x, c) if axis == "x" else device(1 - y, z, x, c)
        return self.copy(axis, (j, dz), there, there, to)

    def diag(self, j, half):
        y, z, x, c = self.place
        at = blocks(self.weights, j, c)
        na, nb = cut(j)
        if half == 0:
            src = at(y, ALL, 1 - x, ALL, pl.ds(0, na))
            to = device(1 - y, z, x, c)
        else:
            src = at(1 - y, ALL, x, ALL, pl.ds(na, nb))
            to = device(y, z, 1 - x, c)
        return self.copy("g", (j, half), src, src, to)

    def diag_in(self, j, half):
        y, z, x, c = self.place
        at = blocks(self.weights, j, c)
        na, nb = cut(j)
        there = at(1 - y, ALL, 1 - x, ALL, pl.ds(0, na) if half == 0 else pl.ds(na, nb))
        to = device(1 - y, z, x, c) if half == 0 else device(y, z, 1 - x, c)
        return self.copy("g", (j, half), there, there, to)

    def down(self, j, q, par=None):
        y, z, x, c = self.place
        at = blocks(self.weights, j, c if par is None else par)
        yy = y if q < 2 else 1 - y
        xx = x if q % 2 == 0 else 1 - x
        src = at(yy, ALL, xx)
        return self.copy("d", (j, q), src, src, device(y, z, x, 1 - c))

    def down_in(self, j, q):
        return self.down(j, q, 1 - self.place[3])

    def begin(self, j):
        for dz in (1, 2, 3):
            self.z(j, dz).start()
        self.side(j, 0, "x").start()
        self.side(j, 0, "y").start()

    def forward(self, j):
        for dz in (1, 2, 3):
            self.z_in(j, dz).wait_recv()
            self.side(j, dz, "x").start()
            self.side(j, dz, "y").start()
        self.down(j, 0).start()

    def cross(self, j):
        for dz in range(4):
            self.side_in(j, dz, "x").wait_recv()
        self.diag(j, 0).start()
        self.down(j, 1).start()
        for dz in range(4):
            self.side_in(j, dz, "y").wait_recv()
        self.diag(j, 1).start()
        self.down(j, 2).start()

    def finish(self, j):
        self.diag_in(j, 0).wait_recv()
        self.diag_in(j, 1).wait_recv()
        self.down(j, 3).start()

    def arrive(self, j):
        for q in range(4):
            self.down_in(j, q).wait_recv()

    def sent(self, j):
        for dz in (1, 2, 3):
            self.z(j, dz).wait_send()
        for dz in range(4):
            self.side(j, dz, "x").wait_send()
            self.side(j, dz, "y").wait_send()
        self.diag(j, 0).wait_send()
        self.diag(j, 1).wait_send()
        for q in range(4):
            self.down(j, q).wait_send()


GATHER_SEMS = {"z": 3, "x": 4, "y": 4, "g": 2, "d": 4}


class Scatter:
    def __init__(self, place, sums, bufs, sems):
        self.place = place
        self.sums = sums
        self.bufs = bufs
        self.sems = sems

    def copy(self, kind, i, src, dst, to):
        send, recv = self.sems[kind]
        return pltpu.make_async_remote_copy(src_ref=src, dst_ref=dst, send_sem=send.at[i], recv_sem=recv.at[i], device_id=to, device_id_type=MESH)

    def a(self, j):
        y, z, x, c = self.place
        src = blocks(self.sums, j, 1 - c)(ALL, ALL, ALL)
        return self.copy("a", (j,), src, self.bufs["a"](j), device(y, z, x, 1 - c))

    def b(self, j, half):
        y, z, x, c = self.place
        at = blocks(self.sums, j, c)
        na, nb = cut(j)
        if half == 0:
            return self.copy("b", (j, 0), at(1 - y, ALL, ALL, ALL, pl.ds(0, na)), self.bufs["b0"](j), device(1 - y, z, x, c))
        return self.copy("b", (j, 1), at(ALL, ALL, 1 - x, ALL, pl.ds(na, nb)), self.bufs["b1"](j), device(y, z, 1 - x, c))

    def c(self, j, half):
        y, z, x, c = self.place
        at = blocks(self.sums, j, c)
        na, nb = cut(j)
        if half == 0:
            return self.copy("c", (j, 0), at(y, ALL, 1 - x, ALL, pl.ds(0, na)), self.bufs["c0"](j), device(y, z, 1 - x, c))
        return self.copy("c", (j, 1), at(1 - y, ALL, x, ALL, pl.ds(na, nb)), self.bufs["c1"](j), device(1 - y, z, x, c))

    def d(self, j, dz):
        y, z, x, c = self.place
        at = blocks(self.sums, j, c)
        return self.copy("d", (j, dz - 1), at(y, other(z, dz), x), self.bufs["d"](j, dz), device(y, other(z, dz), x, c))

    def e(self, j):
        y, z, x, c = self.place
        return self.copy("e", (j,), self.bufs["f"](j).at[1 - c], self.bufs["e"](j), device(y, z, x, 1 - c))

    def begin(self, j):
        self.a(j).start()

    def add_a(self, j):
        y, z, x, c = self.place
        self.a(j).wait_recv()
        at = blocks(self.sums, j, c)
        got = self.bufs["a"](j)

        @pl.loop(0, 16)
        def _(i):
            yy, zz, xx = i // 8, (i // 2) % 4, i % 2
            own = at(yy, zz, xx)
            own[...] = (own[...].astype(jnp.float32) + got[yy, zz, xx].astype(jnp.float32)).astype(own.dtype)

        self.b(j, 0).start()
        self.b(j, 1).start()

    def add_b(self, j):
        y, z, x, c = self.place
        na, nb = cut(j)
        at = blocks(self.sums, j, c)
        self.b(j, 0).wait_recv()
        got = self.bufs["b0"](j)

        @pl.loop(0, 8)
        def _(i):
            zz, xx = i // 2, i % 2
            own = at(y, zz, xx, ALL, pl.ds(0, na))
            own[...] = (own[...].astype(jnp.float32) + got[zz, xx].astype(jnp.float32)).astype(own.dtype)

        self.c(j, 0).start()
        self.b(j, 1).wait_recv()
        got1 = self.bufs["b1"](j)

        @pl.loop(0, 8)
        def _(i):
            yy, zz = i // 4, i % 4
            own = at(yy, zz, x, ALL, pl.ds(na, nb))
            own[...] = (own[...].astype(jnp.float32) + got1[yy, zz].astype(jnp.float32)).astype(own.dtype)

        self.c(j, 1).start()

    def add_c(self, j):
        y, z, x, c = self.place
        na, nb = cut(j)
        at = blocks(self.sums, j, c)
        self.c(j, 0).wait_recv()
        self.c(j, 1).wait_recv()
        got0, got1 = self.bufs["c0"](j), self.bufs["c1"](j)

        @pl.loop(0, 4)
        def _(zz):
            own = at(y, zz, x, ALL, pl.ds(0, na))
            own[...] = (own[...].astype(jnp.float32) + got0[zz].astype(jnp.float32)).astype(own.dtype)
            own1 = at(y, zz, x, ALL, pl.ds(na, nb))
            own1[...] = (own1[...].astype(jnp.float32) + got1[zz].astype(jnp.float32)).astype(own1.dtype)

        for dz in (1, 2, 3):
            self.d(j, dz).start()

    def add_d(self, j):
        y, z, x, c = self.place
        for dz in (1, 2, 3):
            self.d(j, dz).wait_recv()
        total = blocks(self.sums, j, c)(y, z, x)[...].astype(jnp.float32)
        for dz in (1, 2, 3):
            total = total + self.bufs["d"](j, dz)[...].astype(jnp.float32)
        out = self.bufs["f"](j)
        if j < 4:
            out[0] = total[:24]
            out[1] = total[24:]
            self.e(j).start()
        else:
            out[...] = total

    def sent(self, j):
        self.a(j).wait_send()
        for half in (0, 1):
            self.b(j, half).wait_send()
            self.c(j, half).wait_send()
        for dz in (1, 2, 3):
            self.d(j, dz).wait_send()
        if j < 4:
            self.e(j).wait_send()


SCATTER_SEMS = {"a": 0, "b": 2, "c": 2, "d": 3, "e": 0}


def sem_shapes(table):
    return [pltpu.SemaphoreType.DMA((ROUNDS, n) if n else (ROUNDS,)) for n in table.values() for _ in (0, 1)]


def sem_dict(table, refs):
    return {k: (refs[2 * i], refs[2 * i + 1]) for i, k in enumerate(table)}


def barrier(place):
    y, z, x, c = place
    bar = pltpu.get_barrier_semaphore()
    peers = [device(y, z, x, 1 - c), device(y, z, 1 - x, c), device(1 - y, z, x, c)] + [device(y, other(z, dz), x, c) for dz in (1, 2, 3)]
    for p in peers:
        pl.semaphore_signal(bar, inc=1, device_id=p, device_id_type=MESH)
    pl.semaphore_wait(bar, len(peers))

W_SHAPES = [(2, 2, 4, 2, 48, 768 + EXT), (6, 2, 4, 2, 48, 768), (2, 4, 2, 4, 48, 768)]

def stage_shards(place, ins, weights, s0, r0, s0sem):
    y, z, x, c = place
    qkv, out, up, down, ext = ins
    def piece(p):
        if p < 3:
            v = qkv[:, 768 * p : 768 * (p + 1)].astype(jnp.float32)
            return jnp.concatenate([v, ext[...].astype(jnp.float32)], axis=1) if p < 2 else v
        if p == 3:
            return out[...].astype(jnp.float32)
        return up[:, 768 * (p - 4) : 768 * (p - 3)].astype(jnp.float32)
    def shard_copy(j):
        n = 896 if j == 0 else 768
        return pltpu.make_async_remote_copy(src_ref=s0.at[j, :, pl.ds(0, n)], dst_ref=r0.at[j, :, pl.ds(0, n)], send_sem=s0sem.at[0, j], recv_sem=s0sem.at[1, j], device_id=device(y, z, x, 1 - c), device_id_type=MESH)
    def send(j):
        n = 896 if j == 0 else 768
        even, odd = piece(2 * j), piece(2 * j + 1)
        s0[j, :, pl.ds(0, n)] = jnp.where(c == 0, odd, even)
        shard_copy(j).start()
    def build(j):
        n = 896 if j == 0 else 768
        even, odd = piece(2 * j), piece(2 * j + 1)
        mine = jnp.where(c == 0, even, odd)
        shard_copy(j).wait_recv()
        got = r0[j, :, pl.ds(0, n)]
        blk = jnp.where(c == 0, jnp.concatenate([mine, got], axis=0), jnp.concatenate([got, mine], axis=0))
        blocks(weights, j, c)(y, z, x)[...] = blk.astype(jnp.bfloat16)
    def build_down():
        for k in (0, 1):
            weights[2][y, z, x, 2 * c + k] = down[48 * k : 48 * (k + 1), :]
    return shard_copy, send, build, build_down

def gather_kernel(qkv, out, up, down, ext, o0, o1, od, w0, w1, wd, s0, r0, s0sem, osem, *sems):
    place = coords()
    sd = sem_dict(GATHER_SEMS, sems)
    weights = (w0, w1, wd)
    barrier(place)
    shard_copy, send, build, build_down = stage_shards(place, (qkv, out, up, down, ext), weights, s0, r0, s0sem)
    g = Gather(place, weights, sd)
    for j in range(4): send(j)
    for j in range(4):
        build(j); g.begin(j)
    build_down()
    g.begin(4); g.begin(5)
    for step in range(ROUNDS + 2):
        if step < ROUNDS: g.forward(step)
        if 0 <= step - 1 < ROUNDS: g.cross(step - 1)
        if 0 <= step - 2 < ROUNDS: g.finish(step - 2)
    for j in range(ROUNDS): g.arrive(j)
    cps = [pltpu.make_async_copy(a, b, osem.at[i]) for i, (a, b) in enumerate(((w0, o0), (w1, o1), (wd, od)))]
    for cp in cps: cp.start()
    for j in range(ROUNDS): g.sent(j)
    for j in range(4): shard_copy(j).wait_send()
    for cp in cps: cp.wait()

def gather_call(qkv, out, up, down, ext):
    return pl.pallas_call(
        gather_kernel,
        out_shape=[jax.ShapeDtypeStruct(s, jnp.bfloat16) for s in W_SHAPES],
        in_specs=[pl.BlockSpec(memory_space=pltpu.VMEM)] * 5,
        out_specs=[pl.BlockSpec(memory_space=pl.ANY)] * 3,
        scratch_shapes=[pltpu.VMEM(s, jnp.bfloat16) for s in W_SHAPES] + [pltpu.VMEM((4, 24, 896), jnp.float32)] * 2
        + [pltpu.SemaphoreType.DMA((2, 4)), pltpu.SemaphoreType.DMA((3,))] + sem_shapes(GATHER_SEMS),
        compiler_params=pltpu.CompilerParams(collective_id=0, has_side_effects=True, vmem_limit_bytes=40 * 2**20),
        name="gather_weights",
    )(qkv, out, up, down, ext)

def scatter_kernel(i0, i1, id_, o0, o1, od, g0, g1, gd, ra0, ra, b0a, b0, b1a, b1, c0a, c0, c1a, c1, rda, rd, fs0, fs, fd, re0, re, isem, *sems):
    place = coords()
    sd = sem_dict(SCATTER_SEMS, sems)
    sums = (g0, g1, gd)
    cps = [pltpu.make_async_copy(a, b, isem.at[i]) for i, (a, b) in enumerate(((i0, g0), (i1, g1), (id_, gd)))]
    for cp in cps: cp.start()
    barrier(place)
    def pick(first, rest):
        return lambda j: first.at[0] if j == 0 else rest.at[j - 1]
    bufs = {"a": pick(ra0, ra), "b0": pick(b0a, b0), "b1": pick(b1a, b1), "c0": pick(c0a, c0), "c1": pick(c1a, c1),
            "d": lambda j, dz: rda.at[dz - 1] if j == 0 else rd.at[j - 1, dz - 1],
            "f": lambda j: fs0 if j == 0 else (fs.at[j - 1] if j < 4 else fd.at[j - 4]),
            "e": lambda j: re0 if j == 0 else re.at[j - 1]}
    s = Scatter(place, sums, bufs, sd)
    for cp in cps: cp.wait()
    order = [4, 5, 2, 3, 1, 0]
    for j in order: s.begin(j)
    fns = [s.add_a, s.add_b, s.add_c, s.add_d]
    for step in range(ROUNDS + 3):
        for lag in range(4):
            i = step - lag
            if 0 <= i < ROUNDS: fns[lag](order[i])
    c = place[3]
    for j in range(4):
        s.e(j).wait_recv()
        own = bufs["f"](j)[c]
        got = bufs["e"](j)[...]
        o = o0 if j == 0 else o1
        base = 0 if j == 0 else 2 * (j - 1)
        o[base] = jnp.where(c == 0, own, got)
        o[base + 1] = jnp.where(c == 0, got, own)
    for k in (0, 1):
        od[48 * k : 48 * (k + 1), :] = fd[k]
    for j in range(ROUNDS): s.sent(j)

def scatter_call(g0, g1, gd):
    bf = lambda *s: pltpu.VMEM(s, jnp.bfloat16)
    f = lambda *s: pltpu.VMEM(s, jnp.float32)
    return pl.pallas_call(
        scatter_kernel,
        out_shape=[jax.ShapeDtypeStruct((2, 24, 896), jnp.float32), jax.ShapeDtypeStruct((6, 24, 768), jnp.float32), jax.ShapeDtypeStruct((96, 768), jnp.float32)],
        in_specs=[pl.BlockSpec(memory_space=pl.ANY)] * 3,
        out_specs=[pl.BlockSpec(memory_space=pltpu.VMEM)] * 3,
        scratch_shapes=[bf(*s) for s in W_SHAPES] + [
            bf(1, 2, 4, 2, 48, 896), bf(5, 2, 4, 2, 48, 768),
            bf(1, 4, 2, 48, 384), bf(5, 4, 2, 48, 384),
            bf(1, 2, 4, 48, 512), bf(5, 2, 4, 48, 384),
            bf(1, 4, 48, 384), bf(5, 4, 48, 384),
            bf(1, 4, 48, 512), bf(5, 4, 48, 384),
            bf(3, 48, 896), bf(5, 3, 48, 768),
            f(2, 24, 896), f(3, 2, 24, 768), f(2, 48, 768),
            f(24, 896), f(3, 24, 768),
            pltpu.SemaphoreType.DMA((3,))] + sem_shapes(SCATTER_SEMS),
        compiler_params=pltpu.CompilerParams(collective_id=1, has_side_effects=True, vmem_limit_bytes=56 * 2**20),
        name="scatter_sums",
    )(g0, g1, gd)


def one_slice(patches, visible_index, visible_count, qkv_weight, out_weight, up_weight, down_weight, attention_gain, attention_shift, feedforward_gain, feedforward_shift, cotangent):
    small = jnp.stack([attention_gain, attention_shift, feedforward_gain, feedforward_shift], axis=1)
    ext = jnp.pad(small, ((0, 0), (0, EXT - 4)))
    w0, w1, wd = gather_call(qkv_weight, out_weight, up_weight, down_weight, ext)
    w0 = w0.reshape(2, 768, 768 + EXT)
    w1 = w1.reshape(6, 768, 768)
    gains = w0[0][:, 768:772]
    weights = (
        jnp.concatenate([w0[0][:, :768], w0[1][:, :768], w1[0]], axis=1),
        w1[1],
        jnp.concatenate([w1[2], w1[3], w1[4], w1[5]], axis=1),
        wd.reshape(3072, 768),
        gains[:, 0], gains[:, 1], gains[:, 2], gains[:, 3],
    )
    micro = patches.shape[0]
    strip = lambda a: a.reshape((micro,) + a.shape[2:])
    output, gradients, patch_part = layer(weights, strip(patches), strip(visible_index), strip(visible_count), strip(cotangent))
    qkv, out, up, down = [g.astype(jnp.bfloat16) for g in gradients[:4]]
    side = jnp.pad(jnp.stack(gradients[4:], axis=1), ((0, 0), (0, EXT - 4))).astype(jnp.bfloat16)
    g0 = jnp.stack([jnp.concatenate([qkv[:, 0:768], side], axis=1), jnp.concatenate([qkv[:, 768:1536], side], axis=1)]).reshape(W_SHAPES[0])
    g1 = jnp.stack([qkv[:, 1536:], out, up[:, :768], up[:, 768:1536], up[:, 1536:2304], up[:, 2304:]]).reshape(W_SHAPES[1])
    o0, o1, od = scatter_call(g0, g1, down.reshape(W_SHAPES[2]))
    return (
        output.reshape((micro, 1) + output.shape[1:]),
        patch_part.reshape((micro, 1) + patch_part.shape[1:]),
        jnp.concatenate([o0[0][:, :768], o0[1][:, :768], o1[0]], axis=1),
        o1[1],
        jnp.concatenate([o1[2], o1[3], o1[4], o1[5]], axis=1),
        od,
        o0[0][:, 768], o0[0][:, 769], o0[0][:, 770], o0[0][:, 771],
    )


def solution(mesh):
    strips = lambda n: P(None, AXES, *([None] * n))
    rows, row = P(AXES, None), P(AXES)
    body = one_slice if tuple(mesh.shape.values()) == (2, 16) else any_slice
    return jax.shard_map(
        body,
        mesh=mesh,
        in_specs=(strips(2), strips(1), strips(0), rows, rows, rows, rows, row, row, row, row, strips(2)),
        out_specs=(strips(2), strips(2), rows, rows, rows, rows, row, row, row, row),
        check_vma=False,
    )
```

```python
import jax
import jax.numpy as jnp
from jax import lax
from jax.experimental import pallas as pl
from jax.experimental.pallas import tpu as pltpu
from jax.sharding import PartitionSpec as P

HEADS = 12
AXES = ("dp", "fsdp")
MASKED = -1000000000.0
EPSILON = 1e-06
F32 = jnp.float32
BF16 = jnp.bfloat16


def norm_forward(features, scaling, offset):
    center = features - jnp.mean(features, axis=-1, keepdims=True)
    inverse = lax.rsqrt(jnp.mean(center * center, axis=-1, keepdims=True) + EPSILON)
    normed = center * inverse
    return (normed * scaling.astype(F32) + offset.astype(F32), normed, inverse)


def norm_backward(upstream, normed, inverse, scaling):
    through = upstream * scaling.astype(F32)
    inward = inverse * (
        through
        - jnp.mean(through, axis=-1, keepdims=True)
        - normed * jnp.mean(through * normed, axis=-1, keepdims=True)
    )
    return (inward, jnp.sum(upstream * normed, axis=0), jnp.sum(upstream, axis=0))


def sums(equation, left, right):
    return jnp.einsum(equation, left, right, preferred_element_type=F32)


def layer(weights, patches, indices, counts, cotangent):
    qkv_full, out_full, up_full, down_full, first_gain, first_shift, second_gain, second_shift = weights
    strips, visible, patch_count = (indices.shape[0], indices.shape[1], patches.shape[1])
    width = out_full.shape[1]
    rows = strips * visible
    heads = (strips, visible, HEADS, width // HEADS)
    scale = (width // HEADS) ** (-0.5)
    present = jnp.arange(visible)[None, :] < counts[:, None]
    onehot = ((indices[:, :, None] == jnp.arange(patch_count)[None, None, :]) & present[:, :, None]).astype(BF16)
    inputs = sums("bvp,bpd->bvd", onehot, patches).reshape(rows, width)
    first_norm, first_normed, first_inverse = norm_forward(inputs, first_gain, first_shift)
    first_low = first_norm.astype(BF16)
    projected = jnp.dot(first_low, qkv_full, preferred_element_type=F32).astype(BF16)
    queries = projected[:, :width].reshape(heads)
    keys = projected[:, width : 2 * width].reshape(heads)
    values = projected[:, 2 * width :].reshape(heads)
    scores = sums("bqhe,bkhe->bhqk", queries, keys) * scale
    scores = jnp.where(present[:, None, None, :], scores, MASKED)
    attention = jax.nn.softmax(scores, axis=-1)
    attention_low = attention.astype(BF16)
    mixed = sums("bhqk,bkhe->bqhe", attention_low, values).astype(BF16).reshape(rows, width)
    middle = inputs + jnp.dot(mixed, out_full, preferred_element_type=F32)
    second_norm, second_normed, second_inverse = norm_forward(middle, second_gain, second_shift)
    second_low = second_norm.astype(BF16)
    hidden_pre = jnp.dot(second_low, up_full, preferred_element_type=F32)
    hidden, gelu_pull = jax.vjp(lambda v: jax.nn.gelu(v, approximate=False), hidden_pre)
    hidden_low = hidden.astype(BF16)
    branch = jnp.dot(hidden_low, down_full, preferred_element_type=F32)
    live = present.reshape(rows, 1)
    output = ((middle + branch) * live.astype(F32)).reshape(strips, visible, width)

    upstream = cotangent.reshape(rows, width) * live.astype(BF16)
    down_grad = sums("rf,rd->fd", hidden_low, upstream)
    pre_low = gelu_pull(sums("rd,fd->rf", upstream, down_full))[0].astype(BF16)
    up_grad = sums("rf,rd->fd", second_low, pre_low)
    second_back = sums("rd,fd->rf", pre_low, up_full)
    inward, second_gain_grad, second_shift_grad = norm_backward(second_back, second_normed, second_inverse, second_gain)
    middle_grad = upstream.astype(F32) + inward
    middle_low = middle_grad.astype(BF16)
    out_grad = sums("rf,rd->fd", mixed, middle_low)
    mixed_grad = sums("rd,fd->rf", middle_low, out_full).astype(BF16).reshape(heads)
    prob_grad = sums("bqhe,bkhe->bhqk", mixed_grad, values)
    value_grad = sums("bhqk,bqhe->bkhe", attention_low, mixed_grad)
    score_low = (attention * (prob_grad - jnp.sum(attention * prob_grad, axis=-1, keepdims=True))).astype(BF16)
    query_grad = sums("bhqk,bkhe->bqhe", score_low, keys) * scale
    key_grad = sums("bhqk,bqhe->bkhe", score_low, queries) * scale
    projected_grad = jnp.concatenate([g.reshape(rows, width) for g in (query_grad, key_grad, value_grad)], axis=1).astype(BF16)
    qkv_grad = sums("rf,rd->fd", first_low, projected_grad)
    first_back = sums("rd,fd->rf", projected_grad, qkv_full)
    inward, first_gain_grad, first_shift_grad = norm_backward(first_back, first_normed, first_inverse, first_gain)
    input_low = (middle_grad + inward).astype(BF16).reshape(strips, visible, width)
    patch_part = sums("bvp,bvd->bpd", onehot, input_low)
    gradients = (qkv_grad, out_grad, up_grad, down_grad, first_gain_grad, first_shift_grad, second_gain_grad, second_shift_grad)
    return (output, gradients, patch_part)


def any_slice(patches, visible_index, visible_count, *rest):
    weights, cotangent = rest[:-1], rest[-1]
    whole = [lax.all_gather(w, AXES, axis=0, tiled=True) for w in weights]
    micro, strips = patches.shape[:2]
    flat = lambda a: a.reshape((micro * strips,) + a.shape[2:])
    output, gradients, patch_part = layer(whole, flat(patches), flat(visible_index), flat(visible_count), flat(cotangent))
    shares = [lax.psum_scatter(g, AXES, scatter_dimension=0, tiled=True) for g in gradients]
    back = lambda a: a.reshape((micro, strips) + a.shape[1:])
    return (back(output), back(patch_part), *shares)


MESH = pl.DeviceIdType.MESH
EXT = 128
ALL = slice(None)


def coords():
    y = lax.axis_index("dp")
    f = lax.axis_index("fsdp")
    return y, f // 4, (f // 2) % 2, f % 2


def device(y, z, x, c):
    return (y, z * 4 + x * 2 + c)


def other(z, dz):
    if dz == 0:
        return z
    if dz == 1:
        return z + 1 - 2 * (z % 2)
    if dz == 2:
        return (z + 2) % 4
    return 3 - z


def at_z(z):
    return (z // 2, z % 2)


class Round:
    def __init__(self, i, ref, lead, start, width, first):
        self.i, self.ref, self.lead, self.start, self.width = i, ref, lead, start, width
        self.halves = (pl.ds(start, first), pl.ds(start + first, width - first))
        self.cols = pl.ds(start, width)
        self.local = pl.ds(0, first), pl.ds(0, width - first)

    def at(self, par):
        def block(y, z, x, cols=None):
            before, after = self.lead(par)
            return self.ref.at[before + (y,) + z + (x,) + after + (ALL, self.cols if cols is None else cols)]

        return block


def piece(n):
    return lambda par: ((n + par,), ())


def part(n, step=1):
    return lambda par: ((), (n + step * par,))


def gather_rounds(w0, w1, wd):
    return [
        Round(0, w0, piece(0), 0, 384 + EXT, 256),
        Round(1, w1, piece(0), 0, 384, 256),
        Round(2, w0, piece(0), 384 + EXT, 384, 128),
        Round(3, w1, piece(0), 384, 384, 128),
        Round(4, wd, part(0, 2), 0, 768, 384),
        Round(5, wd, part(1, 2), 0, 768, 384),
        Round(6, w1, piece(2), 0, 768, 384),
        Round(7, w1, piece(4), 0, 384, 256),
        Round(8, w1, piece(4), 384, 384, 128),
    ]


def scatter_rounds(w1, gd):
    return [
        Round(0, gd, part(0, 2), 0, 768, 384),
        Round(1, gd, part(1, 2), 0, 768, 384),
        Round(2, w1, piece(2), 0, 768, 384),
        Round(3, w1, piece(4), 0, 768, 384),
        Round(4, gd, part(2), 0, 384, 256),
        Round(5, gd, part(0), 0, 384, 128),
        Round(6, gd, part(2), 384, 384, 256),
        Round(7, gd, part(0), 384, 384, 128),
    ]


class Peers:
    def __init__(self, place, rounds, sems):
        y, z, x, c = self.place = place
        self.rounds, self.sems = rounds, sems
        self.all_z, self.pair, self.odd = (ALL, ALL), (ALL, z % 2), (ALL, 1 - z % 2)
        self.x_side, self.y_side = device(y, z, 1 - x, c), device(1 - y, z, x, c)
        self.sibling = device(y, z, x, 1 - c)

    def z_peer(self, dz):
        y, z, x, c = self.place
        return device(y, other(z, dz), x, c)

    def copy(self, kind, i, src, dst, to):
        send, recv = self.sems[kind]
        return pltpu.make_async_remote_copy(
            src_ref=src, dst_ref=dst, send_sem=send.at[i], recv_sem=recv.at[i], device_id=to, device_id_type=MESH
        )


class Gather(Peers):
    def same(self, kind, i, ref, to):
        return self.copy(kind, i, ref, ref, to)

    def at(self, j, par=None):
        return self.rounds[j].at(self.place[3] if par is None else par)

    def z(self, j, dz, there=0):
        y, z, x, c = self.place
        return self.same("z", (j, dz - 1), self.at(j)(y, at_z(other(z, there)), x), self.z_peer(dz))

    def side(self, j, dz, axis, there=False):
        y, z, x, c = self.place
        zz = at_z(other(z, dz))
        if axis == "x":
            return self.same("x", (j, dz), self.at(j)(y, zz, 1 - x if there else x), self.x_side)
        return self.same("y", (j, dz), self.at(j)(1 - y if there else y, zz, x), self.y_side)

    def diag(self, j, half, there=False):
        y, z, x, c = self.place
        cols = self.rounds[j].halves[half]
        yy = 1 - y if there or half == 1 else y
        xx = 1 - x if there or half == 0 else x
        return self.same("g", (j, half), self.at(j)(yy, self.pair, xx, cols), self.y_side if half == 0 else self.x_side)

    def turn(self, j, there=False):
        y, z, x, c = self.place
        return self.same("t", (j,), self.at(j)(1 - y, self.odd if there else self.pair, 1 - x), self.z_peer(1))

    def down(self, j, q, there=False):
        y, z, x, c = self.place
        yy = y if q < 2 else 1 - y
        xx = x if q in (0, 2) else 1 - x
        zz = self.all_z if q < 3 else self.pair if q == 3 else self.odd
        return self.same("d", (j, q), self.at(j, 1 - c if there else c)(yy, zz, xx), self.sibling)

    def begin(self, j):
        for dz in (1, 2, 3):
            self.z(j, dz).start()

    def own(self, j):
        self.side(j, 0, "x").start()
        self.side(j, 0, "y").start()

    def forward(self, j):
        for dz in (1, 2, 3):
            self.z(j, dz, dz).wait_recv()
            self.side(j, dz, "x").start()
            self.side(j, dz, "y").start()
        self.down(j, 0).start()

    def cross(self, j):
        for half, axis in enumerate(("x", "y")):
            self.side(j, 0, axis, True).wait_recv()
            self.side(j, 2, axis, True).wait_recv()
            self.diag(j, half).start()
        for half, axis in enumerate(("x", "y")):
            self.side(j, 1, axis, True).wait_recv()
            self.side(j, 3, axis, True).wait_recv()
            self.down(j, 1 + half).start()

    def finish(self, j):
        self.diag(j, 0, True).wait_recv()
        self.diag(j, 1, True).wait_recv()
        self.turn(j).start()
        self.down(j, 3).start()

    def last(self, j):
        self.turn(j, True).wait_recv()
        self.down(j, 4).start()

    def arrive(self, j):
        for q in range(5):
            self.down(j, q, True).wait_recv()

    def sent(self, j):
        for dz in (1, 2, 3):
            self.z(j, dz).wait_send()
        for dz in range(4):
            self.side(j, dz, "x").wait_send()
            self.side(j, dz, "y").wait_send()
        for half in range(2):
            self.diag(j, half).wait_send()
        self.turn(j).wait_send()
        for q in range(5):
            self.down(j, q).wait_send()


GATHER_SEMS = {"z": 3, "x": 4, "y": 4, "g": 2, "t": 0, "d": 5}


def add_to(own, got):
    own[...] = (own[...].astype(F32) + got[...].astype(F32)).astype(BF16)


class Scatter(Peers):
    def __init__(self, place, rounds, bufs, sems, free):
        super().__init__(place, rounds, sems)
        self.bufs, self.free = bufs, free

    def at(self, j, par=None):
        return self.rounds[j].at(self.place[3] if par is None else par)

    def a(self, j):
        return self.copy("a", (j,), self.at(j, 1 - self.place[3])(ALL, self.all_z, ALL), self.bufs["a"](j), self.sibling)

    def turn(self, j):
        y, z, x, c = self.place
        return self.copy("t", (j,), self.at(j)(1 - y, self.odd, 1 - x), self.bufs["t"](j), self.z_peer(1))

    def diag(self, j, half):
        y, z, x, c = self.place
        cols = self.rounds[j].halves[half]
        src = self.at(j)(1 - y, self.pair, 1 - x, cols)
        return self.copy("g", (j, half), src, self.bufs["g"](j, half), self.y_side if half == 0 else self.x_side)

    def side(self, j, k, axis):
        y, z, x, c = self.place
        zz = self.pair if k else self.odd
        if axis == "x":
            return self.copy("x", (j, k), self.at(j)(y, zz, 1 - x), self.bufs["x"](j, k), self.x_side)
        return self.copy("y", (j, k), self.at(j)(1 - y, zz, x), self.bufs["y"](j, k), self.y_side)

    def d(self, j, dz):
        y, z, x, c = self.place
        return self.copy("d", (j, dz - 1), self.at(j)(y, at_z(other(z, dz)), x), self.bufs["d"](j, dz), self.z_peer(dz))

    def e(self, j):
        return self.copy("e", (j,), self.bufs["f"](j).at[1 - self.place[3]], self.bufs["e"](j), self.sibling)

    def begin(self, j):
        if j >= 2:
            pl.semaphore_wait(self.free.at[j % 2], 1)
        self.a(j).start()

    def add_a(self, j):
        self.a(j).wait_recv()
        at, got = self.at(j), self.bufs["a"](j)

        @pl.loop(0, 16)
        def _(i):
            y, z, x = i // 8, at_z((i // 2) % 4), i % 2
            add_to(at(y, z, x), got.at[(y,) + z + (x,)])

        self.turn(j).start()
        self.side(j, 0, "x").start()
        self.side(j, 0, "y").start()
        if j < len(self.rounds) - 2:
            pl.semaphore_signal(self.free.at[j % 2], inc=1, device_id=self.sibling, device_id_type=MESH)

    def add_t(self, j):
        y, z, x, c = self.place
        self.turn(j).wait_recv()
        for h in range(2):
            add_to(self.at(j)(1 - y, (h, z % 2), 1 - x), self.bufs["t"](j).at[h])
        self.diag(j, 0).start()
        self.diag(j, 1).start()

    def add_g(self, j):
        y, z, x, c = self.place
        first, second = self.rounds[j].halves
        self.diag(j, 0).wait_recv()
        for h in range(2):
            add_to(self.at(j)(y, (h, z % 2), 1 - x, first), self.bufs["g"](j, 0).at[h])
        self.side(j, 1, "x").start()
        self.diag(j, 1).wait_recv()
        for h in range(2):
            add_to(self.at(j)(1 - y, (h, z % 2), x, second), self.bufs["g"](j, 1).at[h])
        self.side(j, 1, "y").start()

    def add_s(self, j):
        y, z, x, c = self.place
        for k in range(2):
            self.side(j, k, "x").wait_recv()
            self.side(j, k, "y").wait_recv()
            low = z % 2 if k else 1 - z % 2

            @pl.loop(0, 2)
            def _(h):
                own = self.at(j)(y, (h, low), x)
                both = self.bufs["x"](j, k)[h].astype(F32) + self.bufs["y"](j, k)[h].astype(F32)
                own[...] = (own[...].astype(F32) + both).astype(BF16)

        for dz in (1, 2, 3):
            self.d(j, dz).start()

    def add_d(self, j):
        y, z, x, c = self.place
        for dz in (1, 2, 3):
            self.d(j, dz).wait_recv()
        total = self.at(j)(y, at_z(z), x)[...].astype(F32)
        for dz in (1, 2, 3):
            total = total + self.bufs["d"](j, dz)[...].astype(F32)
        out = self.bufs["f"](j)
        if j < 2:
            out[...] = total
        else:
            out[0] = total[:24]
            out[1] = total[24:]
            self.e(j).start()

    def sent(self, j):
        self.a(j).wait_send()
        self.turn(j).wait_send()
        for k in range(2):
            self.diag(j, k).wait_send()
            self.side(j, k, "x").wait_send()
            self.side(j, k, "y").wait_send()
        for dz in (1, 2, 3):
            self.d(j, dz).wait_send()
        if j > 1:
            self.e(j).wait_send()


class Total(Peers):
    def __init__(self, place, side, send, recv):
        super().__init__(place, None, None)
        self.side, self.sems = side, {"v": (send, recv)}
        self.peers = (self.sibling, self.x_side, self.y_side, self.z_peer(1), self.z_peer(2))

    def step(self, i):
        return self.copy("v", (i,), self.side.at[i], self.side.at[5 + i], self.peers[i])

    def begin(self):
        self.step(0).start()

    def add(self, i):
        self.step(i).wait_recv()
        total = self.side[i] + self.side[5 + i]
        if i < 4:
            self.side[i + 1] = total
            self.step(i + 1).start()
        return total

    def sent(self):
        for i in range(5):
            self.step(i).wait_send()


SCATTER_SEMS = {"a": 0, "t": 0, "g": 2, "x": 2, "y": 2, "d": 3, "e": 0}


def sem_shapes(table, rounds):
    return [pltpu.SemaphoreType.DMA((rounds, n) if n else (rounds,)) for n in table.values() for _ in (0, 1)]


def sem_dict(table, refs):
    return {k: (refs[2 * i], refs[2 * i + 1]) for i, k in enumerate(table)}


def mm(a, b):
    return lax.dot_general(a, b, (((1,), (0,)), ((), ())), preferred_element_type=F32)


def mt(a, b):
    return lax.dot_general(a, b, (((1,), (1,)), ((), ())), preferred_element_type=F32)


def tm(a, b):
    return lax.dot_general(a, b, (((0,), (0,)), ((), ())), preferred_element_type=F32)


def lanes(i, n):
    return pl.ds(pl.multiple_of(i * n, 128), n)


def rows_at(i, n):
    return pl.ds(pl.multiple_of(i * n, 16), n)


def normal(v):
    center = v - jnp.mean(v, axis=-1, keepdims=True)
    inverse = lax.rsqrt(jnp.mean(center * center, axis=-1, keepdims=True) + EPSILON)
    return center * inverse, inverse


def gelu_parts(v):
    cdf = 0.5 * lax.erf(v * (0.5**0.5)) + 0.5
    return v * cdf, cdf + v * jnp.exp2(v * v * (-0.5 * 1.4426950408889634) - 1.3257480647361593)


class Layer:
    def __init__(self, r):
        self.__dict__.update(r)

    def weight(self, p, start=0, width=768):
        if p < 2:
            return self.w0[p, :, :, :, :, :, pl.ds(EXT + start, width)].reshape(768, width)
        return self.w1[p - 2, :, :, :, :, :, pl.ds(start, width)].reshape(768, width)

    def live(self, s, shape, axis):
        return lax.broadcasted_iota(jnp.int32, shape, axis) < self.count[s]

    def take(self):
        @pl.loop(0, 2)
        def _(s):
            row = lax.broadcasted_iota(jnp.int32, (1058, 400), 0)
            hot = (row == 2 * self.index[s] + s) & self.live(s, (1058, 400), 1)
            got = tm(hot.astype(F32).astype(BF16), self.pool[...].reshape(1058, 768))
            self.inputs[rows_at(s, 400), :] = got.astype(BF16)
            self.ups[s] = jnp.where(self.live(s, (400, 768), 0), self.ups[s], jnp.zeros((), BF16))

    def gains(self):
        side = self.w0[0, :, :, :, :, :, pl.ds(0, EXT)].reshape(768, EXT).astype(F32)
        self.gain[...] = side.T[0:8]

    def first(self):
        @pl.loop(0, 2)
        def _(s):
            normed, _ = normal(self.inputs[rows_at(s, 400), :].astype(F32))
            self.first_low[rows_at(s, 400), :] = (normed * self.gain[0:1] + self.gain[1:2]).astype(BF16)

    def project(self, half, pieces):
        start = 384 * half
        w = jnp.concatenate([self.weight(p, start, 384) for p in pieces], axis=1)

        got = mm(self.first_low[...], w).astype(BF16)
        for i, p in enumerate(pieces):
            self.proj[:, pl.ds(768 * p + start, 384)] = got[:, 384 * i : 384 * (i + 1)]

    def last_keys(self, s, shape, axis):
        return lax.broadcasted_iota(jnp.int32, shape, axis) + 384 < self.count[s]

    def attend(self, i):
        s, t = i % 2, i // 2
        rows = rows_at(s, 400)
        q, k, v = (self.proj[rows, lanes(6 * p + t, 128)] for p in range(3))
        lane = lax.broadcasted_iota(jnp.int32, (400, 128), 1)
        alive = self.last_keys(s, (400, 16), 1)
        halves = (lane < 64, lane >= 64)
        eighth = q * jnp.asarray(0.125, BF16)
        scores = [mt(jnp.where(mine, eighth, jnp.zeros((), BF16)), k) for mine in halves]
        scores = jnp.concatenate([jnp.concatenate([x[:, :384], jnp.where(alive, x[:, 384:], MASKED)], axis=1) for x in scores], axis=0)
        top = jnp.max(scores, axis=1, keepdims=True)
        e = jnp.exp(scores - top)
        total = jnp.sum(e, axis=1, keepdims=True)
        e = e.astype(BF16)
        mixed = jnp.concatenate([mm(e[400 * h : 400 * (h + 1)], v) for h in range(2)], axis=0) * (1.0 / total)
        self.mixed[rows, lanes(t, 128)] = jnp.where(halves[0], mixed[:400], mixed[400:]).astype(BF16)
        logs = top + jnp.log(total)
        stat = self.stat[s, pl.ds(0, 400), :]
        for h in range(2):
            stat = jnp.where(lane == 2 * t + h, logs[400 * h : 400 * (h + 1)], stat)
        self.stat[s, pl.ds(0, 400), :] = stat

    def turn_stat(self):
        for s in range(2):
            self.turned[s] = self.stat[s].T[0:16]

    def mix(self):
        w = self.weight(3)
        @pl.loop(0, 2)
        def _(s):
            rows = rows_at(s, 400)
            middle = self.inputs[rows, :].astype(F32) + mm(self.mixed[rows, :], w)
            self.mid[s, pl.ds(0, 400), :] = middle
            normed, _ = normal(middle)
            self.second_low[rows, :] = (normed * self.gain[2:3] + self.gain[3:4]).astype(BF16)

    def hide(self, parts):
        w = jnp.concatenate([self.weight(4 + p, start, width) for p, start, width in parts], axis=1)

        for s in range(2):
            rows, at = rows_at(s, 400), 0
            pre = mm(self.second_low[rows, :], w)
            for p, start, width in parts:
                act, slope = gelu_parts(pre[:, at : at + width])
                cols = pl.ds(768 * p + start, width)
                self.hidden[rows, cols] = act.astype(BF16)
                self.slope[rows, cols] = (slope * self.slope[rows, cols].astype(F32)).astype(BF16)
                at += width

    def down_terms(self, chunks):
        left = jnp.concatenate([self.hidden[:, pl.ds(384 * i, 384)] for i in chunks], axis=1)
        g = tm(left, self.ups[...].reshape(800, 768)).astype(BF16)
        for n, i in enumerate(chunks):
            self.gd[i // 4, (i % 4) // 2, i % 2] = g[384 * n : 384 * (n + 1)].reshape(2, 4, 48, 768)

    def branch(self, n, stage):
        w = self.wd[:, :, :, :, :, :, lanes(n, 256)].reshape(3072, 256)
        for s in range(2):
            got = mm(self.hidden[pl.ds(400 * s, 400), :], w)
            got = (got + self.mid[s, pl.ds(0, 400), lanes(n, 256)]) * self.live(s, (400, 256), 0).astype(F32)
            stage[s] = got

    def hide_back(self, p):
        w = self.wd[p // 2, p % 2].reshape(768, 768)
        self.slope[:, pl.ds(768 * p, 768)] = mt(self.ups[...].reshape(800, 768), w).astype(BF16)

    def up_terms(self, p):
        g = tm(self.second_low[...], self.slope[:, pl.ds(768 * p, 768)])
        self.g1[2 + p] = g.astype(BF16).reshape(2, 2, 2, 2, 48, 768)

    def second_back(self):
        self.vec[0] = jnp.zeros((8, 768), F32)

        @pl.loop(0, 2)
        def _(s):
            rows = rows_at(s, 400)
            back = mt(self.slope[rows, :], jnp.concatenate([self.weight(4 + p) for p in range(4)], axis=1))
            normed, inverse = normal(self.mid[s, pl.ds(0, 400), :])
            inward, dg, db = self.norm_back(back, normed, inverse, self.gain[2:3])
            self.ups[s] = (self.ups[s].astype(F32) + inward).astype(BF16)
            self.vec[0, 2:3] += dg
            self.vec[0, 3:4] += db

    def norm_back(self, back, normed, inverse, gain):
        through = back * gain
        inward = inverse * (
            through
            - jnp.mean(through, axis=-1, keepdims=True)
            - normed * jnp.mean(through * normed, axis=-1, keepdims=True)
        )
        return inward, jnp.sum(back * normed, axis=0, keepdims=True), jnp.sum(back, axis=0, keepdims=True)

    def mix_back(self):
        w = self.weight(3)
        self.second_low[...] = mt(self.ups[...].reshape(800, 768), w).astype(BF16)

    def out_terms(self):
        g = tm(self.mixed[...], self.ups[...].reshape(800, 768))
        self.gd[:, :, :, :, 3] = g.astype(BF16).reshape(2, 2, 2, 2, 48, 768)

    def attend_back(self, i):
        s, t = i % 2, i // 2
        rows = rows_at(s, 400)
        q, k, v = (self.proj[rows, lanes(6 * p + t, 128)] for p in range(3))
        do = self.second_low[rows, lanes(t, 128)]
        first_half = lax.broadcasted_iota(jnp.int32, (400, 128), 1) < 64
        alive = self.last_keys(s, (16, 400), 0)
        zero = jnp.zeros((), BF16)
        halves = (first_half, ~first_half)
        eighth = k * jnp.asarray(0.125, BF16)
        scores = [mt(jnp.where(mine, eighth, zero), q) for mine in halves]
        shares = []
        for h in range(2):
            p = jnp.exp(scores[h] - self.turned[s, pl.ds(2 * t + h, 1), pl.ds(0, 400)])
            shares.append(jnp.concatenate([p[:384], jnp.where(alive, p[384:], 0.0)], axis=0))
        dv = mm(jnp.concatenate([p.astype(BF16) for p in shares], axis=0), do)
        back = [mt(jnp.where(mine, v, zero), do) for mine in halves]
        ds = [(p * (dp - jnp.sum(p * dp, axis=0, keepdims=True))).astype(BF16) for p, dp in zip(shares, back)]
        dk = mm(jnp.concatenate(ds, axis=0), q)
        dq = [tm(x, k) for x in ds]
        for i, (first, second, scale) in enumerate(((dq[0], dq[1], 0.125), (dk[:400], dk[400:], 0.125), (dv[:400], dv[400:], 1.0))):
            g = jnp.where(first_half, first, second) * scale
            self.proj[rows, lanes(6 * i + t, 128)] = g.astype(BF16)

    def project_terms(self, half):
        start = 384 * half

        right = jnp.concatenate([self.proj[:, pl.ds(768 * p + start, 384)] for p in range(3)], axis=1)
        g = tm(self.first_low[...], right).astype(BF16)
        for p in range(3):
            self.gd[:, :, :, :, p, :, pl.ds(start, 384)] = g[:, 384 * p : 384 * (p + 1)].reshape(2, 2, 2, 2, 48, 384)

    def first_back(self):
        @pl.loop(0, 2)
        def _(s):
            rows = rows_at(s, 400)
            back = mt(self.proj[rows, :], jnp.concatenate([self.weight(p) for p in range(3)], axis=1))
            normed, inverse = normal(self.inputs[rows, :].astype(F32))
            inward, dg, db = self.norm_back(back, normed, inverse, self.gain[0:1])
            low = self.ups.at[s]
            low[...] = (low[...].astype(F32) + inward).astype(BF16)
            self.vec[0, 0:1] += dg
            self.vec[0, 1:2] += db

    def give(self):
        @pl.loop(0, 2)
        def _(s):
            at = lax.broadcasted_iota(jnp.int32, (529, 400), 0)
            hot = (at == self.index[s]) & self.live(s, (529, 400), 1)
            self.mid[s] = mm(hot.astype(F32).astype(BF16), self.ups[s])


W_SHAPES = ((2, 2, 2, 2, 2, 48, 768 + EXT), (6, 2, 2, 2, 2, 48, 768), (2, 2, 2, 2, 4, 48, 768))


def greet(place):
    y, z, x, c = place
    barrier = pltpu.get_barrier_semaphore()
    peers = [device(y, z, x, 1 - c), device(y, z, 1 - x, c), device(1 - y, z, x, c)]
    peers += [device(y, other(z, dz), x, c) for dz in (1, 2, 3)]
    for peer in peers:
        pl.semaphore_signal(barrier, inc=1, device_id=peer, device_id_type=MESH)
    return lambda: pl.semaphore_wait(barrier, len(peers))


class Shards:
    def __init__(self, place, own, weights, sent, got, sems):
        self.place, self.own, self.weights = place, own, weights
        self.sent, self.got, self.sems = sent, got, sems

    def width(self, j):
        return 768 + EXT if j == 0 else 768

    def piece(self, p):
        qkv, out, up, _, ext = self.own
        if p == 3:
            return out[...].astype(F32)
        if p > 3:
            return up[:, 768 * (p - 4) : 768 * (p - 3)].astype(F32)
        v = qkv[:, 768 * p : 768 * (p + 1)].astype(F32)
        return jnp.concatenate([ext[...].astype(F32), v], axis=1) if p < 2 else v

    def copy(self, j):
        y, z, x, c = self.place
        cols = pl.ds(0, self.width(j))
        return pltpu.make_async_remote_copy(
            src_ref=self.sent.at[j, :, cols],
            dst_ref=self.got.at[j, :, cols],
            send_sem=self.sems.at[0, j],
            recv_sem=self.sems.at[1, j],
            device_id=device(y, z, x, 1 - c),
            device_id_type=MESH,
        )

    def stage(self, j):
        c = self.place[3]
        self.sent[j, :, pl.ds(0, self.width(j))] = jnp.where(c == 0, self.piece(2 * j + 1), self.piece(2 * j))

    def build(self, j):
        y, z, x, c = self.place
        mine = jnp.where(c == 0, self.piece(2 * j), self.piece(2 * j + 1))
        self.copy(j).wait_recv()
        got = self.got[j, :, pl.ds(0, self.width(j))]
        both = jnp.where(c == 0, jnp.concatenate([mine, got], axis=0), jnp.concatenate([got, mine], axis=0))
        if j == 0:
            self.weights[0][c, y, z // 2, z % 2, x] = both.astype(BF16)
        else:
            self.weights[1][2 * (j - 1) + c, y, z // 2, z % 2, x] = both.astype(BF16)

    def close(self):
        for j in range(4):
            self.copy(j).wait_send()

    def build_down(self):
        y, z, x, c = self.place
        for k in (0, 1):
            self.weights[2][y, z // 2, z % 2, x, 2 * c + k] = self.own[3][48 * k : 48 * (k + 1), :]


class Refs:
    pass


def bf16(*shape):
    return pltpu.VMEM(shape, BF16)


def f32(*shape):
    return pltpu.VMEM(shape, F32)


INS = ["count", "index", "patches", "cot", "qkv", "out", "up", "down", "ext"]
OUTS = ["layer_out", "patch_out", "o_qkv", "o_out", "o_up", "o_down", "o_side"]
SCRATCH = dict(
    w0=bf16(*W_SHAPES[0]), w1=bf16(*W_SHAPES[1]), wd=bf16(*W_SHAPES[2]), gd=bf16(*W_SHAPES[2]),
    inputs=bf16(800, 768), first_low=bf16(800, 768), proj=bf16(800, 2304), mixed=bf16(800, 768),
    mid=f32(2, 529, 768), second_low=bf16(800, 768), hidden=bf16(800, 3072), slope=bf16(800, 3072),
    ups=bf16(2, 400, 768), gain=f32(8, 768), pool=bf16(529, 2, 768), stage=f32(2, 400, 256),
    stat=f32(2, 512, 128), turned=f32(2, 16, 512), vec=f32(10, 8, 768),
    s0=f32(4, 24, 768 + EXT), r0=f32(4, 24, 768 + EXT), ra=bf16(2, 2, 2, 2, 2, 48, 768),
    rt=bf16(4, 2, 48, 768), rx=bf16(4, 2, 2, 48, 768), ry=bf16(4, 2, 2, 48, 768), rg=bf16(4, 2, 2, 48, 384), rd=bf16(4, 3, 48, 768),
    ht=bf16(4, 2, 48, 384), hx=bf16(4, 2, 2, 48, 384), hy=bf16(4, 2, 2, 48, 384), hg=bf16(4, 2, 2, 48, 256), hd=bf16(4, 3, 48, 384),
    fd=f32(2, 48, 768), fs=f32(6, 2, 24, 768), re=f32(6, 24, 768),
    free=pltpu.SemaphoreType.REGULAR((2,)), pair=pltpu.SemaphoreType.DMA((2, 4)), local=pltpu.SemaphoreType.DMA((4,)), vs=pltpu.SemaphoreType.DMA((5,)), vr=pltpu.SemaphoreType.DMA((5,)),
)


def make_scatter(place, R, sems):
    rounds = scatter_rounds(R.w1, R.gd)

    def pick(full, half):
        return lambda j, *at: full.at[(j,) + at] if j < 4 else half.at[(j - 4,) + at]

    def corner(j, half):
        cols = rounds[j].local[half]
        return R.rg.at[j, half] if j < 4 else R.hg.at[j - 4, half, :, :, cols]

    bufs = dict(
        a=lambda j: R.ra.at[j % 2, :, :, :, :, :, pl.ds(0, rounds[j].width)],
        t=pick(R.rt, R.ht),
        x=pick(R.rx, R.hx),
        y=pick(R.ry, R.hy),
        g=corner,
        d=lambda j, dz: R.rd.at[j, dz - 1] if j < 4 else R.hd.at[j - 4, dz - 1],
        f=lambda j: R.fd.at[j] if j < 2 else R.fs.at[j - 2, :, :, pl.ds(0, rounds[j].width)],
        e=lambda j: R.re.at[j - 2, :, pl.ds(0, rounds[j].width)],
    )
    return Scatter(place, rounds, bufs, sem_dict(SCATTER_SEMS, sems), R.free)


def mega(*refs):
    names = INS + OUTS + list(SCRATCH)
    r = dict(zip(names, refs))
    n = len(names)
    m = n + 2 * len(GATHER_SEMS)
    R = Refs()
    R.__dict__.update(r)
    R.g1 = R.w1
    place = coords()
    c = place[3]
    weights = (R.w0, R.w1, R.wd)
    cot_copy = pltpu.make_async_copy(R.cot, R.ups, R.local.at[0])
    cot_copy.start()
    patch_in = pltpu.make_async_copy(R.patches, R.pool, R.local.at[3])
    patch_in.start()
    met = greet(place)
    shards = Shards(place, (R.qkv, R.out, R.up, R.down, R.ext), weights, R.s0, R.r0, R.pair)
    g = Gather(place, gather_rounds(*weights), sem_dict(GATHER_SEMS, refs[n:m]))
    v = Total(place, R.vec, R.vs, R.vr)

    s = make_scatter(place, R, refs[m:])
    L = Layer(R.__dict__)
    patch_copies = [pltpu.make_async_copy(R.mid.at[i], R.patch_out.at[i, :, 0, :], R.local.at[i]) for i in (0, 1)]

    def give():
        L.give()
        for copy in patch_copies:
            copy.start()


    def branch(k):
        copies = [pltpu.make_async_copy(R.stage, R.layer_out.at[:, :, pl.ds(256 * i, 256)], R.local.at[2]) for i in (k - 1, k)]
        if k:
            copies[0].wait()
        L.branch(k, R.stage)
        copies[1].start()
        if k == 2:
            copies[1].wait()


    def start(j):
        g.begin(j)
        g.own(j)

    for j in range(4):
        shards.stage(j)
    shards.build_down()
    met()
    for j in range(4):
        shards.copy(j).start()
    shards.build(0)
    start(0)
    shards.build(1)
    start(1)
    shards.build(2)
    shards.build(3)
    cot_copy.wait()
    patch_in.wait()
    L.take()

    def over(step, first, last):
        pl.loop(first, last)(step)

    qk, v_only = (0, 1), (2,)

    def close():
        for j in range(9):
            g.sent(j)
        shards.close()

    early, late = [(2, 0, 384), (3, 0, 384)], [(2, 384, 384), (3, 384, 384)]
    plan = [
        (g.forward, 0), (g.forward, 1), (g.cross, 0), (start, 2), (g.finish, 0), (g.cross, 1), (start, 3), (g.last, 0),
        (g.forward, 2), (g.finish, 1), (g.arrive, 0), (start, 4), (L.gains,), (L.first,), (L.project, 0, qk),
        (g.forward, 3), (g.cross, 2), (g.last, 1), (g.arrive, 1), (start, 5), (L.project, 0, v_only),
        (g.finish, 2), (g.cross, 3), (g.forward, 4), (over, L.attend, 0, 3), (g.last, 2), (g.finish, 3), (start, 6), (over, L.attend, 3, 6),
        (g.forward, 5), (g.cross, 4), (g.last, 3), (g.arrive, 2), (L.project, 1, qk), (g.arrive, 3), (L.project, 1, v_only),
        (start, 7), (start, 8), (over, L.attend, 6, 8), (g.finish, 4), (g.cross, 5), (g.forward, 6), (over, L.attend, 8, 10), (g.last, 4),
        (over, L.attend, 10, 12), (g.finish, 5), (g.forward, 7), (L.mix,), (g.cross, 6), (g.arrive, 4), (L.turn_stat,), (g.forward, 8), (g.last, 5), (g.cross, 7),
        (g.arrive, 5), (L.hide_back, 0), (g.finish, 6), (L.hide_back, 1), (g.cross, 8), (L.hide_back, 2), (g.last, 6), (g.finish, 7), (L.hide_back, 3),
        (g.finish, 8), (g.arrive, 6), (L.hide, [(0, 0, 768)]), (g.last, 7), (L.hide, [(1, 0, 768)]), (g.last, 8), (L.down_terms, (0, 1)), (L.down_terms, (2, 3)),
        (g.arrive, 7), (L.hide, early), (L.down_terms, (4, 6)), (g.arrive, 8), (L.hide, late), (L.down_terms, (5, 7)),
        (s.begin, 0), (s.begin, 1), (L.second_back,), (close,), (s.add_a, 0), (s.add_a, 1),
        (L.up_terms, 0), (L.up_terms, 1), (s.begin, 2), (s.add_t, 0), (L.up_terms, 2), (s.add_t, 1), (s.add_g, 0), (L.up_terms, 3), (s.begin, 3),
        (s.add_a, 2), (s.add_g, 1), (L.mix_back,), (s.add_s, 0), (s.add_a, 3), (over, L.attend_back, 0, 2), (s.add_s, 1), (s.add_t, 2), (s.add_d, 0),
        (over, L.attend_back, 2, 4), (s.add_t, 3), (s.add_g, 2), (s.add_d, 1), (over, L.attend_back, 4, 6), (s.add_g, 3), (s.sent, 0), (s.sent, 1),
        (L.project_terms, 0), (s.add_s, 2), (L.out_terms,), (s.begin, 4), (s.begin, 5), (over, L.attend_back, 6, 8), (s.add_s, 3), (s.add_d, 2), (s.add_a, 4), (s.add_a, 5),
        (over, L.attend_back, 8, 10), (s.add_t, 4), (s.add_t, 5), (over, L.attend_back, 10, 12), (s.add_d, 3),
        (s.add_g, 4), (s.add_g, 5), (L.project_terms, 1), (s.begin, 6), (s.begin, 7), (s.add_s, 4), (s.add_s, 5),
        (s.add_a, 6), (s.add_a, 7), (L.first_back,), (v.begin,), (s.add_t, 6), (s.add_t, 7), (s.add_d, 4),
        (branch, 0), (s.add_g, 6), (s.add_g, 7), (s.add_d, 5), (v.add, 0), (branch, 1), (v.add, 1), (s.add_s, 6), (s.add_s, 7), (branch, 2), (v.add, 2),
        (give,), (v.add, 3), (s.add_d, 6), (s.add_d, 7),
    ]
    for step, *at in plan:
        step(*at)
    R.o_side[...] = v.add(4)
    targets = {
        2: (R.o_up, 0, R.o_up, 768),
        3: (R.o_up, 1536, R.o_up, 2304),
        4: (R.o_qkv, 1536, R.o_out, 0),
        5: (R.o_qkv, 0, R.o_qkv, 768),
        6: (R.o_qkv, 1920, R.o_out, 384),
        7: (R.o_qkv, 384, R.o_qkv, 1152),
    }
    for j, (even, even_at, odd, odd_at) in targets.items():
        s.e(j).wait_recv()
        own = s.bufs["f"](j)[c]
        got = s.bufs["e"](j)[...]
        even[:, pl.ds(even_at, s.rounds[j].width)] = jnp.where(c == 0, own, got)
        odd[:, pl.ds(odd_at, s.rounds[j].width)] = jnp.where(c == 0, got, own)
    for k in (0, 1):
        R.o_down[48 * k : 48 * (k + 1), :] = R.fd[k]
    for j in range(2, 8):
        s.sent(j)
    v.sent()
    for copy in patch_copies:
        copy.wait()


def one_slice(patches, visible_index, visible_count, qkv_weight, out_weight, up_weight, down_weight, attention_gain, attention_shift, feedforward_gain, feedforward_shift, cotangent):
    small = jnp.stack([attention_gain, attention_shift, feedforward_gain, feedforward_shift], axis=1)
    ext = jnp.pad(small, ((0, 0), (0, EXT - 4)))
    whole = pl.BlockSpec(memory_space=pltpu.VMEM)
    anywhere = pl.BlockSpec(memory_space=pl.ANY)
    shapes = ((2, 400, 768), (2, 529, 1, 768), (24, 2304), (24, 768), (24, 3072), (96, 768), (8, 768))
    layer_out, patch_out, *grads, side = pl.pallas_call(
        mega,
        out_shape=[jax.ShapeDtypeStruct(shape, F32) for shape in shapes],
        in_specs=[pl.BlockSpec(memory_space=pltpu.SMEM), whole] + [anywhere] * 2 + [whole] * 5,
        out_specs=[anywhere] * 2 + [whole] * 5,
        scratch_shapes=list(SCRATCH.values()) + sem_shapes(GATHER_SEMS, 9) + sem_shapes(SCATTER_SEMS, 8),
        compiler_params=pltpu.CompilerParams(collective_id=0, has_side_effects=True, vmem_limit_bytes=62 * 2**20),
        name="layer_step",
    )(
        visible_count.reshape(2),
        visible_index.reshape(2, 1, 400),
        jnp.transpose(patches.reshape(2, 529, 768), (1, 0, 2)),
        cotangent.reshape(2, 400, 768),
        qkv_weight,
        out_weight,
        up_weight,
        down_weight,
        ext,
    )
    here = (lax.axis_index(AXES[0]) * 16 + lax.axis_index(AXES[1])) * 24
    own_side = lax.dynamic_slice(side, (0, here), (8, 24))
    return (layer_out[:, None], jnp.transpose(patch_out, (0, 2, 1, 3)), *grads, *(own_side[i] for i in range(4)))


def solution(mesh):
    strips = lambda n: P(None, AXES, *([None] * n))
    rows, row = P(AXES, None), P(AXES)
    body = one_slice if tuple(mesh.shape.values()) == (2, 16) else any_slice
    return jax.shard_map(
        body,
        mesh=mesh,
        in_specs=(strips(2), strips(1), strips(0), rows, rows, rows, rows, row, row, row, row, strips(2)),
        out_specs=(strips(2), strips(2), rows, rows, rows, rows, row, row, row, row),
        check_vma=False,
    )
```

```python
import jax
import jax.numpy as jnp
from jax import lax
from jax.experimental import pallas as pl
from jax.experimental.pallas import tpu as pltpu
from jax.sharding import PartitionSpec as P

HEADS = 12
AXES = ("dp", "fsdp")
MASKED = -1000000000.0
EPSILON = 1e-06
F32 = jnp.float32
BF16 = jnp.bfloat16


def norm_forward(features, scaling, offset):
    center = features - jnp.mean(features, axis=-1, keepdims=True)
    inverse = lax.rsqrt(jnp.mean(center * center, axis=-1, keepdims=True) + EPSILON)
    normed = center * inverse
    return (normed * scaling.astype(F32) + offset.astype(F32), normed, inverse)


def norm_backward(upstream, normed, inverse, scaling):
    through = upstream * scaling.astype(F32)
    inward = inverse * (
        through
        - jnp.mean(through, axis=-1, keepdims=True)
        - normed * jnp.mean(through * normed, axis=-1, keepdims=True)
    )
    return (inward, jnp.sum(upstream * normed, axis=0), jnp.sum(upstream, axis=0))


def sums(equation, left, right):
    return jnp.einsum(equation, left, right, preferred_element_type=F32)


def layer(weights, patches, indices, counts, cotangent):
    qkv_full, out_full, up_full, down_full, first_gain, first_shift, second_gain, second_shift = weights
    strips, visible, patch_count = (indices.shape[0], indices.shape[1], patches.shape[1])
    width = out_full.shape[1]
    rows = strips * visible
    heads = (strips, visible, HEADS, width // HEADS)
    scale = (width // HEADS) ** (-0.5)
    present = jnp.arange(visible)[None, :] < counts[:, None]
    onehot = ((indices[:, :, None] == jnp.arange(patch_count)[None, None, :]) & present[:, :, None]).astype(BF16)
    inputs = sums("bvp,bpd->bvd", onehot, patches).reshape(rows, width)
    first_norm, first_normed, first_inverse = norm_forward(inputs, first_gain, first_shift)
    first_low = first_norm.astype(BF16)
    projected = jnp.dot(first_low, qkv_full, preferred_element_type=F32).astype(BF16)
    queries = projected[:, :width].reshape(heads)
    keys = projected[:, width : 2 * width].reshape(heads)
    values = projected[:, 2 * width :].reshape(heads)
    scores = sums("bqhe,bkhe->bhqk", queries, keys) * scale
    scores = jnp.where(present[:, None, None, :], scores, MASKED)
    attention = jax.nn.softmax(scores, axis=-1)
    attention_low = attention.astype(BF16)
    mixed = sums("bhqk,bkhe->bqhe", attention_low, values).astype(BF16).reshape(rows, width)
    middle = inputs + jnp.dot(mixed, out_full, preferred_element_type=F32)
    second_norm, second_normed, second_inverse = norm_forward(middle, second_gain, second_shift)
    second_low = second_norm.astype(BF16)
    hidden_pre = jnp.dot(second_low, up_full, preferred_element_type=F32)
    hidden, gelu_pull = jax.vjp(lambda v: jax.nn.gelu(v, approximate=False), hidden_pre)
    hidden_low = hidden.astype(BF16)
    branch = jnp.dot(hidden_low, down_full, preferred_element_type=F32)
    live = present.reshape(rows, 1)
    output = ((middle + branch) * live.astype(F32)).reshape(strips, visible, width)

    upstream = cotangent.reshape(rows, width) * live.astype(BF16)
    down_grad = sums("rf,rd->fd", hidden_low, upstream)
    pre_low = gelu_pull(sums("rd,fd->rf", upstream, down_full))[0].astype(BF16)
    up_grad = sums("rf,rd->fd", second_low, pre_low)
    second_back = sums("rd,fd->rf", pre_low, up_full)
    inward, second_gain_grad, second_shift_grad = norm_backward(second_back, second_normed, second_inverse, second_gain)
    middle_grad = upstream.astype(F32) + inward
    middle_low = middle_grad.astype(BF16)
    out_grad = sums("rf,rd->fd", mixed, middle_low)
    mixed_grad = sums("rd,fd->rf", middle_low, out_full).astype(BF16).reshape(heads)
    prob_grad = sums("bqhe,bkhe->bhqk", mixed_grad, values)
    value_grad = sums("bhqk,bqhe->bkhe", attention_low, mixed_grad)
    score_low = (attention * (prob_grad - jnp.sum(attention * prob_grad, axis=-1, keepdims=True))).astype(BF16)
    query_grad = sums("bhqk,bkhe->bqhe", score_low, keys) * scale
    key_grad = sums("bhqk,bqhe->bkhe", score_low, queries) * scale
    projected_grad = jnp.concatenate([g.reshape(rows, width) for g in (query_grad, key_grad, value_grad)], axis=1).astype(BF16)
    qkv_grad = sums("rf,rd->fd", first_low, projected_grad)
    first_back = sums("rd,fd->rf", projected_grad, qkv_full)
    inward, first_gain_grad, first_shift_grad = norm_backward(first_back, first_normed, first_inverse, first_gain)
    input_low = (middle_grad + inward).astype(BF16).reshape(strips, visible, width)
    patch_part = sums("bvp,bvd->bpd", onehot, input_low)
    gradients = (qkv_grad, out_grad, up_grad, down_grad, first_gain_grad, first_shift_grad, second_gain_grad, second_shift_grad)
    return (output, gradients, patch_part)


def any_slice(patches, visible_index, visible_count, *rest):
    weights, cotangent = rest[:-1], rest[-1]
    whole = [lax.all_gather(w, AXES, axis=0, tiled=True) for w in weights]
    micro, strips = patches.shape[:2]
    flat = lambda a: a.reshape((micro * strips,) + a.shape[2:])
    output, gradients, patch_part = layer(whole, flat(patches), flat(visible_index), flat(visible_count), flat(cotangent))
    shares = [lax.psum_scatter(g, AXES, scatter_dimension=0, tiled=True) for g in gradients]
    back = lambda a: a.reshape((micro, strips) + a.shape[1:])
    return (back(output), back(patch_part), *shares)


MESH = pl.DeviceIdType.MESH
EXT = 128
ALL = slice(None)


def coords():
    y = lax.axis_index("dp")
    f = lax.axis_index("fsdp")
    return y, f // 4, (f // 2) % 2, f % 2


def device(y, z, x, c):
    return (y, z * 4 + x * 2 + c)


def other(z, dz):
    if dz == 0:
        return z
    if dz == 1:
        return z + 1 - 2 * (z % 2)
    if dz == 2:
        return (z + 2) % 4
    return 3 - z


def at_z(z):
    return (z // 2, z % 2)


class Round:
    def __init__(self, i, ref, lead, start, width, first):
        self.i, self.ref, self.lead, self.start, self.width = i, ref, lead, start, width
        self.halves = (pl.ds(start, first), pl.ds(start + first, width - first))
        self.cols = pl.ds(start, width)
        self.local = pl.ds(0, first), pl.ds(0, width - first)

    def at(self, par):
        def block(y, z, x, cols=None):
            before, after = self.lead(par)
            return self.ref.at[before + (y,) + z + (x,) + after + (ALL, self.cols if cols is None else cols)]

        return block


def piece(n):
    return lambda par: ((n + par,), ())


def part(n, step=1):
    return lambda par: ((), (n + step * par,))


def gather_rounds(w0, w1, wd):
    return [
        Round(0, w0, piece(0), 0, 384 + EXT, 256),
        Round(1, w1, piece(0), 0, 384, 256),
        Round(2, w0, piece(0), 384 + EXT, 384, 128),
        Round(3, w1, piece(0), 384, 384, 128),
        Round(4, w1, piece(2), 0, 768, 384),
        Round(5, w1, piece(4), 0, 768, 384),
        Round(6, wd, part(0, 2), 0, 768, 384),
        Round(7, wd, part(1, 2), 0, 384, 256),
        Round(8, wd, part(1, 2), 384, 384, 128),
    ]


def scatter_rounds(w1, gd):
    return [
        Round(0, gd, part(0, 2), 0, 768, 384),
        Round(1, gd, part(1, 2), 0, 768, 384),
        Round(2, w1, piece(2), 0, 768, 384),
        Round(3, w1, piece(4), 0, 768, 384),
        Round(4, gd, part(2), 0, 384, 256),
        Round(5, gd, part(0), 0, 384, 128),
        Round(6, gd, part(2), 384, 384, 256),
        Round(7, gd, part(0), 384, 384, 128),
    ]


class Peers:
    def __init__(self, place, rounds, sems):
        y, z, x, c = self.place = place
        self.rounds, self.sems = rounds, sems
        self.all_z, self.pair, self.odd = (ALL, ALL), (ALL, z % 2), (ALL, 1 - z % 2)
        self.x_side, self.y_side = device(y, z, 1 - x, c), device(1 - y, z, x, c)
        self.sibling = device(y, z, x, 1 - c)

    def z_peer(self, dz):
        y, z, x, c = self.place
        return device(y, other(z, dz), x, c)

    def copy(self, send, recv, j, src, dst, to):
        sent, got = self.sems
        return pltpu.make_async_remote_copy(
            src_ref=src, dst_ref=dst, send_sem=sent.at[j, send], recv_sem=got.at[j, recv], device_id=to, device_id_type=MESH
        )


class Gather(Peers):
    def same(self, send, recv, j, ref, to):
        return self.copy(send, recv, j, ref, ref, to)

    def at(self, j, par=None):
        return self.rounds[j].at(self.place[3] if par is None else par)

    def z(self, j, dz, there=0):
        y, z, x, c = self.place
        return self.same(dz - 1, dz - 1, j, self.at(j)(y, at_z(other(z, there)), x), self.z_peer(dz))

    def side(self, j, dz, axis):
        y, z, x, c = self.place
        ref = self.at(j)(y, at_z(other(z, dz)), x)
        if axis == "x":
            return self.same(3, 3 + dz % 2, j, ref, self.x_side)
        return self.same(3, 5 + dz % 2, j, ref, self.y_side)

    def sides_in(self, j, odd, axis):
        y, z, x, c = self.place
        zz = self.odd if odd else self.pair
        if axis == "x":
            return self.same(3, 3 + odd, j, self.at(j)(y, zz, 1 - x), self.x_side)
        return self.same(3, 5 + odd, j, self.at(j)(1 - y, zz, x), self.y_side)

    def diag(self, j, half, there=False):
        y, z, x, c = self.place
        cols = self.rounds[j].halves[half]
        yy = 1 - y if there or half == 1 else y
        xx = 1 - x if there or half == 0 else x
        return self.same(4, 7 + half, j, self.at(j)(yy, self.pair, xx, cols), self.y_side if half == 0 else self.x_side)

    def turn(self, j, there=False):
        y, z, x, c = self.place
        return self.same(4, 9, j, self.at(j)(1 - y, self.odd if there else self.pair, 1 - x), self.z_peer(1))

    def down(self, j, q):
        y, z, x, c = self.place
        yy = y if q < 2 else 1 - y
        xx = x if q in (0, 2) else 1 - x
        zz = self.all_z if q < 3 else self.pair if q == 3 else self.odd
        return self.same(5, 10, j, self.at(j)(yy, zz, xx), self.sibling)

    def downs(self, j, par):
        return self.same(5, 10, j, self.at(j, par)(ALL, self.all_z, ALL), self.sibling)

    def begin(self, j):
        for dz in (1, 2, 3):
            self.z(j, dz).start()

    def own(self, j):
        self.side(j, 0, "x").start()
        self.side(j, 0, "y").start()

    def forward(self, j):
        for dz in (1, 2, 3):
            self.z(j, dz, dz).wait_recv()
            self.side(j, dz, "x").start()
            self.side(j, dz, "y").start()
        self.down(j, 0).start()

    def cross(self, j):
        for half, axis in enumerate(("x", "y")):
            self.sides_in(j, 0, axis).wait_recv()
            self.diag(j, half).start()
        for half, axis in enumerate(("x", "y")):
            self.sides_in(j, 1, axis).wait_recv()
            self.down(j, 1 + half).start()

    def finish(self, j):
        self.diag(j, 0, True).wait_recv()
        self.diag(j, 1, True).wait_recv()
        self.turn(j).start()
        self.down(j, 3).start()

    def last(self, j):
        self.turn(j, True).wait_recv()
        self.down(j, 4).start()

    def arrive(self, j):
        self.downs(j, 1 - self.place[3]).wait_recv()

    def sent(self, j):
        y, z, x, c = self.place
        for dz in (1, 2, 3):
            self.z(j, dz).wait_send()
        self.same(3, 3, j, self.at(j)(y, self.all_z, ALL), self.x_side).wait_send()
        self.same(4, 7, j, self.at(j)(y, self.all_z, x), self.y_side).wait_send()
        self.downs(j, c).wait_send()


def add_to(own, got):
    own[...] = (own[...].astype(F32) + got[...].astype(F32)).astype(BF16)


class Scatter(Peers):
    def __init__(self, place, rounds, bufs, sems, free):
        super().__init__(place, rounds, sems)
        self.bufs, self.free = bufs, free

    def at(self, j, par=None):
        return self.rounds[j].at(self.place[3] if par is None else par)

    def a(self, j):
        return self.copy(0, 0, j, self.at(j, 1 - self.place[3])(ALL, self.all_z, ALL), self.bufs["a"](j), self.sibling)

    def turn(self, j):
        y, z, x, c = self.place
        return self.copy(1, 1, j, self.at(j)(1 - y, self.odd, 1 - x), self.bufs["t"](j), self.z_peer(1))

    def diag(self, j, half):
        y, z, x, c = self.place
        cols = self.rounds[j].halves[half]
        src = self.at(j)(1 - y, self.pair, 1 - x, cols)
        return self.copy(1, 2 + half, j, src, self.bufs["g"](j, half), self.y_side if half == 0 else self.x_side)

    def side(self, j, k, axis):
        y, z, x, c = self.place
        zz = self.pair if k else self.odd
        if axis == "x":
            return self.copy(2, 4 + k, j, self.at(j)(y, zz, 1 - x), self.bufs["x"](j, k), self.x_side)
        return self.copy(2, 6 + k, j, self.at(j)(1 - y, zz, x), self.bufs["y"](j, k), self.y_side)

    def d(self, j, dz):
        y, z, x, c = self.place
        return self.copy(3, 8, j, self.at(j)(y, at_z(other(z, dz)), x), self.bufs["d"](j).at[dz - 1], self.z_peer(dz))

    def ds(self, j):
        return self.copy(3, 8, j, self.bufs["d"](j), self.bufs["d"](j), self.z_peer(1))

    def e(self, j):
        return self.copy(4, 9, j, self.bufs["f"](j).at[1 - self.place[3]], self.bufs["e"](j), self.sibling)

    def begin(self, j):
        if j >= 2:
            pl.semaphore_wait(self.free.at[j % 2], 1)
        self.a(j).start()

    def add_a(self, j):
        self.a(j).wait_recv()
        at, got = self.at(j), self.bufs["a"](j)

        @pl.loop(0, 16)
        def _(i):
            y, z, x = i // 8, at_z((i // 2) % 4), i % 2
            add_to(at(y, z, x), got.at[(y,) + z + (x,)])

        self.turn(j).start()
        self.side(j, 0, "x").start()
        self.side(j, 0, "y").start()
        if j < len(self.rounds) - 2:
            pl.semaphore_signal(self.free.at[j % 2], inc=1, device_id=self.sibling, device_id_type=MESH)

    def add_t(self, j):
        y, z, x, c = self.place
        self.turn(j).wait_recv()
        for h in range(2):
            add_to(self.at(j)(1 - y, (h, z % 2), 1 - x), self.bufs["t"](j).at[h])
        self.diag(j, 0).start()
        self.diag(j, 1).start()

    def add_g(self, j):
        y, z, x, c = self.place
        first, second = self.rounds[j].halves
        self.diag(j, 0).wait_recv()
        for h in range(2):
            add_to(self.at(j)(y, (h, z % 2), 1 - x, first), self.bufs["g"](j, 0).at[h])
        self.side(j, 1, "x").start()
        self.diag(j, 1).wait_recv()
        for h in range(2):
            add_to(self.at(j)(1 - y, (h, z % 2), x, second), self.bufs["g"](j, 1).at[h])
        self.side(j, 1, "y").start()

    def add_s(self, j):
        y, z, x, c = self.place
        for k in range(2):
            self.side(j, k, "x").wait_recv()
            self.side(j, k, "y").wait_recv()
            low = z % 2 if k else 1 - z % 2

            @pl.loop(0, 2)
            def _(h):
                own = self.at(j)(y, (h, low), x)
                both = self.bufs["x"](j, k)[h].astype(F32) + self.bufs["y"](j, k)[h].astype(F32)
                own[...] = (own[...].astype(F32) + both).astype(BF16)

        for dz in (1, 2, 3):
            self.d(j, dz).start()

    def add_d(self, j):
        y, z, x, c = self.place
        self.ds(j).wait_recv()
        total = self.at(j)(y, at_z(z), x)[...].astype(F32)
        for dz in (1, 2, 3):
            total = total + self.bufs["d"](j)[dz - 1].astype(F32)
        out = self.bufs["f"](j)
        if j < 2:
            out[...] = total
        else:
            out[0] = total[:24]
            out[1] = total[24:]
            self.e(j).start()

    def sent(self, j):
        y, z, x, c = self.place
        at = self.at(j)
        self.a(j).wait_send()
        self.copy(1, 1, j, at(y, self.all_z, x), at(y, self.all_z, x), self.z_peer(1)).wait_send()
        self.copy(2, 4, j, at(y, self.all_z, ALL), at(y, self.all_z, ALL), self.x_side).wait_send()
        self.ds(j).wait_send()
        if j > 1:
            self.e(j).wait_send()


class Total(Peers):
    def __init__(self, place, side, send, recv):
        super().__init__(place, None, None)
        self.side, self.sems = side, (send, recv)
        self.peers = (self.sibling, self.x_side, self.y_side, self.z_peer(1), self.z_peer(2))

    def step(self, i):
        return self.copy(0, 0, i, self.side.at[i], self.side.at[5 + i], self.peers[i])

    def begin(self):
        self.step(0).start()

    def add(self, i):
        self.step(i).wait_recv()
        total = self.side[i] + self.side[5 + i]
        if i < 4:
            self.side[i + 1] = total
            self.step(i + 1).start()
        return total

    def sent(self):
        for i in range(5):
            self.step(i).wait_send()


def sem_shapes(rounds, sends, receives):
    return [pltpu.SemaphoreType.DMA((rounds, n)) for n in (sends, receives)]


def mm(a, b):
    return lax.dot_general(a, b, (((1,), (0,)), ((), ())), preferred_element_type=F32)


def mt(a, b):
    return lax.dot_general(a, b, (((1,), (1,)), ((), ())), preferred_element_type=F32)


def tm(a, b):
    return lax.dot_general(a, b, (((0,), (0,)), ((), ())), preferred_element_type=F32)


def lanes(i, n):
    return pl.ds(pl.multiple_of(i * n, 128), n)


def rows_at(i, n):
    return pl.ds(pl.multiple_of(i * n, 16), n)


def normal(v):
    center = v - jnp.mean(v, axis=-1, keepdims=True)
    inverse = lax.rsqrt(jnp.mean(center * center, axis=-1, keepdims=True) + EPSILON)
    return center * inverse, inverse


def gelu_parts(v):
    cdf = 0.5 * lax.erf(v * (0.5**0.5)) + 0.5
    return v * cdf, cdf + v * jnp.exp2(v * v * (-0.5 * 1.4426950408889634) - 1.3257480647361593)


class Layer:
    def __init__(self, r):
        self.__dict__.update(r)

    def weight(self, p, start=0, width=768):
        if p < 2:
            return self.w0[p, :, :, :, :, :, pl.ds(EXT + start, width)].reshape(768, width)
        return self.w1[p - 2, :, :, :, :, :, pl.ds(start, width)].reshape(768, width)

    def live(self, s, shape, axis):
        return lax.broadcasted_iota(jnp.int32, shape, axis) < self.count[s]

    def take(self):
        @pl.loop(0, 2)
        def _(s):
            row = lax.broadcasted_iota(jnp.int32, (1058, 400), 0)
            hot = (row == 2 * self.index[s] + s) & self.live(s, (1058, 400), 1)
            got = tm(hot.astype(F32).astype(BF16), self.pool[...].reshape(1058, 768))
            self.inputs[rows_at(s, 400), :] = got.astype(BF16)
            self.ups[s] = jnp.where(self.live(s, (400, 768), 0), self.ups[s], jnp.zeros((), BF16))

    def gains(self):
        side = self.w0[0, :, :, :, :, :, pl.ds(0, EXT)].reshape(768, EXT).astype(F32)
        self.gain[...] = side.T[0:8]

    def first(self):
        @pl.loop(0, 2)
        def _(s):
            normed, _ = normal(self.inputs[rows_at(s, 400), :].astype(F32))
            self.first_low[rows_at(s, 400), :] = (normed * self.gain[0:1] + self.gain[1:2]).astype(BF16)

    def project(self, half, pieces):
        start = 384 * half
        w = jnp.concatenate([self.weight(p, start, 384) for p in pieces], axis=1)

        got = mm(self.first_low[...], w).astype(BF16)
        for i, p in enumerate(pieces):
            self.proj[:, pl.ds(768 * p + start, 384)] = got[:, 384 * i : 384 * (i + 1)]

    def last_keys(self, s, shape, axis):
        return lax.broadcasted_iota(jnp.int32, shape, axis) + 384 < self.count[s]

    def attend(self, i):
        s, t = i % 2, i // 2
        rows = rows_at(s, 400)
        q, k, v = (self.proj[rows, lanes(6 * p + t, 128)] for p in range(3))
        lane = lax.broadcasted_iota(jnp.int32, (400, 128), 1)
        alive = self.last_keys(s, (400, 16), 1)
        halves = (lane < 64, lane >= 64)
        eighth = q * jnp.asarray(0.125, BF16)
        scores = [mt(jnp.where(mine, eighth, jnp.zeros((), BF16)), k) for mine in halves]
        scores = jnp.concatenate([jnp.concatenate([x[:, :384], jnp.where(alive, x[:, 384:], MASKED)], axis=1) for x in scores], axis=0)
        top = jnp.max(scores, axis=1, keepdims=True)
        e = jnp.exp(scores - top)
        total = jnp.sum(e, axis=1, keepdims=True)
        e = e.astype(BF16)
        mixed = jnp.concatenate([mm(e[400 * h : 400 * (h + 1)], v) for h in range(2)], axis=0) * (1.0 / total)
        self.mixed[rows, lanes(t, 128)] = jnp.where(halves[0], mixed[:400], mixed[400:]).astype(BF16)
        logs = top + jnp.log(total)
        stat = self.stat[s, pl.ds(0, 400), :]
        for h in range(2):
            stat = jnp.where(lane == 2 * t + h, logs[400 * h : 400 * (h + 1)], stat)
        self.stat[s, pl.ds(0, 400), :] = stat

    def turn_stat(self):
        for s in range(2):
            self.turned[s] = self.stat[s].T[0:16]

    def mix(self):
        w = self.weight(3)
        @pl.loop(0, 2)
        def _(s):
            rows = rows_at(s, 400)
            middle = self.inputs[rows, :].astype(F32) + mm(self.mixed[rows, :], w)
            self.mid[s, pl.ds(0, 400), :] = middle
            normed, _ = normal(middle)
            self.second_low[rows, :] = (normed * self.gain[2:3] + self.gain[3:4]).astype(BF16)

    def hide(self, p):
        w = self.weight(4 + p)
        cols = pl.ds(768 * p, 768)
        for s in range(2):
            rows = pl.ds(400 * s, 400)
            act, slope = gelu_parts(mm(self.second_low[rows, :], w))
            self.hidden[rows, cols] = act.astype(BF16)
            self.slope[rows, cols] = slope.astype(BF16)

    def down_terms(self, chunks):
        left = jnp.concatenate([self.hidden[:, pl.ds(384 * i, 384)] for i in chunks], axis=1)
        g = tm(left, self.ups[...].reshape(800, 768)).astype(BF16)
        for n, i in enumerate(chunks):
            self.gd[i // 4, (i % 4) // 2, i % 2] = g[384 * n : 384 * (n + 1)].reshape(2, 4, 48, 768)

    def branch(self, n, stage):
        w = self.wd[:, :, :, :, :, :, lanes(n, 256)].reshape(3072, 256)
        for s in range(2):
            got = mm(self.hidden[pl.ds(400 * s, 400), :], w)
            got = (got + self.mid[s, pl.ds(0, 400), lanes(n, 256)]) * self.live(s, (400, 256), 0).astype(F32)
            stage[s] = got

    def hide_back(self, p):
        w = self.wd[p // 2, p % 2].reshape(768, 768)
        cols = pl.ds(768 * p, 768)
        for s in range(2):
            rows = pl.ds(400 * s, 400)
            self.slope[rows, cols] = (mt(self.ups[s], w) * self.slope[rows, cols].astype(F32)).astype(BF16)

    def up_terms(self, p):
        g = tm(self.second_low[...], self.slope[:, pl.ds(768 * p, 768)])
        self.g1[2 + p] = g.astype(BF16).reshape(2, 2, 2, 2, 48, 768)

    def second_back(self, s):
        if s == 0:
            self.vec[0] = jnp.zeros((8, 768), F32)
        rows = pl.ds(400 * s, 400)
        back = mt(self.slope[rows, :], jnp.concatenate([self.weight(4 + p) for p in range(4)], axis=1))
        normed, inverse = normal(self.mid[s, pl.ds(0, 400), :])
        inward, dg, db = self.norm_back(back, normed, inverse, self.gain[2:3])
        self.ups[s] = (self.ups[s].astype(F32) + inward).astype(BF16)
        self.vec[0, 2:3] += dg
        self.vec[0, 3:4] += db

    def norm_back(self, back, normed, inverse, gain):
        through = back * gain
        inward = inverse * (
            through
            - jnp.mean(through, axis=-1, keepdims=True)
            - normed * jnp.mean(through * normed, axis=-1, keepdims=True)
        )
        return inward, jnp.sum(back * normed, axis=0, keepdims=True), jnp.sum(back, axis=0, keepdims=True)

    def mix_back(self):
        w = self.weight(3)
        self.second_low[...] = mt(self.ups[...].reshape(800, 768), w).astype(BF16)

    def out_terms(self):
        g = tm(self.mixed[...], self.ups[...].reshape(800, 768))
        self.gd[:, :, :, :, 3] = g.astype(BF16).reshape(2, 2, 2, 2, 48, 768)

    def attend_back(self, i):
        s, t = i % 2, i // 2
        rows = rows_at(s, 400)
        q, k, v = (self.proj[rows, lanes(6 * p + t, 128)] for p in range(3))
        do = self.second_low[rows, lanes(t, 128)]
        first_half = lax.broadcasted_iota(jnp.int32, (400, 128), 1) < 64
        alive = self.last_keys(s, (16, 400), 0)
        zero = jnp.zeros((), BF16)
        halves = (first_half, ~first_half)
        eighth = k * jnp.asarray(0.125, BF16)
        scores = [mt(jnp.where(mine, eighth, zero), q) for mine in halves]
        shares = []
        for h in range(2):
            p = jnp.exp(scores[h] - self.turned[s, pl.ds(2 * t + h, 1), pl.ds(0, 400)])
            shares.append(jnp.concatenate([p[:384], jnp.where(alive, p[384:], 0.0)], axis=0))
        dv = mm(jnp.concatenate([p.astype(BF16) for p in shares], axis=0), do)
        back = [mt(jnp.where(mine, v, zero), do) for mine in halves]
        ds = [(p * (dp - jnp.sum(p * dp, axis=0, keepdims=True))).astype(BF16) for p, dp in zip(shares, back)]
        dk = mm(jnp.concatenate(ds, axis=0), q)
        dq = [tm(x, k) for x in ds]
        for i, (first, second, scale) in enumerate(((dq[0], dq[1], 0.125), (dk[:400], dk[400:], 0.125), (dv[:400], dv[400:], 1.0))):
            g = jnp.where(first_half, first, second) * scale
            self.proj[rows, lanes(6 * i + t, 128)] = g.astype(BF16)

    def project_terms(self, half):
        start = 384 * half

        right = jnp.concatenate([self.proj[:, pl.ds(768 * p + start, 384)] for p in range(3)], axis=1)
        g = tm(self.first_low[...], right).astype(BF16)
        for p in range(3):
            self.gd[:, :, :, :, p, :, pl.ds(start, 384)] = g[:, 384 * p : 384 * (p + 1)].reshape(2, 2, 2, 2, 48, 384)

    def first_back(self, s):
        rows = pl.ds(400 * s, 400)
        back = mt(self.proj[rows, :], jnp.concatenate([self.weight(p) for p in range(3)], axis=1))
        normed, inverse = normal(self.inputs[rows, :].astype(F32))
        inward, dg, db = self.norm_back(back, normed, inverse, self.gain[0:1])
        self.ups[s] = (self.ups[s].astype(F32) + inward).astype(BF16)
        self.vec[0, 0:1] += dg
        self.vec[0, 1:2] += db

    def give(self):
        @pl.loop(0, 2)
        def _(s):
            at = lax.broadcasted_iota(jnp.int32, (529, 400), 0)
            hot = (at == self.index[s]) & self.live(s, (529, 400), 1)
            self.mid[s] = mm(hot.astype(F32).astype(BF16), self.ups[s])


W_SHAPES = ((2, 2, 2, 2, 2, 48, 768 + EXT), (6, 2, 2, 2, 2, 48, 768), (2, 2, 2, 2, 4, 48, 768))


def greet(place):
    y, z, x, c = place
    barrier = pltpu.get_barrier_semaphore()
    peers = [device(y, z, x, 1 - c), device(y, z, 1 - x, c), device(1 - y, z, x, c)]
    peers += [device(y, other(z, dz), x, c) for dz in (1, 2, 3)]
    for peer in peers:
        pl.semaphore_signal(barrier, inc=1, device_id=peer, device_id_type=MESH)
    return lambda: pl.semaphore_wait(barrier, len(peers))


class Shards:
    def __init__(self, place, own, weights, sent, got, sems):
        self.place, self.own, self.weights = place, own, weights
        self.sent, self.got, self.sems = sent, got, sems

    def width(self, j):
        return 768 + EXT if j == 0 else 768

    def piece(self, p):
        qkv, out, up, _, ext = self.own
        if p == 3:
            return out[...].astype(F32)
        if p > 3:
            return up[:, 768 * (p - 4) : 768 * (p - 3)].astype(F32)
        v = qkv[:, 768 * p : 768 * (p + 1)].astype(F32)
        return jnp.concatenate([ext[...].astype(F32), v], axis=1) if p < 2 else v

    def copy(self, j):
        y, z, x, c = self.place
        cols = pl.ds(0, self.width(j))
        return pltpu.make_async_remote_copy(
            src_ref=self.sent.at[j, :, cols],
            dst_ref=self.got.at[j, :, cols],
            send_sem=self.sems.at[0, j],
            recv_sem=self.sems.at[1, j],
            device_id=device(y, z, x, 1 - c),
            device_id_type=MESH,
        )

    def stage(self, j):
        c = self.place[3]
        self.sent[j, :, pl.ds(0, self.width(j))] = jnp.where(c == 0, self.piece(2 * j + 1), self.piece(2 * j))

    def build(self, j):
        y, z, x, c = self.place
        mine = jnp.where(c == 0, self.piece(2 * j), self.piece(2 * j + 1))
        self.copy(j).wait_recv()
        got = self.got[j, :, pl.ds(0, self.width(j))]
        both = jnp.where(c == 0, jnp.concatenate([mine, got], axis=0), jnp.concatenate([got, mine], axis=0))
        if j == 0:
            self.weights[0][c, y, z // 2, z % 2, x] = both.astype(BF16)
        else:
            self.weights[1][2 * (j - 1) + c, y, z // 2, z % 2, x] = both.astype(BF16)

    def close(self):
        for j in range(4):
            self.copy(j).wait_send()

    def build_down(self):
        y, z, x, c = self.place
        for k in (0, 1):
            self.weights[2][y, z // 2, z % 2, x, 2 * c + k] = self.own[3][48 * k : 48 * (k + 1), :]


class Refs:
    pass


def bf16(*shape):
    return pltpu.VMEM(shape, BF16)


def f32(*shape):
    return pltpu.VMEM(shape, F32)


INS = ["count", "index", "patches", "cot", "qkv", "out", "up", "down", "ext"]
OUTS = ["layer_out", "patch_out", "o_qkv", "o_out", "o_up", "o_down", "o_side"]
SCRATCH = dict(
    w0=bf16(*W_SHAPES[0]), w1=bf16(*W_SHAPES[1]), wd=bf16(*W_SHAPES[2]), gd=bf16(*W_SHAPES[2]),
    inputs=bf16(800, 768), first_low=bf16(800, 768), proj=bf16(800, 2304), mixed=bf16(800, 768),
    mid=f32(2, 529, 768), second_low=bf16(800, 768), hidden=bf16(800, 3072), slope=bf16(800, 3072),
    ups=bf16(2, 400, 768), gain=f32(8, 768), pool=bf16(529, 2, 768), stage=f32(2, 400, 256),
    stat=f32(2, 512, 128), turned=f32(2, 16, 512), vec=f32(10, 8, 768),
    s0=f32(4, 24, 768 + EXT), r0=f32(4, 24, 768 + EXT), ra=bf16(2, 2, 2, 2, 2, 48, 768),
    rt=bf16(4, 2, 48, 768), rx=bf16(4, 2, 2, 48, 768), ry=bf16(4, 2, 2, 48, 768), rg=bf16(4, 2, 2, 48, 384), rd=bf16(4, 3, 48, 768),
    ht=bf16(4, 2, 48, 384), hx=bf16(4, 2, 2, 48, 384), hy=bf16(4, 2, 2, 48, 384), hg=bf16(4, 2, 2, 48, 256), hd=bf16(4, 3, 48, 384),
    fd=f32(2, 48, 768), fs=f32(6, 2, 24, 768), re=f32(6, 24, 768),
    free=pltpu.SemaphoreType.REGULAR((2,)), pair=pltpu.SemaphoreType.DMA((2, 4)), local=pltpu.SemaphoreType.DMA((4,)), vs=pltpu.SemaphoreType.DMA((5, 1)), vr=pltpu.SemaphoreType.DMA((5, 1)),
)


def make_scatter(place, R, sems):
    rounds = scatter_rounds(R.w1, R.gd)

    def pick(full, half):
        return lambda j, *at: full.at[(j,) + at] if j < 4 else half.at[(j - 4,) + at]

    def corner(j, half):
        cols = rounds[j].local[half]
        return R.rg.at[j, half] if j < 4 else R.hg.at[j - 4, half, :, :, cols]

    bufs = dict(
        a=lambda j: R.ra.at[j % 2, :, :, :, :, :, pl.ds(0, rounds[j].width)],
        t=pick(R.rt, R.ht),
        x=pick(R.rx, R.hx),
        y=pick(R.ry, R.hy),
        g=corner,
        d=pick(R.rd, R.hd),
        f=lambda j: R.fd.at[j] if j < 2 else R.fs.at[j - 2, :, :, pl.ds(0, rounds[j].width)],
        e=lambda j: R.re.at[j - 2, :, pl.ds(0, rounds[j].width)],
    )
    return Scatter(place, rounds, bufs, sems, R.free)


def mega(*refs):
    names = INS + OUTS + list(SCRATCH)
    r = dict(zip(names, refs))
    n = len(names)
    m = n + 2
    R = Refs()
    R.__dict__.update(r)
    R.g1 = R.w1
    place = coords()
    c = place[3]
    weights = (R.w0, R.w1, R.wd)
    cot_copy = pltpu.make_async_copy(R.cot, R.ups, R.local.at[0])
    cot_copy.start()
    patch_in = pltpu.make_async_copy(R.patches, R.pool, R.local.at[3])
    patch_in.start()
    met = greet(place)
    shards = Shards(place, (R.qkv, R.out, R.up, R.down, R.ext), weights, R.s0, R.r0, R.pair)
    g = Gather(place, gather_rounds(*weights), refs[n:m])
    v = Total(place, R.vec, R.vs, R.vr)

    s = make_scatter(place, R, refs[m:])
    L = Layer(R.__dict__)
    patch_copies = [pltpu.make_async_copy(R.mid.at[i], R.patch_out.at[i, :, 0, :], R.local.at[i]) for i in (0, 1)]

    def give():
        L.give()
        for copy in patch_copies:
            copy.start()


    def branch(k):
        copies = [pltpu.make_async_copy(R.stage, R.layer_out.at[:, :, pl.ds(256 * i, 256)], R.local.at[2]) for i in (k - 1, k)]
        if k:
            copies[0].wait()
        L.branch(k, R.stage)
        copies[1].start()
        if k == 2:
            copies[1].wait()


    def start(j):
        g.begin(j)
        g.own(j)

    for j in range(4):
        shards.stage(j)
    shards.build_down()
    met()
    for j in range(4):
        shards.copy(j).start()
    shards.build(0)
    start(0)
    shards.build(1)
    start(1)
    shards.build(2)
    shards.build(3)
    cot_copy.wait()
    patch_in.wait()
    L.take()

    def over(step, first, last):
        pl.loop(first, last)(step)

    qk, v_only = (0, 1), (2,)

    def close():
        for j in range(9):
            g.sent(j)
        shards.close()

    plan = [
        (g.forward, 0), (g.forward, 1), (g.cross, 0), (start, 2), (g.finish, 0), (g.cross, 1), (start, 3), (g.last, 0),
        (g.forward, 2), (g.finish, 1), (g.arrive, 0), (start, 4), (L.gains,), (L.first,), (L.project, 0, qk),
        (g.forward, 3), (g.cross, 2), (g.last, 1), (g.arrive, 1), (start, 5), (L.project, 0, v_only), (over, L.attend, 0, 4),
        (g.finish, 2), (g.cross, 3), (g.forward, 4), (over, L.attend, 4, 6), (g.last, 2), (g.finish, 3), (start, 6), (g.arrive, 2), (L.project, 1, qk),
        (g.cross, 4), (g.forward, 5), (g.last, 3), (g.arrive, 3), (L.project, 1, v_only), (start, 7), (start, 8), (g.finish, 4),
        (over, L.attend, 6, 10), (g.cross, 5), (g.forward, 6), (over, L.attend, 10, 12), (L.mix,), (L.turn_stat,),
        (g.last, 4), (g.finish, 5), (g.arrive, 4), (L.hide, 0), (g.forward, 7), (L.hide, 1), (L.down_terms, (0, 1)),
        (g.cross, 6), (g.last, 5), (g.forward, 8), (g.arrive, 5), (L.down_terms, (2, 3)), (g.cross, 7), (L.hide, 2), (g.finish, 6),
        (L.hide, 3), (g.cross, 8), (L.down_terms, (4, 5)), (g.last, 6), (g.finish, 7), (g.finish, 8), (L.down_terms, (6, 7)),
        (s.begin, 0), (s.begin, 1), (g.last, 7), (g.last, 8), (g.arrive, 6), (g.arrive, 7), (g.arrive, 8),
        (s.add_a, 0), (s.add_a, 1), (L.hide_back, 0), (L.hide_back, 1), (L.hide_back, 2), (L.hide_back, 3),
        (s.add_t, 0), (L.second_back, 0), (s.add_t, 1), (s.add_g, 0), (L.second_back, 1), (close,), (s.add_g, 1),
        (L.up_terms, 0), (L.up_terms, 1), (s.begin, 2), (s.add_s, 0), (L.up_terms, 2), (s.add_a, 2), (L.up_terms, 3), (s.begin, 3),
        (s.add_s, 1), (L.mix_back,), (s.add_a, 3), (over, L.attend_back, 0, 3), (s.add_t, 2),
        (over, L.attend_back, 3, 5), (s.add_g, 2), (s.add_t, 3), (over, L.attend_back, 5, 6), (s.add_d, 0), (s.add_d, 1), (s.sent, 0), (s.sent, 1),
        (L.project_terms, 0), (s.add_g, 3), (L.out_terms,), (s.begin, 4), (s.begin, 5), (s.add_s, 2), (over, L.attend_back, 6, 8), (s.add_a, 4), (s.add_a, 5),
        (over, L.attend_back, 8, 10), (s.add_s, 3), (over, L.attend_back, 10, 12), (s.add_t, 4), (s.add_t, 5), (L.project_terms, 1),
        (s.begin, 6), (s.begin, 7), (s.add_g, 4), (s.add_g, 5), (s.add_a, 6), (s.add_a, 7), (L.first_back, 0), (s.add_t, 6), (s.add_s, 4), (L.first_back, 1), (v.begin,),
        (s.add_t, 7), (s.add_g, 6), (s.add_s, 5), (branch, 0), (s.add_g, 7), (v.add, 0), (branch, 1), (s.add_s, 6), (v.add, 1), (s.add_s, 7),
        (s.add_d, 2), (s.add_d, 3), (branch, 2), (v.add, 2), (s.add_d, 4), (s.add_d, 5), (give,), (v.add, 3), (s.add_d, 6), (s.add_d, 7),
    ]
    for step, *at in plan:
        step(*at)
    R.o_side[...] = v.add(4)
    targets = {
        2: (R.o_up, 0, R.o_up, 768),
        3: (R.o_up, 1536, R.o_up, 2304),
        4: (R.o_qkv, 1536, R.o_out, 0),
        5: (R.o_qkv, 0, R.o_qkv, 768),
        6: (R.o_qkv, 1920, R.o_out, 384),
        7: (R.o_qkv, 384, R.o_qkv, 1152),
    }
    for j, (even, even_at, odd, odd_at) in targets.items():
        s.e(j).wait_recv()
        own = s.bufs["f"](j)[c]
        got = s.bufs["e"](j)[...]
        even[:, pl.ds(even_at, s.rounds[j].width)] = jnp.where(c == 0, own, got)
        odd[:, pl.ds(odd_at, s.rounds[j].width)] = jnp.where(c == 0, got, own)
    for k in (0, 1):
        R.o_down[48 * k : 48 * (k + 1), :] = R.fd[k]
    for j in range(2, 8):
        s.sent(j)
    v.sent()
    for copy in patch_copies:
        copy.wait()


def one_slice(patches, visible_index, visible_count, qkv_weight, out_weight, up_weight, down_weight, attention_gain, attention_shift, feedforward_gain, feedforward_shift, cotangent):
    small = jnp.stack([attention_gain, attention_shift, feedforward_gain, feedforward_shift], axis=1)
    ext = jnp.pad(small, ((0, 0), (0, EXT - 4)))
    whole = pl.BlockSpec(memory_space=pltpu.VMEM)
    anywhere = pl.BlockSpec(memory_space=pl.ANY)
    shapes = ((2, 400, 768), (2, 529, 1, 768), (24, 2304), (24, 768), (24, 3072), (96, 768), (8, 768))
    layer_out, patch_out, *grads, side = pl.pallas_call(
        mega,
        out_shape=[jax.ShapeDtypeStruct(shape, F32) for shape in shapes],
        in_specs=[pl.BlockSpec(memory_space=pltpu.SMEM), whole] + [anywhere] * 2 + [whole] * 5,
        out_specs=[anywhere] * 2 + [whole] * 5,
        scratch_shapes=list(SCRATCH.values()) + sem_shapes(9, 6, 11) + sem_shapes(8, 5, 10),
        compiler_params=pltpu.CompilerParams(collective_id=0, has_side_effects=True, vmem_limit_bytes=62 * 2**20),
        name="layer_step",
    )(
        visible_count.reshape(2),
        visible_index.reshape(2, 1, 400),
        jnp.transpose(patches.reshape(2, 529, 768), (1, 0, 2)),
        cotangent.reshape(2, 400, 768),
        qkv_weight,
        out_weight,
        up_weight,
        down_weight,
        ext,
    )
    here = (lax.axis_index(AXES[0]) * 16 + lax.axis_index(AXES[1])) * 24
    own_side = lax.dynamic_slice(side, (0, here), (8, 24))
    return (layer_out[:, None], jnp.transpose(patch_out, (0, 2, 1, 3)), *grads, *(own_side[i] for i in range(4)))


def solution(mesh):
    strips = lambda n: P(None, AXES, *([None] * n))
    rows, row = P(AXES, None), P(AXES)
    body = one_slice if tuple(mesh.shape.values()) == (2, 16) else any_slice
    return jax.shard_map(
        body,
        mesh=mesh,
        in_specs=(strips(2), strips(1), strips(0), rows, rows, rows, rows, row, row, row, row, strips(2)),
        out_specs=(strips(2), strips(2), rows, rows, rows, rows, row, row, row, row),
        check_vma=False,
    )
```

```python
import jax
import jax.numpy as jnp
from jax import lax
from jax.experimental import pallas as pl
from jax.experimental.pallas import tpu as pltpu
from jax.sharding import PartitionSpec as P

HEADS = 12
AXES = ("dp", "fsdp")
MASKED = -1000000000.0
EPSILON = 1e-06
F32 = jnp.float32
BF16 = jnp.bfloat16


def norm_forward(features, scaling, offset):
    center = features - jnp.mean(features, axis=-1, keepdims=True)
    inverse = lax.rsqrt(jnp.mean(center * center, axis=-1, keepdims=True) + EPSILON)
    normed = center * inverse
    return (normed * scaling.astype(F32) + offset.astype(F32), normed, inverse)


def norm_backward(upstream, normed, inverse, scaling):
    through = upstream * scaling.astype(F32)
    inward = inverse * (
        through
        - jnp.mean(through, axis=-1, keepdims=True)
        - normed * jnp.mean(through * normed, axis=-1, keepdims=True)
    )
    return (inward, jnp.sum(upstream * normed, axis=0), jnp.sum(upstream, axis=0))


def sums(equation, left, right):
    return jnp.einsum(equation, left, right, preferred_element_type=F32)


def layer(weights, patches, indices, counts, cotangent):
    qkv_full, out_full, up_full, down_full, first_gain, first_shift, second_gain, second_shift = weights
    strips, visible, patch_count = (indices.shape[0], indices.shape[1], patches.shape[1])
    width = out_full.shape[1]
    rows = strips * visible
    heads = (strips, visible, HEADS, width // HEADS)
    scale = (width // HEADS) ** (-0.5)
    present = jnp.arange(visible)[None, :] < counts[:, None]
    onehot = ((indices[:, :, None] == jnp.arange(patch_count)[None, None, :]) & present[:, :, None]).astype(BF16)
    inputs = sums("bvp,bpd->bvd", onehot, patches).reshape(rows, width)
    first_norm, first_normed, first_inverse = norm_forward(inputs, first_gain, first_shift)
    first_low = first_norm.astype(BF16)
    projected = jnp.dot(first_low, qkv_full, preferred_element_type=F32).astype(BF16)
    queries = projected[:, :width].reshape(heads)
    keys = projected[:, width : 2 * width].reshape(heads)
    values = projected[:, 2 * width :].reshape(heads)
    scores = sums("bqhe,bkhe->bhqk", queries, keys) * scale
    scores = jnp.where(present[:, None, None, :], scores, MASKED)
    attention = jax.nn.softmax(scores, axis=-1)
    attention_low = attention.astype(BF16)
    mixed = sums("bhqk,bkhe->bqhe", attention_low, values).astype(BF16).reshape(rows, width)
    middle = inputs + jnp.dot(mixed, out_full, preferred_element_type=F32)
    second_norm, second_normed, second_inverse = norm_forward(middle, second_gain, second_shift)
    second_low = second_norm.astype(BF16)
    hidden_pre = jnp.dot(second_low, up_full, preferred_element_type=F32)
    hidden, gelu_pull = jax.vjp(lambda v: jax.nn.gelu(v, approximate=False), hidden_pre)
    hidden_low = hidden.astype(BF16)
    branch = jnp.dot(hidden_low, down_full, preferred_element_type=F32)
    live = present.reshape(rows, 1)
    output = ((middle + branch) * live.astype(F32)).reshape(strips, visible, width)

    upstream = cotangent.reshape(rows, width) * live.astype(BF16)
    down_grad = sums("rf,rd->fd", hidden_low, upstream)
    pre_low = gelu_pull(sums("rd,fd->rf", upstream, down_full))[0].astype(BF16)
    up_grad = sums("rf,rd->fd", second_low, pre_low)
    second_back = sums("rd,fd->rf", pre_low, up_full)
    inward, second_gain_grad, second_shift_grad = norm_backward(second_back, second_normed, second_inverse, second_gain)
    middle_grad = upstream.astype(F32) + inward
    middle_low = middle_grad.astype(BF16)
    out_grad = sums("rf,rd->fd", mixed, middle_low)
    mixed_grad = sums("rd,fd->rf", middle_low, out_full).astype(BF16).reshape(heads)
    prob_grad = sums("bqhe,bkhe->bhqk", mixed_grad, values)
    value_grad = sums("bhqk,bqhe->bkhe", attention_low, mixed_grad)
    score_low = (attention * (prob_grad - jnp.sum(attention * prob_grad, axis=-1, keepdims=True))).astype(BF16)
    query_grad = sums("bhqk,bkhe->bqhe", score_low, keys) * scale
    key_grad = sums("bhqk,bqhe->bkhe", score_low, queries) * scale
    projected_grad = jnp.concatenate([g.reshape(rows, width) for g in (query_grad, key_grad, value_grad)], axis=1).astype(BF16)
    qkv_grad = sums("rf,rd->fd", first_low, projected_grad)
    first_back = sums("rd,fd->rf", projected_grad, qkv_full)
    inward, first_gain_grad, first_shift_grad = norm_backward(first_back, first_normed, first_inverse, first_gain)
    input_low = (middle_grad + inward).astype(BF16).reshape(strips, visible, width)
    patch_part = sums("bvp,bvd->bpd", onehot, input_low)
    gradients = (qkv_grad, out_grad, up_grad, down_grad, first_gain_grad, first_shift_grad, second_gain_grad, second_shift_grad)
    return (output, gradients, patch_part)


def any_slice(patches, visible_index, visible_count, *rest):
    weights, cotangent = rest[:-1], rest[-1]
    whole = [lax.all_gather(w, AXES, axis=0, tiled=True) for w in weights]
    micro, strips = patches.shape[:2]
    flat = lambda a: a.reshape((micro * strips,) + a.shape[2:])
    output, gradients, patch_part = layer(whole, flat(patches), flat(visible_index), flat(visible_count), flat(cotangent))
    shares = [lax.psum_scatter(g, AXES, scatter_dimension=0, tiled=True) for g in gradients]
    back = lambda a: a.reshape((micro, strips) + a.shape[1:])
    return (back(output), back(patch_part), *shares)


MESH = pl.DeviceIdType.MESH
EXT = 128
ALL = slice(None)


def coords():
    y = lax.axis_index("dp")
    f = lax.axis_index("fsdp")
    return y, f // 4, (f // 2) % 2, f % 2


def device(y, z, x, c):
    return (y, z * 4 + x * 2 + c)


def other(z, dz):
    if dz == 0:
        return z
    if dz == 1:
        return z + 1 - 2 * (z % 2)
    if dz == 2:
        return (z + 2) % 4
    return 3 - z


def at_z(z):
    return (z // 2, z % 2)


class Round:
    def __init__(self, i, ref, lead, start, width, first):
        self.i, self.ref, self.lead, self.start, self.width = i, ref, lead, start, width
        self.halves = (pl.ds(start, first), pl.ds(start + first, width - first))
        self.cols = pl.ds(start, width)
        self.local = pl.ds(0, first), pl.ds(0, width - first)

    def at(self, par):
        def block(y, z, x, cols=None):
            before, after = self.lead(par)
            return self.ref.at[before + (y,) + z + (x,) + after + (ALL, self.cols if cols is None else cols)]

        return block


def piece(n):
    return lambda par: ((n + par,), ())


def part(n, step=1):
    return lambda par: ((), (n + step * par,))


def gather_rounds(w0, w1, wd):
    return [
        Round(0, w0, piece(0), 0, 384 + EXT, 256),
        Round(1, w1, piece(0), 0, 384, 256),
        Round(2, w0, piece(0), 384 + EXT, 384, 128),
        Round(3, w1, piece(0), 384, 384, 128),
        Round(4, w1, piece(2), 0, 768, 384),
        Round(5, w1, piece(4), 0, 768, 384),
        Round(6, wd, part(0, 2), 0, 768, 384),
        Round(7, wd, part(1, 2), 0, 384, 256),
        Round(8, wd, part(1, 2), 384, 384, 128),
    ]


def scatter_rounds(w1, gd):
    return [
        Round(0, gd, part(0, 2), 0, 768, 384),
        Round(1, gd, part(1, 2), 0, 768, 384),
        Round(2, w1, piece(2), 0, 768, 384),
        Round(3, w1, piece(4), 0, 768, 384),
        Round(4, gd, part(2), 0, 384, 256),
        Round(5, gd, part(0), 0, 384, 128),
        Round(6, gd, part(2), 384, 384, 256),
        Round(7, gd, part(0), 384, 384, 128),
    ]


class Peers:
    def __init__(self, place, rounds, sems):
        y, z, x, c = self.place = place
        self.rounds, self.sems = rounds, sems
        self.all_z, self.pair, self.odd = (ALL, ALL), (ALL, z % 2), (ALL, 1 - z % 2)
        self.x_side, self.y_side = device(y, z, 1 - x, c), device(1 - y, z, x, c)
        self.sibling = device(y, z, x, 1 - c)

    def z_peer(self, dz):
        y, z, x, c = self.place
        return device(y, other(z, dz), x, c)

    def copy(self, send, recv, j, src, dst, to):
        sent, got = self.sems
        return pltpu.make_async_remote_copy(
            src_ref=src, dst_ref=dst, send_sem=sent.at[j, send], recv_sem=got.at[j, recv], device_id=to, device_id_type=MESH
        )


class Gather(Peers):
    def same(self, send, recv, j, ref, to):
        return self.copy(send, recv, j, ref, ref, to)

    def at(self, j, par=None):
        return self.rounds[j].at(self.place[3] if par is None else par)

    def z(self, j, dz, there=0):
        y, z, x, c = self.place
        return self.same(dz - 1, dz - 1, j, self.at(j)(y, at_z(other(z, there)), x), self.z_peer(dz))

    def side(self, j, dz, axis):
        y, z, x, c = self.place
        ref = self.at(j)(y, at_z(other(z, dz)), x)
        if axis == "x":
            return self.same(3, 3 + dz % 2, j, ref, self.x_side)
        return self.same(3, 5 + dz % 2, j, ref, self.y_side)

    def sides_in(self, j, odd, axis):
        y, z, x, c = self.place
        zz = self.odd if odd else self.pair
        if axis == "x":
            return self.same(3, 3 + odd, j, self.at(j)(y, zz, 1 - x), self.x_side)
        return self.same(3, 5 + odd, j, self.at(j)(1 - y, zz, x), self.y_side)

    def diag(self, j, half, there=False):
        y, z, x, c = self.place
        cols = self.rounds[j].halves[half]
        yy = 1 - y if there or half == 1 else y
        xx = 1 - x if there or half == 0 else x
        return self.same(4, 7 + half, j, self.at(j)(yy, self.pair, xx, cols), self.y_side if half == 0 else self.x_side)

    def turn(self, j, there=False):
        y, z, x, c = self.place
        return self.same(4, 9, j, self.at(j)(1 - y, self.odd if there else self.pair, 1 - x), self.z_peer(1))

    def down(self, j, q):
        y, z, x, c = self.place
        yy = y if q < 2 else 1 - y
        xx = x if q in (0, 2) else 1 - x
        zz = self.all_z if q < 3 else self.pair if q == 3 else self.odd
        return self.same(5, 10, j, self.at(j)(yy, zz, xx), self.sibling)

    def downs(self, j, par):
        return self.same(5, 10, j, self.at(j, par)(ALL, self.all_z, ALL), self.sibling)

    def begin(self, j):
        for dz in (1, 2, 3):
            self.z(j, dz).start()

    def own(self, j):
        self.side(j, 0, "x").start()
        self.side(j, 0, "y").start()

    def forward(self, j):
        for dz in (1, 2, 3):
            self.z(j, dz, dz).wait_recv()
            self.side(j, dz, "x").start()
            self.side(j, dz, "y").start()
        self.down(j, 0).start()

    def cross(self, j):
        for half, axis in enumerate(("x", "y")):
            self.sides_in(j, 0, axis).wait_recv()
            self.diag(j, half).start()
        for half, axis in enumerate(("x", "y")):
            self.sides_in(j, 1, axis).wait_recv()
            self.down(j, 1 + half).start()

    def finish(self, j):
        self.diag(j, 0, True).wait_recv()
        self.diag(j, 1, True).wait_recv()
        self.turn(j).start()
        self.down(j, 3).start()

    def last(self, j):
        self.turn(j, True).wait_recv()
        self.down(j, 4).start()

    def arrive(self, j):
        self.downs(j, 1 - self.place[3]).wait_recv()

    def sent(self, j):
        y, z, x, c = self.place
        for dz in (1, 2, 3):
            self.z(j, dz).wait_send()
        self.same(3, 3, j, self.at(j)(y, self.all_z, ALL), self.x_side).wait_send()
        self.same(4, 7, j, self.at(j)(y, self.all_z, x), self.y_side).wait_send()
        self.downs(j, c).wait_send()


def add_to(own, got):
    own[...] = (own[...].astype(F32) + got[...].astype(F32)).astype(BF16)


class Scatter(Peers):
    def __init__(self, place, rounds, bufs, sems, free):
        super().__init__(place, rounds, sems)
        self.bufs, self.free = bufs, free

    def at(self, j, par=None):
        return self.rounds[j].at(self.place[3] if par is None else par)

    def a(self, j):
        return self.copy(0, 0, j, self.at(j, 1 - self.place[3])(ALL, self.all_z, ALL), self.bufs["a"](j), self.sibling)

    def turn(self, j):
        y, z, x, c = self.place
        return self.copy(1, 1, j, self.at(j)(1 - y, self.odd, 1 - x), self.bufs["t"](j), self.z_peer(1))

    def diag(self, j, half):
        y, z, x, c = self.place
        cols = self.rounds[j].halves[half]
        src = self.at(j)(1 - y, self.pair, 1 - x, cols)
        return self.copy(1, 2 + half, j, src, self.bufs["g"](j, half), self.y_side if half == 0 else self.x_side)

    def side(self, j, k, axis):
        y, z, x, c = self.place
        zz = self.pair if k else self.odd
        if axis == "x":
            return self.copy(2, 4 + k, j, self.at(j)(y, zz, 1 - x), self.bufs["x"](j, k), self.x_side)
        return self.copy(2, 6 + k, j, self.at(j)(1 - y, zz, x), self.bufs["y"](j, k), self.y_side)

    def d(self, j, dz):
        y, z, x, c = self.place
        return self.copy(3, 8, j, self.at(j)(y, at_z(other(z, dz)), x), self.bufs["d"](j).at[dz - 1], self.z_peer(dz))

    def ds(self, j):
        return self.copy(3, 8, j, self.bufs["d"](j), self.bufs["d"](j), self.z_peer(1))

    def e(self, j):
        return self.copy(4, 9, j, self.bufs["f"](j).at[1 - self.place[3]], self.bufs["e"](j), self.sibling)

    def begin(self, j):
        if j >= 2:
            pl.semaphore_wait(self.free.at[j % 2], 1)
        self.a(j).start()

    def add_a(self, j):
        self.a(j).wait_recv()
        at, got = self.at(j), self.bufs["a"](j)

        @pl.loop(0, 16)
        def _(i):
            y, z, x = i // 8, at_z((i // 2) % 4), i % 2
            add_to(at(y, z, x), got.at[(y,) + z + (x,)])

        self.turn(j).start()
        self.side(j, 0, "x").start()
        self.side(j, 0, "y").start()
        if j < len(self.rounds) - 2:
            pl.semaphore_signal(self.free.at[j % 2], inc=1, device_id=self.sibling, device_id_type=MESH)

    def add_t(self, j):
        y, z, x, c = self.place
        self.turn(j).wait_recv()
        for h in range(2):
            add_to(self.at(j)(1 - y, (h, z % 2), 1 - x), self.bufs["t"](j).at[h])
        self.diag(j, 0).start()
        self.diag(j, 1).start()

    def add_g(self, j):
        y, z, x, c = self.place
        first, second = self.rounds[j].halves
        self.diag(j, 0).wait_recv()
        for h in range(2):
            add_to(self.at(j)(y, (h, z % 2), 1 - x, first), self.bufs["g"](j, 0).at[h])
        self.side(j, 1, "x").start()
        self.diag(j, 1).wait_recv()
        for h in range(2):
            add_to(self.at(j)(1 - y, (h, z % 2), x, second), self.bufs["g"](j, 1).at[h])
        self.side(j, 1, "y").start()

    def add_s(self, j):
        y, z, x, c = self.place
        for k in range(2):
            self.side(j, k, "x").wait_recv()
            self.side(j, k, "y").wait_recv()
            low = z % 2 if k else 1 - z % 2

            @pl.loop(0, 2)
            def _(h):
                own = self.at(j)(y, (h, low), x)
                both = self.bufs["x"](j, k)[h].astype(F32) + self.bufs["y"](j, k)[h].astype(F32)
                own[...] = (own[...].astype(F32) + both).astype(BF16)

        for dz in (1, 2, 3):
            self.d(j, dz).start()

    def add_d(self, j):
        y, z, x, c = self.place
        self.ds(j).wait_recv()
        total = self.at(j)(y, at_z(z), x)[...].astype(F32)
        for dz in (1, 2, 3):
            total = total + self.bufs["d"](j)[dz - 1].astype(F32)
        out = self.bufs["f"](j)
        if j < 2:
            out[...] = total
        else:
            out[0] = total[:24]
            out[1] = total[24:]
            self.e(j).start()

    def sent(self, j):
        y, z, x, c = self.place
        at = self.at(j)
        self.a(j).wait_send()
        self.copy(1, 1, j, at(y, self.all_z, x), at(y, self.all_z, x), self.z_peer(1)).wait_send()
        self.copy(2, 4, j, at(y, self.all_z, ALL), at(y, self.all_z, ALL), self.x_side).wait_send()
        self.ds(j).wait_send()
        if j > 1:
            self.e(j).wait_send()


class Total(Peers):
    def __init__(self, place, side, send, recv):
        super().__init__(place, None, (send, recv))
        self.side = side

    def step(self, i):
        if i == 1:
            return [self.copy(0, 0, 1, self.side.at[1], self.side.at[4 + dz], self.z_peer(dz)) for dz in (1, 2, 3)]
        peer = (self.sibling, None, self.x_side, self.y_side)[i]
        at = (4, None, 8, 9)[i]
        return [self.copy(0, 0, i, self.side.at[i], self.side.at[at], peer)]

    def whole(self, i):
        got = self.side.at[pl.ds((4, 5, 8, 9)[i], 3 if i == 1 else 1)]
        return self.copy(0, 0, i, got, got, self.sibling)

    def begin(self):
        self.step(0)[0].start()

    def add(self, i):
        self.whole(i).wait_recv()
        total = self.side[i]
        for n in ((4,), (5, 6, 7), (8,), (9,))[i]:
            total = total + self.side[n]
        if i < 3:
            self.side[i + 1] = total
            for copy in self.step(i + 1):
                copy.start()
        return total

    def sent(self):
        for i in range(4):
            self.whole(i).wait_send()


def sem_shapes(rounds, sends, receives):
    return [pltpu.SemaphoreType.DMA((rounds, n)) for n in (sends, receives)]


def mm(a, b):
    return lax.dot_general(a, b, (((1,), (0,)), ((), ())), preferred_element_type=F32)


def mt(a, b):
    return lax.dot_general(a, b, (((1,), (1,)), ((), ())), preferred_element_type=F32)


def tm(a, b):
    return lax.dot_general(a, b, (((0,), (0,)), ((), ())), preferred_element_type=F32)


def lanes(i, n):
    return pl.ds(pl.multiple_of(i * n, 128), n)


def rows_at(i, n):
    return pl.ds(pl.multiple_of(i * n, 16), n)


def normal(v):
    center = v - jnp.mean(v, axis=-1, keepdims=True)
    inverse = lax.rsqrt(jnp.mean(center * center, axis=-1, keepdims=True) + EPSILON)
    return center * inverse, inverse


def gelu_parts(v):
    cdf = 0.5 * lax.erf(v * (0.5**0.5)) + 0.5
    return v * cdf, cdf + v * jnp.exp2(v * v * (-0.5 * 1.4426950408889634) - 1.3257480647361593)


class Layer:
    def __init__(self, r):
        self.__dict__.update(r)

    def weight(self, p, start=0, width=768):
        if p < 2:
            return self.w0[p, :, :, :, :, :, pl.ds(EXT + start, width)].reshape(768, width)
        return self.w1[p - 2, :, :, :, :, :, pl.ds(start, width)].reshape(768, width)

    def live(self, s, shape, axis):
        return lax.broadcasted_iota(jnp.int32, shape, axis) < self.count[s]

    def take(self):
        @pl.loop(0, 2)
        def _(s):
            row = lax.broadcasted_iota(jnp.int32, (1058, 400), 0)
            hot = (row == 2 * self.index[s] + s) & self.live(s, (1058, 400), 1)
            got = tm(hot.astype(F32).astype(BF16), self.pool[...].reshape(1058, 768))
            self.inputs[rows_at(s, 400), :] = got.astype(BF16)
            self.ups[s] = jnp.where(self.live(s, (400, 768), 0), self.ups[s], jnp.zeros((), BF16))

    def gains(self):
        side = self.w0[0, :, :, :, :, :, pl.ds(0, EXT)].reshape(768, EXT).astype(F32)
        self.gain[...] = side.T[0:8]

    def first(self):
        @pl.loop(0, 2)
        def _(s):
            normed, _ = normal(self.inputs[rows_at(s, 400), :].astype(F32))
            self.first_low[rows_at(s, 400), :] = (normed * self.gain[0:1] + self.gain[1:2]).astype(BF16)

    def project(self, half, pieces):
        start = 384 * half
        w = jnp.concatenate([self.weight(p, start, 384) for p in pieces], axis=1)

        got = mm(self.first_low[...], w).astype(BF16)
        for i, p in enumerate(pieces):
            self.proj[:, pl.ds(768 * p + start, 384)] = got[:, 384 * i : 384 * (i + 1)]

    def last_keys(self, s, shape, axis):
        return lax.broadcasted_iota(jnp.int32, shape, axis) + 384 < self.count[s]

    def attend(self, i):
        s, t = i % 2, i // 2
        rows = rows_at(s, 400)
        q, k, v = (self.proj[rows, lanes(6 * p + t, 128)] for p in range(3))
        lane = lax.broadcasted_iota(jnp.int32, (400, 128), 1)
        alive = self.last_keys(s, (400, 16), 1)
        halves = (lane < 64, lane >= 64)
        eighth = q * jnp.asarray(0.125, BF16)
        scores = [mt(jnp.where(mine, eighth, jnp.zeros((), BF16)), k) for mine in halves]
        scores = jnp.concatenate([jnp.concatenate([x[:, :384], jnp.where(alive, x[:, 384:], MASKED)], axis=1) for x in scores], axis=0)
        top = jnp.max(scores, axis=1, keepdims=True)
        e = jnp.exp(scores - top)
        total = jnp.sum(e, axis=1, keepdims=True)
        e = e.astype(BF16)
        mixed = jnp.concatenate([mm(e[400 * h : 400 * (h + 1)], v) for h in range(2)], axis=0) * (1.0 / total)
        self.mixed[rows, lanes(t, 128)] = jnp.where(halves[0], mixed[:400], mixed[400:]).astype(BF16)
        logs = top + jnp.log(total)
        stat = self.stat[s, pl.ds(0, 400), :]
        for h in range(2):
            stat = jnp.where(lane == 2 * t + h, logs[400 * h : 400 * (h + 1)], stat)
        self.stat[s, pl.ds(0, 400), :] = stat

    def turn_stat(self):
        for s in range(2):
            self.turned[s] = self.stat[s].T[0:16]

    def mix(self):
        w = self.weight(3)
        @pl.loop(0, 2)
        def _(s):
            rows = rows_at(s, 400)
            middle = self.inputs[rows, :].astype(F32) + mm(self.mixed[rows, :], w)
            self.mid[s, pl.ds(0, 400), :] = middle
            normed, _ = normal(middle)
            self.second_low[rows, :] = (normed * self.gain[2:3] + self.gain[3:4]).astype(BF16)

    def hide(self, p):
        w = self.weight(4 + p)
        cols = pl.ds(768 * p, 768)
        for s in range(2):
            rows = pl.ds(400 * s, 400)
            act, slope = gelu_parts(mm(self.second_low[rows, :], w))
            self.hidden[rows, cols] = act.astype(BF16)
            self.slope[rows, cols] = slope.astype(BF16)

    def down_terms(self, chunks):
        left = jnp.concatenate([self.hidden[:, pl.ds(384 * i, 384)] for i in chunks], axis=1)
        g = tm(left, self.ups[...].reshape(800, 768)).astype(BF16)
        for n, i in enumerate(chunks):
            self.gd[i // 4, (i % 4) // 2, i % 2] = g[384 * n : 384 * (n + 1)].reshape(2, 4, 48, 768)

    def branch(self, n, stage):
        w = self.wd[:, :, :, :, :, :, lanes(n, 256)].reshape(3072, 256)
        for s in range(2):
            got = mm(self.hidden[pl.ds(400 * s, 400), :], w)
            got = (got + self.mid[s, pl.ds(0, 400), lanes(n, 256)]) * self.live(s, (400, 256), 0).astype(F32)
            stage[s] = got

    def hide_back(self, p):
        w = self.wd[p // 2, p % 2].reshape(768, 768)
        cols = pl.ds(768 * p, 768)
        for s in range(2):
            rows = pl.ds(400 * s, 400)
            self.slope[rows, cols] = (mt(self.ups[s], w) * self.slope[rows, cols].astype(F32)).astype(BF16)

    def up_terms(self, p):
        g = tm(self.second_low[...], self.slope[:, pl.ds(768 * p, 768)])
        self.g1[2 + p] = g.astype(BF16).reshape(2, 2, 2, 2, 48, 768)

    def second_back(self, s):
        if s == 0:
            self.vec[0] = jnp.zeros((8, 768), F32)
        rows = pl.ds(400 * s, 400)
        back = mt(self.slope[rows, :], jnp.concatenate([self.weight(4 + p) for p in range(4)], axis=1))
        normed, inverse = normal(self.mid[s, pl.ds(0, 400), :])
        inward, dg, db = self.norm_back(back, normed, inverse, self.gain[2:3])
        self.ups[s] = (self.ups[s].astype(F32) + inward).astype(BF16)
        self.vec[0, 2:3] += dg
        self.vec[0, 3:4] += db

    def norm_back(self, back, normed, inverse, gain):
        through = back * gain
        inward = inverse * (
            through
            - jnp.mean(through, axis=-1, keepdims=True)
            - normed * jnp.mean(through * normed, axis=-1, keepdims=True)
        )
        return inward, jnp.sum(back * normed, axis=0, keepdims=True), jnp.sum(back, axis=0, keepdims=True)

    def mix_back(self):
        w = self.weight(3)
        self.second_low[...] = mt(self.ups[...].reshape(800, 768), w).astype(BF16)

    def out_terms(self):
        g = tm(self.mixed[...], self.ups[...].reshape(800, 768))
        self.gd[:, :, :, :, 3] = g.astype(BF16).reshape(2, 2, 2, 2, 48, 768)

    def attend_back(self, i):
        s, t = i % 2, i // 2
        rows = rows_at(s, 400)
        q, k, v = (self.proj[rows, lanes(6 * p + t, 128)] for p in range(3))
        do = self.second_low[rows, lanes(t, 128)]
        first_half = lax.broadcasted_iota(jnp.int32, (400, 128), 1) < 64
        alive = self.last_keys(s, (16, 400), 0)
        zero = jnp.zeros((), BF16)
        halves = (first_half, ~first_half)
        eighth = k * jnp.asarray(0.125, BF16)
        scores = [mt(jnp.where(mine, eighth, zero), q) for mine in halves]
        shares = []
        for h in range(2):
            p = jnp.exp(scores[h] - self.turned[s, pl.ds(2 * t + h, 1), pl.ds(0, 400)])
            shares.append(jnp.concatenate([p[:384], jnp.where(alive, p[384:], 0.0)], axis=0))
        dv = mm(jnp.concatenate([p.astype(BF16) for p in shares], axis=0), do)
        back = [mt(jnp.where(mine, v, zero), do) for mine in halves]
        ds = [(p * (dp - jnp.sum(p * dp, axis=0, keepdims=True))).astype(BF16) for p, dp in zip(shares, back)]
        dk = mm(jnp.concatenate(ds, axis=0), q)
        dq = [tm(x, k) for x in ds]
        for i, (first, second, scale) in enumerate(((dq[0], dq[1], 0.125), (dk[:400], dk[400:], 0.125), (dv[:400], dv[400:], 1.0))):
            g = jnp.where(first_half, first, second) * scale
            self.proj[rows, lanes(6 * i + t, 128)] = g.astype(BF16)

    def project_terms(self, half):
        start = 384 * half

        right = jnp.concatenate([self.proj[:, pl.ds(768 * p + start, 384)] for p in range(3)], axis=1)
        g = tm(self.first_low[...], right).astype(BF16)
        for p in range(3):
            self.gd[:, :, :, :, p, :, pl.ds(start, 384)] = g[:, 384 * p : 384 * (p + 1)].reshape(2, 2, 2, 2, 48, 384)

    def first_back(self, s):
        rows = pl.ds(400 * s, 400)
        back = mt(self.proj[rows, :], jnp.concatenate([self.weight(p) for p in range(3)], axis=1))
        normed, inverse = normal(self.inputs[rows, :].astype(F32))
        inward, dg, db = self.norm_back(back, normed, inverse, self.gain[0:1])
        self.ups[s] = (self.ups[s].astype(F32) + inward).astype(BF16)
        self.vec[0, 0:1] += dg
        self.vec[0, 1:2] += db


W_SHAPES = ((2, 2, 2, 2, 2, 48, 768 + EXT), (6, 2, 2, 2, 2, 48, 768), (2, 2, 2, 2, 4, 48, 768))


def greet(place):
    y, z, x, c = place
    barrier = pltpu.get_barrier_semaphore()
    peers = [device(y, z, x, 1 - c), device(y, z, 1 - x, c), device(1 - y, z, x, c)]
    peers += [device(y, other(z, dz), x, c) for dz in (1, 2, 3)]
    for peer in peers:
        pl.semaphore_signal(barrier, inc=1, device_id=peer, device_id_type=MESH)
    return lambda: pl.semaphore_wait(barrier, len(peers))


class Shards:
    def __init__(self, place, own, weights, sent, got, sems):
        self.place, self.own, self.weights = place, own, weights
        self.sent, self.got, self.sems = sent, got, sems

    def width(self, j):
        return 768 + EXT if j == 0 else 768

    def piece(self, p):
        qkv, out, up, _, ext = self.own
        if p == 3:
            return out[...].astype(F32)
        if p > 3:
            return up[:, 768 * (p - 4) : 768 * (p - 3)].astype(F32)
        v = qkv[:, 768 * p : 768 * (p + 1)].astype(F32)
        return jnp.concatenate([ext[...].astype(F32), v], axis=1) if p < 2 else v

    def copy(self, j):
        y, z, x, c = self.place
        cols = pl.ds(0, self.width(j))
        return pltpu.make_async_remote_copy(
            src_ref=self.sent.at[j, :, cols],
            dst_ref=self.got.at[j, :, cols],
            send_sem=self.sems.at[0, j],
            recv_sem=self.sems.at[1, j],
            device_id=device(y, z, x, 1 - c),
            device_id_type=MESH,
        )

    def stage(self, j):
        c = self.place[3]
        self.sent[j, :, pl.ds(0, self.width(j))] = jnp.where(c == 0, self.piece(2 * j + 1), self.piece(2 * j))

    def build(self, j):
        y, z, x, c = self.place
        mine = jnp.where(c == 0, self.piece(2 * j), self.piece(2 * j + 1))
        self.copy(j).wait_recv()
        got = self.got[j, :, pl.ds(0, self.width(j))]
        both = jnp.where(c == 0, jnp.concatenate([mine, got], axis=0), jnp.concatenate([got, mine], axis=0))
        if j == 0:
            self.weights[0][c, y, z // 2, z % 2, x] = both.astype(BF16)
        else:
            self.weights[1][2 * (j - 1) + c, y, z // 2, z % 2, x] = both.astype(BF16)

    def close(self):
        for j in range(4):
            self.copy(j).wait_send()

    def build_down(self):
        y, z, x, c = self.place
        for k in (0, 1):
            self.weights[2][y, z // 2, z % 2, x, 2 * c + k] = self.own[3][48 * k : 48 * (k + 1), :]


class Refs:
    pass


def bf16(*shape):
    return pltpu.VMEM(shape, BF16)


def f32(*shape):
    return pltpu.VMEM(shape, F32)


INS = ["count", "index", "patches", "cot", "qkv", "out", "up", "down", "ext"]
OUTS = ["layer_out", "low_out", "o_qkv", "o_out", "o_up", "o_down", "o_side"]
SCRATCH = dict(
    w0=bf16(*W_SHAPES[0]), w1=bf16(*W_SHAPES[1]), wd=bf16(*W_SHAPES[2]), gd=bf16(*W_SHAPES[2]),
    inputs=bf16(800, 768), first_low=bf16(800, 768), proj=bf16(800, 2304), mixed=bf16(800, 768),
    mid=f32(2, 529, 768), second_low=bf16(800, 768), hidden=bf16(800, 3072), slope=bf16(800, 3072),
    ups=bf16(2, 400, 768), gain=f32(8, 768), pool=bf16(529, 2, 768), stage=f32(2, 400, 256),
    stat=f32(2, 512, 128), turned=f32(2, 16, 512), vec=f32(10, 8, 768),
    s0=f32(4, 24, 768 + EXT), r0=f32(4, 24, 768 + EXT), ra=bf16(2, 2, 2, 2, 2, 48, 768),
    rt=bf16(4, 2, 48, 768), rx=bf16(4, 2, 2, 48, 768), ry=bf16(4, 2, 2, 48, 768), rg=bf16(4, 2, 2, 48, 384), rd=bf16(4, 3, 48, 768),
    ht=bf16(4, 2, 48, 384), hx=bf16(4, 2, 2, 48, 384), hy=bf16(4, 2, 2, 48, 384), hg=bf16(4, 2, 2, 48, 256), hd=bf16(4, 3, 48, 384),
    fd=f32(2, 48, 768), fs=f32(6, 2, 24, 768), re=f32(6, 24, 768),
    free=pltpu.SemaphoreType.REGULAR((2,)), pair=pltpu.SemaphoreType.DMA((2, 4)), local=pltpu.SemaphoreType.DMA((4,)), vs=pltpu.SemaphoreType.DMA((4, 1)), vr=pltpu.SemaphoreType.DMA((4, 1)),
)


def make_scatter(place, R, sems):
    rounds = scatter_rounds(R.w1, R.gd)

    def pick(full, half):
        return lambda j, *at: full.at[(j,) + at] if j < 4 else half.at[(j - 4,) + at]

    def corner(j, half):
        cols = rounds[j].local[half]
        return R.rg.at[j, half] if j < 4 else R.hg.at[j - 4, half, :, :, cols]

    bufs = dict(
        a=lambda j: R.ra.at[j % 2, :, :, :, :, :, pl.ds(0, rounds[j].width)],
        t=pick(R.rt, R.ht),
        x=pick(R.rx, R.hx),
        y=pick(R.ry, R.hy),
        g=corner,
        d=pick(R.rd, R.hd),
        f=lambda j: R.fd.at[j] if j < 2 else R.fs.at[j - 2, :, :, pl.ds(0, rounds[j].width)],
        e=lambda j: R.re.at[j - 2, :, pl.ds(0, rounds[j].width)],
    )
    return Scatter(place, rounds, bufs, sems, R.free)


def mega(*refs):
    names = INS + OUTS + list(SCRATCH)
    r = dict(zip(names, refs))
    n = len(names)
    m = n + 2
    R = Refs()
    R.__dict__.update(r)
    R.g1 = R.w1
    place = coords()
    c = place[3]
    weights = (R.w0, R.w1, R.wd)
    cot_copy = pltpu.make_async_copy(R.cot, R.ups, R.local.at[0])
    cot_copy.start()
    patch_in = pltpu.make_async_copy(R.patches, R.pool, R.local.at[3])
    patch_in.start()
    met = greet(place)
    shards = Shards(place, (R.qkv, R.out, R.up, R.down, R.ext), weights, R.s0, R.r0, R.pair)
    g = Gather(place, gather_rounds(*weights), refs[n:m])
    v = Total(place, R.vec, R.vs, R.vr)

    s = make_scatter(place, R, refs[m:])
    L = Layer(R.__dict__)
    low_copy = pltpu.make_async_copy(R.ups, R.low_out, R.local.at[0])

    def branch(k):
        copies = [pltpu.make_async_copy(R.stage, R.layer_out.at[:, :, pl.ds(256 * i, 256)], R.local.at[2]) for i in (k - 1, k)]
        if k:
            copies[0].wait()
        L.branch(k, R.stage)
        copies[1].start()
        if k == 2:
            copies[1].wait()


    def start(j):
        g.begin(j)
        g.own(j)

    for j in range(4):
        shards.stage(j)
    shards.build_down()
    met()
    for j in range(4):
        shards.copy(j).start()
    shards.build(0)
    start(0)
    shards.build(1)
    start(1)
    shards.build(2)
    shards.build(3)
    cot_copy.wait()
    patch_in.wait()
    L.take()

    def over(step, first, last):
        pl.loop(first, last)(step)

    qk, v_only = (0, 1), (2,)

    def close():
        for j in range(9):
            g.sent(j)
        shards.close()

    plan = [
        (g.forward, 0), (g.forward, 1), (g.cross, 0), (start, 2), (g.finish, 0), (g.cross, 1), (start, 3), (g.last, 0),
        (g.forward, 2), (g.finish, 1), (start, 4), (g.arrive, 0), (L.gains,), (L.first,), (L.project, 0, qk),
        (g.forward, 3), (g.cross, 2), (g.last, 1), (start, 5), (g.arrive, 1), (L.project, 0, v_only), (over, L.attend, 0, 2),
        (g.finish, 2), (g.cross, 3), (g.forward, 4), (over, L.attend, 2, 4), (start, 6), (g.last, 2), (g.finish, 3), (over, L.attend, 4, 6),
        (g.arrive, 2), (g.cross, 4), (g.forward, 5), (L.project, 1, qk), (g.last, 3), (g.finish, 4), (start, 7), (start, 8), (g.arrive, 3),
        (L.project, 1, v_only), (over, L.attend, 6, 10), (g.cross, 5), (g.forward, 6), (over, L.attend, 10, 12), (L.mix,), (L.turn_stat,),
        (g.last, 4), (g.finish, 5), (g.forward, 7), (g.arrive, 4), (L.hide, 0), (L.hide, 1), (g.cross, 6), (g.last, 5), (g.forward, 8),
        (L.down_terms, (0, 1)), (g.arrive, 5), (g.cross, 7), (L.hide, 2), (g.finish, 6), (L.hide, 3), (g.cross, 8),
        (L.down_terms, (2, 3)), (g.last, 6), (g.finish, 7), (L.down_terms, (4, 5)), (g.finish, 8), (L.down_terms, (6, 7)),
        (s.begin, 0), (g.last, 7), (g.last, 8), (g.arrive, 6), (g.arrive, 7), (g.arrive, 8), (s.begin, 1), (s.add_a, 0),
        (L.hide_back, 0), (L.hide_back, 1), (s.add_a, 1), (L.hide_back, 2), (L.hide_back, 3),
        (s.add_t, 0), (L.second_back, 0), (s.add_t, 1), (L.second_back, 1), (s.add_g, 0), (close,),
        (L.up_terms, 0), (L.up_terms, 1), (s.begin, 2), (s.add_g, 1), (L.up_terms, 2), (s.add_s, 0), (L.up_terms, 3), (s.add_a, 2), (s.begin, 3),
        (L.mix_back,), (s.add_s, 1), (over, L.attend_back, 0, 1), (s.add_a, 3), (over, L.attend_back, 1, 4), (s.add_t, 2),
        (over, L.attend_back, 4, 6), (s.add_g, 2), (s.add_d, 0), (s.add_d, 1), (s.sent, 0), (s.sent, 1),
        (L.project_terms, 0), (s.add_t, 3), (L.out_terms,), (s.begin, 4), (s.begin, 5), (s.add_s, 2), (over, L.attend_back, 6, 7), (s.add_g, 3), (s.add_a, 4),
        (over, L.attend_back, 7, 8), (s.add_a, 5), (over, L.attend_back, 8, 10), (s.add_t, 4), (s.add_s, 3), (over, L.attend_back, 10, 12), (L.project_terms, 1),
        (s.begin, 6), (s.begin, 7), (s.add_t, 5), (s.add_g, 4), (s.add_a, 6), (s.add_d, 3), (s.add_a, 7), (L.first_back, 0), (s.add_g, 5), (s.add_t, 6), (s.add_s, 4),
        (L.first_back, 1), (v.begin,), (low_copy.start,), (s.add_t, 7), (s.add_s, 5), (branch, 0), (s.add_g, 6), (v.add, 0), (s.add_g, 7), (branch, 1),
        (s.add_s, 6), (s.add_d, 2), (branch, 2), (s.add_s, 7), (v.add, 1), (s.add_d, 4), (s.add_d, 5), (v.add, 2),
        (s.add_d, 6), (s.add_d, 7),
    ]
    for step, *at in plan:
        step(*at)
    R.o_side[...] = v.add(3)
    targets = {
        2: (R.o_up, 0, R.o_up, 768),
        3: (R.o_up, 1536, R.o_up, 2304),
        4: (R.o_qkv, 1536, R.o_out, 0),
        5: (R.o_qkv, 0, R.o_qkv, 768),
        6: (R.o_qkv, 1920, R.o_out, 384),
        7: (R.o_qkv, 384, R.o_qkv, 1152),
    }
    for j, (even, even_at, odd, odd_at) in targets.items():
        s.e(j).wait_recv()
        own = s.bufs["f"](j)[c]
        got = s.bufs["e"](j)[...]
        even[:, pl.ds(even_at, s.rounds[j].width)] = jnp.where(c == 0, own, got)
        odd[:, pl.ds(odd_at, s.rounds[j].width)] = jnp.where(c == 0, got, own)
    for k in (0, 1):
        R.o_down[48 * k : 48 * (k + 1), :] = R.fd[k]
    for j in range(2, 8):
        s.sent(j)
    v.sent()
    low_copy.wait()


def finish(count, index, low, side, *refs):
    given, (patch_out, side_out), taken, held, (mid, sems) = refs[:5], refs[5:7], refs[7:12], refs[12:17], refs[17:]
    to = [pltpu.make_async_copy(a, b, sems.at[2 + i]) for i, (a, b) in enumerate(zip(given, held))]
    back = [pltpu.make_async_copy(a, b, sems.at[7 + i]) for i, (a, b) in enumerate(zip(held, taken))]
    for copy in to:
        copy.start()
    outs = [pltpu.make_async_copy(mid.at[s], patch_out.at[s, :, 0, :], sems.at[s]) for s in range(2)]
    for s in range(2):
        hot = lax.broadcasted_iota(jnp.int32, (529, 400), 0) == index[s]
        hot = hot & (lax.broadcasted_iota(jnp.int32, (529, 400), 1) < count[s])
        mid[s] = mm(hot.astype(F32).astype(BF16), low[s])
        outs[s].start()
    for first, second in zip(to, back):
        first.wait()
        second.start()
    here = (lax.axis_index(AXES[0]) * 16 + lax.axis_index(AXES[1])) * 24
    side_out[...] = pltpu.roll(side[...], 768 - here, 1)[:, :EXT]
    for copy in outs + back:
        copy.wait()


def one_slice(patches, visible_index, visible_count, qkv_weight, out_weight, up_weight, down_weight, attention_gain, attention_shift, feedforward_gain, feedforward_shift, cotangent):
    small = jnp.stack([attention_gain, attention_shift, feedforward_gain, feedforward_shift], axis=1)
    ext = jnp.pad(small, ((0, 0), (0, EXT - 4)))
    whole = pl.BlockSpec(memory_space=pltpu.VMEM)
    anywhere = pl.BlockSpec(memory_space=pl.ANY)
    smem = pl.BlockSpec(memory_space=pltpu.SMEM)
    shapes = ((2, 400, 768), (2, 400, 768), (24, 2304), (24, 768), (24, 3072), (96, 768), (8, 768))
    types = (F32, BF16, F32, F32, F32, F32, F32)
    counts, index = visible_count.reshape(2), visible_index.reshape(2, 1, 400)
    layer_out, low, *grads, side = pl.pallas_call(
        mega,
        out_shape=[jax.ShapeDtypeStruct(*shape) for shape in zip(shapes, types)],
        in_specs=[smem, whole] + [anywhere] * 2 + [whole] * 5,
        out_specs=[anywhere] * 2 + [whole] * 5,
        scratch_shapes=list(SCRATCH.values()) + sem_shapes(9, 6, 11) + sem_shapes(8, 5, 10),
        compiler_params=pltpu.CompilerParams(collective_id=0, has_side_effects=True, vmem_limit_bytes=62 * 2**20),
        name="layer_step",
    )(
        counts,
        index,
        jnp.transpose(patches.reshape(2, 529, 768), (1, 0, 2)),
        cotangent.reshape(2, 400, 768),
        qkv_weight,
        out_weight,
        up_weight,
        down_weight,
        ext,
    )
    results = [jax.ShapeDtypeStruct(shape, F32) for shape in shapes[:1] + shapes[2:6]]
    patch_out, own_side, layer_out, *grads = pl.pallas_call(
        finish,
        out_shape=[jax.ShapeDtypeStruct((2, 529, 1, 768), F32), jax.ShapeDtypeStruct((8, EXT), F32)] + results,
        in_specs=[smem] + [whole] * 3 + [anywhere] * 5,
        out_specs=[anywhere, whole] + [anywhere] * 5,
        scratch_shapes=[pltpu.VMEM(a.shape, F32) for a in results] + [f32(2, 529, 768), pltpu.SemaphoreType.DMA((12,))],
        compiler_params=pltpu.CompilerParams(vmem_limit_bytes=62 * 2**20),
        name="finish",
    )(counts, index, low, side, layer_out, *grads)
    return (layer_out[:, None], jnp.transpose(patch_out, (0, 2, 1, 3)), *grads, *(own_side[i, :24] for i in range(4)))


def solution(mesh):
    strips = lambda n: P(None, AXES, *([None] * n))
    rows, row = P(AXES, None), P(AXES)
    body = one_slice if tuple(mesh.shape.values()) == (2, 16) else any_slice
    return jax.shard_map(
        body,
        mesh=mesh,
        in_specs=(strips(2), strips(1), strips(0), rows, rows, rows, rows, row, row, row, row, strips(2)),
        out_specs=(strips(2), strips(2), rows, rows, rows, rows, row, row, row, row),
        check_vma=False,
    )
```

```python
import jax
import jax.numpy as jnp
from jax import lax
from jax.experimental import pallas as pl
from jax.experimental.pallas import tpu as pltpu
from jax.sharding import PartitionSpec as P

HEADS = 12
AXES = ("dp", "fsdp")
MASKED = -1000000000.0
EPSILON = 1e-06
F32 = jnp.float32
BF16 = jnp.bfloat16


def norm_forward(features, scaling, offset):
    center = features - jnp.mean(features, axis=-1, keepdims=True)
    inverse = lax.rsqrt(jnp.mean(center * center, axis=-1, keepdims=True) + EPSILON)
    normed = center * inverse
    return (normed * scaling.astype(F32) + offset.astype(F32), normed, inverse)


def norm_backward(upstream, normed, inverse, scaling):
    through = upstream * scaling.astype(F32)
    inward = inverse * (
        through
        - jnp.mean(through, axis=-1, keepdims=True)
        - normed * jnp.mean(through * normed, axis=-1, keepdims=True)
    )
    return (inward, jnp.sum(upstream * normed, axis=0), jnp.sum(upstream, axis=0))


def sums(equation, left, right):
    return jnp.einsum(equation, left, right, preferred_element_type=F32)


def layer(weights, patches, indices, counts, cotangent):
    qkv_full, out_full, up_full, down_full, first_gain, first_shift, second_gain, second_shift = weights
    strips, visible, patch_count = (indices.shape[0], indices.shape[1], patches.shape[1])
    width = out_full.shape[1]
    rows = strips * visible
    heads = (strips, visible, HEADS, width // HEADS)
    scale = (width // HEADS) ** (-0.5)
    present = jnp.arange(visible)[None, :] < counts[:, None]
    onehot = ((indices[:, :, None] == jnp.arange(patch_count)[None, None, :]) & present[:, :, None]).astype(BF16)
    inputs = sums("bvp,bpd->bvd", onehot, patches).reshape(rows, width)
    first_norm, first_normed, first_inverse = norm_forward(inputs, first_gain, first_shift)
    first_low = first_norm.astype(BF16)
    projected = jnp.dot(first_low, qkv_full, preferred_element_type=F32).astype(BF16)
    queries = projected[:, :width].reshape(heads)
    keys = projected[:, width : 2 * width].reshape(heads)
    values = projected[:, 2 * width :].reshape(heads)
    scores = sums("bqhe,bkhe->bhqk", queries, keys) * scale
    scores = jnp.where(present[:, None, None, :], scores, MASKED)
    attention = jax.nn.softmax(scores, axis=-1)
    attention_low = attention.astype(BF16)
    mixed = sums("bhqk,bkhe->bqhe", attention_low, values).astype(BF16).reshape(rows, width)
    middle = inputs + jnp.dot(mixed, out_full, preferred_element_type=F32)
    second_norm, second_normed, second_inverse = norm_forward(middle, second_gain, second_shift)
    second_low = second_norm.astype(BF16)
    hidden_pre = jnp.dot(second_low, up_full, preferred_element_type=F32)
    hidden, gelu_pull = jax.vjp(lambda v: jax.nn.gelu(v, approximate=False), hidden_pre)
    hidden_low = hidden.astype(BF16)
    branch = jnp.dot(hidden_low, down_full, preferred_element_type=F32)
    live = present.reshape(rows, 1)
    output = ((middle + branch) * live.astype(F32)).reshape(strips, visible, width)

    upstream = cotangent.reshape(rows, width) * live.astype(BF16)
    down_grad = sums("rf,rd->fd", hidden_low, upstream)
    pre_low = gelu_pull(sums("rd,fd->rf", upstream, down_full))[0].astype(BF16)
    up_grad = sums("rf,rd->fd", second_low, pre_low)
    second_back = sums("rd,fd->rf", pre_low, up_full)
    inward, second_gain_grad, second_shift_grad = norm_backward(second_back, second_normed, second_inverse, second_gain)
    middle_grad = upstream.astype(F32) + inward
    middle_low = middle_grad.astype(BF16)
    out_grad = sums("rf,rd->fd", mixed, middle_low)
    mixed_grad = sums("rd,fd->rf", middle_low, out_full).astype(BF16).reshape(heads)
    prob_grad = sums("bqhe,bkhe->bhqk", mixed_grad, values)
    value_grad = sums("bhqk,bqhe->bkhe", attention_low, mixed_grad)
    score_low = (attention * (prob_grad - jnp.sum(attention * prob_grad, axis=-1, keepdims=True))).astype(BF16)
    query_grad = sums("bhqk,bkhe->bqhe", score_low, keys) * scale
    key_grad = sums("bhqk,bqhe->bkhe", score_low, queries) * scale
    projected_grad = jnp.concatenate([g.reshape(rows, width) for g in (query_grad, key_grad, value_grad)], axis=1).astype(BF16)
    qkv_grad = sums("rf,rd->fd", first_low, projected_grad)
    first_back = sums("rd,fd->rf", projected_grad, qkv_full)
    inward, first_gain_grad, first_shift_grad = norm_backward(first_back, first_normed, first_inverse, first_gain)
    input_low = (middle_grad + inward).astype(BF16).reshape(strips, visible, width)
    patch_part = sums("bvp,bvd->bpd", onehot, input_low)
    gradients = (qkv_grad, out_grad, up_grad, down_grad, first_gain_grad, first_shift_grad, second_gain_grad, second_shift_grad)
    return (output, gradients, patch_part)


def any_slice(patches, visible_index, visible_count, *rest):
    weights, cotangent = rest[:-1], rest[-1]
    whole = [lax.all_gather(w, AXES, axis=0, tiled=True) for w in weights]
    micro, strips = patches.shape[:2]
    flat = lambda a: a.reshape((micro * strips,) + a.shape[2:])
    output, gradients, patch_part = layer(whole, flat(patches), flat(visible_index), flat(visible_count), flat(cotangent))
    shares = [lax.psum_scatter(g, AXES, scatter_dimension=0, tiled=True) for g in gradients]
    back = lambda a: a.reshape((micro, strips) + a.shape[1:])
    return (back(output), back(patch_part), *shares)


MESH = pl.DeviceIdType.MESH
EXT = 128
ALL = slice(None)


def coords():
    y = lax.axis_index("dp")
    f = lax.axis_index("fsdp")
    return y, f // 4, (f // 2) % 2, f % 2


def device(y, z, x, c):
    return (y, z * 4 + x * 2 + c)


def other(z, dz):
    if dz == 0:
        return z
    if dz == 1:
        return z + 1 - 2 * (z % 2)
    if dz == 2:
        return (z + 2) % 4
    return 3 - z


def at_z(z):
    return (z // 2, z % 2)


class Round:
    def __init__(self, i, ref, lead, start, width, first):
        self.i, self.ref, self.lead, self.start, self.width = i, ref, lead, start, width
        self.halves = (pl.ds(start, first), pl.ds(start + first, width - first))
        self.cols = pl.ds(start, width)
        self.local = pl.ds(0, first), pl.ds(0, width - first)

    def at(self, par):
        def block(y, z, x, cols=None):
            before, after = self.lead(par)
            return self.ref.at[before + (y,) + z + (x,) + after + (ALL, self.cols if cols is None else cols)]

        return block


def piece(n):
    return lambda par: ((n + par,), ())


def part(n, step=1):
    return lambda par: ((), (n + step * par,))


def gather_rounds(w0, w1, wd):
    return [
        Round(0, w0, piece(0), 0, 384 + EXT, 256),
        Round(1, w1, piece(0), 0, 384, 256),
        Round(2, w0, piece(0), 384 + EXT, 384, 128),
        Round(3, w1, piece(0), 384, 384, 128),
        Round(4, w1, piece(2), 0, 768, 384),
        Round(5, w1, piece(4), 0, 768, 384),
        Round(6, wd, part(0, 2), 0, 768, 384),
        Round(7, wd, part(1, 2), 0, 384, 256),
        Round(8, wd, part(1, 2), 384, 384, 128),
    ]


def scatter_rounds(w1, gd):
    return [
        Round(0, gd, part(0, 2), 0, 768, 384),
        Round(1, gd, part(1, 2), 0, 768, 384),
        Round(2, w1, piece(2), 0, 768, 384),
        Round(3, w1, piece(4), 0, 768, 384),
        Round(4, gd, part(2), 0, 384, 256),
        Round(5, gd, part(0), 0, 384, 128),
        Round(6, gd, part(2), 384, 384, 256),
        Round(7, gd, part(0), 384, 384, 128),
    ]


class Peers:
    def __init__(self, place, rounds, sems):
        y, z, x, c = self.place = place
        self.rounds, self.sems = rounds, sems
        self.all_z, self.pair, self.odd = (ALL, ALL), (ALL, z % 2), (ALL, 1 - z % 2)
        self.x_side, self.y_side = device(y, z, 1 - x, c), device(1 - y, z, x, c)
        self.sibling = device(y, z, x, 1 - c)

    def z_peer(self, dz):
        y, z, x, c = self.place
        return device(y, other(z, dz), x, c)

    def copy(self, send, recv, j, src, dst, to):
        sent, got = self.sems
        return pltpu.make_async_remote_copy(
            src_ref=src, dst_ref=dst, send_sem=sent.at[j, send], recv_sem=got.at[j, recv], device_id=to, device_id_type=MESH
        )


class Gather(Peers):
    def same(self, send, recv, j, ref, to):
        return self.copy(send, recv, j, ref, ref, to)

    def at(self, j, par=None):
        return self.rounds[j].at(self.place[3] if par is None else par)

    def z(self, j, dz, there=0):
        y, z, x, c = self.place
        return self.same(dz - 1, dz - 1, j, self.at(j)(y, at_z(other(z, there)), x), self.z_peer(dz))

    def side(self, j, dz, axis):
        y, z, x, c = self.place
        ref = self.at(j)(y, at_z(other(z, dz)), x)
        if axis == "x":
            return self.same(3, 3 + dz % 2, j, ref, self.x_side)
        return self.same(3, 5 + dz % 2, j, ref, self.y_side)

    def sides_in(self, j, odd, axis):
        y, z, x, c = self.place
        zz = self.odd if odd else self.pair
        if axis == "x":
            return self.same(3, 3 + odd, j, self.at(j)(y, zz, 1 - x), self.x_side)
        return self.same(3, 5 + odd, j, self.at(j)(1 - y, zz, x), self.y_side)

    def diag(self, j, half, there=False):
        y, z, x, c = self.place
        cols = self.rounds[j].halves[half]
        yy = 1 - y if there or half == 1 else y
        xx = 1 - x if there or half == 0 else x
        return self.same(4, 7 + half, j, self.at(j)(yy, self.pair, xx, cols), self.y_side if half == 0 else self.x_side)

    def turn(self, j, there=False):
        y, z, x, c = self.place
        return self.same(4, 9, j, self.at(j)(1 - y, self.odd if there else self.pair, 1 - x), self.z_peer(1))

    def down(self, j, q):
        y, z, x, c = self.place
        yy = y if q < 2 else 1 - y
        xx = x if q in (0, 2) else 1 - x
        zz = self.all_z if q < 3 else self.pair if q == 3 else self.odd
        return self.same(5, 10, j, self.at(j)(yy, zz, xx), self.sibling)

    def downs(self, j, par):
        return self.same(5, 10, j, self.at(j, par)(ALL, self.all_z, ALL), self.sibling)

    def begin(self, j):
        for dz in (1, 2, 3):
            self.z(j, dz).start()

    def own(self, j):
        self.side(j, 0, "x").start()
        self.side(j, 0, "y").start()

    def forward(self, j):
        for dz in (1, 2, 3):
            self.z(j, dz, dz).wait_recv()
            self.side(j, dz, "x").start()
            self.side(j, dz, "y").start()
        self.down(j, 0).start()

    def cross(self, j):
        for half, axis in enumerate(("x", "y")):
            self.sides_in(j, 0, axis).wait_recv()
            self.diag(j, half).start()
        for half, axis in enumerate(("x", "y")):
            self.sides_in(j, 1, axis).wait_recv()
            self.down(j, 1 + half).start()

    def finish(self, j):
        self.diag(j, 0, True).wait_recv()
        self.diag(j, 1, True).wait_recv()
        self.turn(j).start()
        self.down(j, 3).start()

    def last(self, j):
        self.turn(j, True).wait_recv()
        self.down(j, 4).start()

    def arrive(self, j):
        self.downs(j, 1 - self.place[3]).wait_recv()

    def sent(self, j):
        y, z, x, c = self.place
        for dz in (1, 2, 3):
            self.z(j, dz).wait_send()
        self.same(3, 3, j, self.at(j)(y, self.all_z, ALL), self.x_side).wait_send()
        self.same(4, 7, j, self.at(j)(y, self.all_z, x), self.y_side).wait_send()
        self.downs(j, c).wait_send()


def add_to(own, got):
    own[...] = (own[...].astype(F32) + got[...].astype(F32)).astype(BF16)


class Scatter(Peers):
    def __init__(self, place, rounds, bufs, sems, free):
        super().__init__(place, rounds, sems)
        self.bufs, self.free = bufs, free

    def at(self, j, par=None):
        return self.rounds[j].at(self.place[3] if par is None else par)

    def a(self, j):
        return self.copy(0, 0, j, self.at(j, 1 - self.place[3])(ALL, self.all_z, ALL), self.bufs["a"](j), self.sibling)

    def turn(self, j):
        y, z, x, c = self.place
        return self.copy(1, 1, j, self.at(j)(1 - y, self.odd, 1 - x), self.bufs["t"](j), self.z_peer(1))

    def diag(self, j, half):
        y, z, x, c = self.place
        cols = self.rounds[j].halves[half]
        src = self.at(j)(1 - y, self.pair, 1 - x, cols)
        return self.copy(1, 2 + half, j, src, self.bufs["g"](j, half), self.y_side if half == 0 else self.x_side)

    def side(self, j, k, axis):
        y, z, x, c = self.place
        zz = self.pair if k else self.odd
        if axis == "x":
            return self.copy(2, 4 + k, j, self.at(j)(y, zz, 1 - x), self.bufs["x"](j, k), self.x_side)
        return self.copy(2, 6 + k, j, self.at(j)(1 - y, zz, x), self.bufs["y"](j, k), self.y_side)

    def d(self, j, dz):
        y, z, x, c = self.place
        return self.copy(3, 8, j, self.at(j)(y, at_z(other(z, dz)), x), self.bufs["d"](j).at[dz - 1], self.z_peer(dz))

    def ds(self, j):
        return self.copy(3, 8, j, self.bufs["d"](j), self.bufs["d"](j), self.z_peer(1))

    def e(self, j):
        return self.copy(4, 9, j, self.bufs["f"](j).at[1 - self.place[3]], self.bufs["e"](j), self.sibling)

    def begin(self, j):
        if j >= 2:
            pl.semaphore_wait(self.free.at[j % 2], 1)
        self.a(j).start()

    def add_a(self, j):
        self.a(j).wait_recv()
        at, got = self.at(j), self.bufs["a"](j)

        @pl.loop(0, 16)
        def _(i):
            y, z, x = i // 8, at_z((i // 2) % 4), i % 2
            add_to(at(y, z, x), got.at[(y,) + z + (x,)])

        self.turn(j).start()
        self.side(j, 0, "x").start()
        self.side(j, 0, "y").start()
        if j < len(self.rounds) - 2:
            pl.semaphore_signal(self.free.at[j % 2], inc=1, device_id=self.sibling, device_id_type=MESH)

    def add_t(self, j):
        y, z, x, c = self.place
        self.turn(j).wait_recv()
        for h in range(2):
            add_to(self.at(j)(1 - y, (h, z % 2), 1 - x), self.bufs["t"](j).at[h])
        self.diag(j, 0).start()
        self.diag(j, 1).start()

    def add_g(self, j):
        y, z, x, c = self.place
        first, second = self.rounds[j].halves
        self.diag(j, 0).wait_recv()
        for h in range(2):
            add_to(self.at(j)(y, (h, z % 2), 1 - x, first), self.bufs["g"](j, 0).at[h])
        self.side(j, 1, "x").start()
        self.diag(j, 1).wait_recv()
        for h in range(2):
            add_to(self.at(j)(1 - y, (h, z % 2), x, second), self.bufs["g"](j, 1).at[h])
        self.side(j, 1, "y").start()

    def add_s(self, j):
        y, z, x, c = self.place
        for k in range(2):
            self.side(j, k, "x").wait_recv()
            self.side(j, k, "y").wait_recv()
            low = z % 2 if k else 1 - z % 2

            @pl.loop(0, 2)
            def _(h):
                own = self.at(j)(y, (h, low), x)
                both = self.bufs["x"](j, k)[h].astype(F32) + self.bufs["y"](j, k)[h].astype(F32)
                own[...] = (own[...].astype(F32) + both).astype(BF16)

        for dz in (1, 2, 3):
            self.d(j, dz).start()

    def add_d(self, j):
        y, z, x, c = self.place
        self.ds(j).wait_recv()
        total = self.at(j)(y, at_z(z), x)[...].astype(F32)
        for dz in (1, 2, 3):
            total = total + self.bufs["d"](j)[dz - 1].astype(F32)
        out = self.bufs["f"](j)
        if j < 2:
            out[...] = total
        else:
            out[0] = total[:24]
            out[1] = total[24:]
            self.e(j).start()

    def sent(self, j):
        y, z, x, c = self.place
        at = self.at(j)
        self.a(j).wait_send()
        self.copy(1, 1, j, at(y, self.all_z, x), at(y, self.all_z, x), self.z_peer(1)).wait_send()
        self.copy(2, 4, j, at(y, self.all_z, ALL), at(y, self.all_z, ALL), self.x_side).wait_send()
        self.ds(j).wait_send()
        if j > 1:
            self.e(j).wait_send()


class Total(Peers):
    def __init__(self, place, side, send, recv):
        super().__init__(place, None, (send, recv))
        self.side = side

    def step(self, i):
        y, z, x, c = self.place
        if i == 0:
            peers = (self.sibling,)
        elif i == 1:
            peers = tuple(self.z_peer(dz) for dz in (1, 2, 3))
        else:
            peers = (self.x_side, self.y_side, device(1 - y, z, 1 - x, c))
        first = (3, 4, 7)[i]
        return [self.copy(0, 0, i, self.side.at[i], self.side.at[first + n], peer) for n, peer in enumerate(peers)]

    def whole(self, i):
        got = self.side.at[pl.ds((3, 4, 7)[i], 3 if i else 1)]
        return self.copy(0, 0, i, got, got, self.sibling)

    def begin(self):
        self.step(0)[0].start()

    def add(self, i):
        self.whole(i).wait_recv()
        total = self.side[i]
        for n in ((3,), (4, 5, 6), (7, 8, 9))[i]:
            total = total + self.side[n]
        if i < 2:
            self.side[i + 1] = total
            for copy in self.step(i + 1):
                copy.start()
        return total

    def sent(self):
        for i in range(3):
            self.whole(i).wait_send()


def sem_shapes(rounds, sends, receives):
    return [pltpu.SemaphoreType.DMA((rounds, n)) for n in (sends, receives)]


def mm(a, b):
    return lax.dot_general(a, b, (((1,), (0,)), ((), ())), preferred_element_type=F32)


def mt(a, b):
    return lax.dot_general(a, b, (((1,), (1,)), ((), ())), preferred_element_type=F32)


def tm(a, b):
    return lax.dot_general(a, b, (((0,), (0,)), ((), ())), preferred_element_type=F32)


def lanes(i, n):
    return pl.ds(pl.multiple_of(i * n, 128), n)


def rows_at(i, n):
    return pl.ds(pl.multiple_of(i * n, 16), n)


def normal(v):
    center = v - jnp.mean(v, axis=-1, keepdims=True)
    inverse = lax.rsqrt(jnp.mean(center * center, axis=-1, keepdims=True) + EPSILON)
    return center * inverse, inverse


def gelu_parts(v):
    cdf = 0.5 * lax.erf(v * (0.5**0.5)) + 0.5
    return v * cdf, cdf + v * jnp.exp2(v * v * (-0.5 * 1.4426950408889634) - 1.3257480647361593)


class Layer:
    def __init__(self, r):
        self.__dict__.update(r)

    def weight(self, p, start=0, width=768):
        if p < 2:
            return self.w0[p, :, :, :, :, :, pl.ds(EXT + start, width)].reshape(768, width)
        return self.w1[p - 2, :, :, :, :, :, pl.ds(start, width)].reshape(768, width)

    def live(self, s, shape, axis):
        return lax.broadcasted_iota(jnp.int32, shape, axis) < self.count[s]

    def take(self):
        @pl.loop(0, 2)
        def _(s):
            row = lax.broadcasted_iota(jnp.int32, (1058, 400), 0)
            hot = (row == 2 * self.index[s] + s) & self.live(s, (1058, 400), 1)
            got = tm(hot.astype(F32).astype(BF16), self.pool[...].reshape(1058, 768))
            self.inputs[rows_at(s, 400), :] = got.astype(BF16)
            self.ups[s] = jnp.where(self.live(s, (400, 768), 0), self.ups[s], jnp.zeros((), BF16))

    def gains(self):
        side = self.w0[0, :, :, :, :, :, pl.ds(0, EXT)].reshape(768, EXT).astype(F32)
        self.gain[...] = side.T[0:8]

    def first(self):
        @pl.loop(0, 2)
        def _(s):
            normed, _ = normal(self.inputs[rows_at(s, 400), :].astype(F32))
            self.first_low[rows_at(s, 400), :] = (normed * self.gain[0:1] + self.gain[1:2]).astype(BF16)

    def project(self, half, pieces):
        start = 384 * half
        w = jnp.concatenate([self.weight(p, start, 384) for p in pieces], axis=1)

        got = mm(self.first_low[...], w).astype(BF16)
        for i, p in enumerate(pieces):
            self.proj[:, pl.ds(768 * p + start, 384)] = got[:, 384 * i : 384 * (i + 1)]

    def last_keys(self, s, shape, axis):
        return lax.broadcasted_iota(jnp.int32, shape, axis) + 384 < self.count[s]

    def attend(self, i):
        s, t = i % 2, i // 2
        rows = rows_at(s, 400)
        q, k, v = (self.proj[rows, lanes(6 * p + t, 128)] for p in range(3))
        lane = lax.broadcasted_iota(jnp.int32, (400, 128), 1)
        alive = self.last_keys(s, (400, 16), 1)
        halves = (lane < 64, lane >= 64)
        eighth = q * jnp.asarray(0.125, BF16)
        scores = [mt(jnp.where(mine, eighth, jnp.zeros((), BF16)), k) for mine in halves]
        scores = jnp.concatenate([jnp.concatenate([x[:, :384], jnp.where(alive, x[:, 384:], MASKED)], axis=1) for x in scores], axis=0)
        top = jnp.max(scores, axis=1, keepdims=True)
        e = jnp.exp(scores - top)
        total = jnp.sum(e, axis=1, keepdims=True)
        e = e.astype(BF16)
        mixed = jnp.concatenate([mm(e[400 * h : 400 * (h + 1)], v) for h in range(2)], axis=0) * (1.0 / total)
        self.mixed[rows, lanes(t, 128)] = jnp.where(halves[0], mixed[:400], mixed[400:]).astype(BF16)
        logs = top + jnp.log(total)
        stat = self.stat[s, pl.ds(0, 400), :]
        for h in range(2):
            stat = jnp.where(lane == 2 * t + h, logs[400 * h : 400 * (h + 1)], stat)
        self.stat[s, pl.ds(0, 400), :] = stat

    def turn_stat(self):
        for s in range(2):
            self.turned[s] = self.stat[s].T[0:16]

    def mix(self):
        w = self.weight(3)
        @pl.loop(0, 2)
        def _(s):
            rows = rows_at(s, 400)
            middle = self.inputs[rows, :].astype(F32) + mm(self.mixed[rows, :], w)
            self.mid[s, pl.ds(0, 400), :] = middle
            normed, _ = normal(middle)
            self.second_low[rows, :] = (normed * self.gain[2:3] + self.gain[3:4]).astype(BF16)

    def hide(self, p):
        w = self.weight(4 + p)
        cols = pl.ds(768 * p, 768)
        for s in range(2):
            rows = pl.ds(400 * s, 400)
            act, slope = gelu_parts(mm(self.second_low[rows, :], w))
            self.hidden[rows, cols] = act.astype(BF16)
            self.slope[rows, cols] = slope.astype(BF16)

    def down_terms(self, chunks):
        left = jnp.concatenate([self.hidden[:, pl.ds(384 * i, 384)] for i in chunks], axis=1)
        g = tm(left, self.ups[...].reshape(800, 768)).astype(BF16)
        for n, i in enumerate(chunks):
            self.gd[i // 4, (i % 4) // 2, i % 2] = g[384 * n : 384 * (n + 1)].reshape(2, 4, 48, 768)

    def branch(self, n, stage):
        w = self.wd[:, :, :, :, :, :, lanes(n, 256)].reshape(3072, 256)
        for s in range(2):
            got = mm(self.hidden[pl.ds(400 * s, 400), :], w)
            got = (got + self.mid[s, pl.ds(0, 400), lanes(n, 256)]) * self.live(s, (400, 256), 0).astype(F32)
            stage[s] = got

    def hide_back(self, p):
        w = self.wd[p // 2, p % 2].reshape(768, 768)
        cols = pl.ds(768 * p, 768)
        for s in range(2):
            rows = pl.ds(400 * s, 400)
            self.slope[rows, cols] = (mt(self.ups[s], w) * self.slope[rows, cols].astype(F32)).astype(BF16)

    def up_terms(self, p):
        g = tm(self.second_low[...], self.slope[:, pl.ds(768 * p, 768)])
        self.g1[2 + p] = g.astype(BF16).reshape(2, 2, 2, 2, 48, 768)

    def second_back(self):
        self.vec[0] = jnp.zeros((8, 768), F32)

        @pl.loop(0, 2)
        def _(s):
            w = jnp.concatenate([self.weight(4 + p) for p in range(4)], axis=1)
            back = mt(self.slope[rows_at(s, 400), :], w)
            normed, inverse = normal(self.mid[s, pl.ds(0, 400), :])
            inward, dg, db = self.norm_back(back, normed, inverse, self.gain[2:3])
            self.ups[s] = (self.ups[s].astype(F32) + inward).astype(BF16)
            self.vec[0, 2:3] += dg
            self.vec[0, 3:4] += db

    def norm_back(self, back, normed, inverse, gain):
        through = back * gain
        inward = inverse * (
            through
            - jnp.mean(through, axis=-1, keepdims=True)
            - normed * jnp.mean(through * normed, axis=-1, keepdims=True)
        )
        return inward, jnp.sum(back * normed, axis=0, keepdims=True), jnp.sum(back, axis=0, keepdims=True)

    def mix_back(self):
        w = self.weight(3)
        self.second_low[...] = mt(self.ups[...].reshape(800, 768), w).astype(BF16)

    def out_terms(self):
        g = tm(self.mixed[...], self.ups[...].reshape(800, 768))
        self.gd[:, :, :, :, 3] = g.astype(BF16).reshape(2, 2, 2, 2, 48, 768)

    def attend_back(self, i):
        s, t = i % 2, i // 2
        rows = rows_at(s, 400)
        q, k, v = (self.proj[rows, lanes(6 * p + t, 128)] for p in range(3))
        do = self.second_low[rows, lanes(t, 128)]
        first_half = lax.broadcasted_iota(jnp.int32, (400, 128), 1) < 64
        alive = self.last_keys(s, (16, 400), 0)
        zero = jnp.zeros((), BF16)
        halves = (first_half, ~first_half)
        eighth = k * jnp.asarray(0.125, BF16)
        scores = [mt(jnp.where(mine, eighth, zero), q) for mine in halves]
        shares = []
        for h in range(2):
            p = jnp.exp(scores[h] - self.turned[s, pl.ds(2 * t + h, 1), pl.ds(0, 400)])
            shares.append(jnp.concatenate([p[:384], jnp.where(alive, p[384:], 0.0)], axis=0))
        dv = mm(jnp.concatenate([p.astype(BF16) for p in shares], axis=0), do)
        back = [mt(jnp.where(mine, v, zero), do) for mine in halves]
        ds = [(p * (dp - jnp.sum(p * dp, axis=0, keepdims=True))).astype(BF16) for p, dp in zip(shares, back)]
        dk = mm(jnp.concatenate(ds, axis=0), q)
        dq = [tm(x, k) for x in ds]
        for i, (first, second, scale) in enumerate(((dq[0], dq[1], 0.125), (dk[:400], dk[400:], 0.125), (dv[:400], dv[400:], 1.0))):
            g = jnp.where(first_half, first, second) * scale
            self.proj[rows, lanes(6 * i + t, 128)] = g.astype(BF16)

    def project_terms(self, half):
        start = 384 * half

        right = jnp.concatenate([self.proj[:, pl.ds(768 * p + start, 384)] for p in range(3)], axis=1)
        g = tm(self.first_low[...], right).astype(BF16)
        for p in range(3):
            self.gd[:, :, :, :, p, :, pl.ds(start, 384)] = g[:, 384 * p : 384 * (p + 1)].reshape(2, 2, 2, 2, 48, 384)

    def first_back(self, s):
        rows = pl.ds(400 * s, 400)
        back = mt(self.proj[rows, :], jnp.concatenate([self.weight(p) for p in range(3)], axis=1))
        normed, inverse = normal(self.inputs[rows, :].astype(F32))
        inward, dg, db = self.norm_back(back, normed, inverse, self.gain[0:1])
        self.ups[s] = (self.ups[s].astype(F32) + inward).astype(BF16)
        self.vec[0, 0:1] += dg
        self.vec[0, 1:2] += db


W_SHAPES = ((2, 2, 2, 2, 2, 48, 768 + EXT), (6, 2, 2, 2, 2, 48, 768), (2, 2, 2, 2, 4, 48, 768))


def greet(place):
    y, z, x, c = place
    barrier = pltpu.get_barrier_semaphore()
    peers = [device(y, z, x, 1 - c), device(y, z, 1 - x, c), device(1 - y, z, x, c)]
    peers += [device(y, other(z, dz), x, c) for dz in (1, 2, 3)] + [device(1 - y, z, 1 - x, c)]
    for peer in peers:
        pl.semaphore_signal(barrier, inc=1, device_id=peer, device_id_type=MESH)
    return lambda: pl.semaphore_wait(barrier, len(peers))


class Shards:
    def __init__(self, place, own, weights, sent, got, sems):
        self.place, self.own, self.weights = place, own, weights
        self.sent, self.got, self.sems = sent, got, sems

    def width(self, j):
        return 768 + EXT if j == 0 else 768

    def piece(self, p):
        qkv, out, up, _, ext = self.own
        if p == 3:
            return out[...].astype(F32)
        if p > 3:
            return up[:, 768 * (p - 4) : 768 * (p - 3)].astype(F32)
        v = qkv[:, 768 * p : 768 * (p + 1)].astype(F32)
        return jnp.concatenate([ext[0:24], v], axis=1) if p < 2 else v

    def copy(self, j):
        y, z, x, c = self.place
        cols = pl.ds(0, self.width(j))
        return pltpu.make_async_remote_copy(
            src_ref=self.sent.at[j, :, cols],
            dst_ref=self.got.at[j, :, cols],
            send_sem=self.sems.at[0, j],
            recv_sem=self.sems.at[1, j],
            device_id=device(y, z, x, 1 - c),
            device_id_type=MESH,
        )

    def stage(self, j):
        c = self.place[3]
        self.sent[j, :, pl.ds(0, self.width(j))] = jnp.where(c == 0, self.piece(2 * j + 1), self.piece(2 * j))

    def build(self, j):
        y, z, x, c = self.place
        mine = jnp.where(c == 0, self.piece(2 * j), self.piece(2 * j + 1))
        self.copy(j).wait_recv()
        got = self.got[j, :, pl.ds(0, self.width(j))]
        both = jnp.where(c == 0, jnp.concatenate([mine, got], axis=0), jnp.concatenate([got, mine], axis=0))
        if j == 0:
            self.weights[0][c, y, z // 2, z % 2, x] = both.astype(BF16)
        else:
            self.weights[1][2 * (j - 1) + c, y, z // 2, z % 2, x] = both.astype(BF16)

    def close(self):
        for j in range(4):
            self.copy(j).wait_send()

    def build_down(self):
        y, z, x, c = self.place
        for k in (0, 1):
            self.weights[2][y, z // 2, z % 2, x, 2 * c + k] = self.own[3][48 * k : 48 * (k + 1), :]


class Refs:
    pass


def bf16(*shape):
    return pltpu.VMEM(shape, BF16)


def f32(*shape):
    return pltpu.VMEM(shape, F32)


INS = ["count", "index", "patches", "cot", "qkv", "out", "up", "down", "gain_1", "shift_1", "gain_2", "shift_2"]
OUTS = ["layer_out", "low_out", "o_qkv", "o_out", "o_up", "o_down", "o_side"]
SCRATCH = dict(
    w0=bf16(*W_SHAPES[0]), w1=bf16(*W_SHAPES[1]), wd=bf16(*W_SHAPES[2]), gd=bf16(*W_SHAPES[2]),
    inputs=bf16(800, 768), first_low=bf16(800, 768), proj=bf16(800, 2304), mixed=bf16(800, 768),
    mid=f32(2, 400, 768), second_low=bf16(800, 768), hidden=bf16(800, 3072), slope=bf16(800, 3072),
    ups=bf16(2, 400, 768), gain=f32(8, 768), pool=bf16(529, 2, 768), stage=f32(2, 400, 256),
    stat=f32(2, 512, 128), turn=f32(EXT, EXT), turned=f32(2, 16, 512), vec=f32(10, 8, 768),
    s0=f32(4, 24, 768 + EXT), r0=f32(4, 24, 768 + EXT), ra=bf16(2, 2, 2, 2, 2, 48, 768),
    rt=bf16(4, 2, 48, 768), rx=bf16(4, 2, 2, 48, 768), ry=bf16(4, 2, 2, 48, 768), rg=bf16(4, 2, 2, 48, 384), rd=bf16(4, 3, 48, 768),
    ht=bf16(4, 2, 48, 384), hx=bf16(4, 2, 2, 48, 384), hy=bf16(4, 2, 2, 48, 384), hg=bf16(4, 2, 2, 48, 256), hd=bf16(4, 3, 48, 384),
    fd=f32(2, 48, 768), fs=f32(6, 2, 24, 768), re=f32(6, 24, 768),
    free=pltpu.SemaphoreType.REGULAR((2,)), pair=pltpu.SemaphoreType.DMA((2, 4)), local=pltpu.SemaphoreType.DMA((4,)), vs=pltpu.SemaphoreType.DMA((3, 1)), vr=pltpu.SemaphoreType.DMA((3, 1)),
)


def make_scatter(place, R, sems):
    rounds = scatter_rounds(R.w1, R.gd)

    def pick(full, half):
        return lambda j, *at: full.at[(j,) + at] if j < 4 else half.at[(j - 4,) + at]

    def corner(j, half):
        cols = rounds[j].local[half]
        return R.rg.at[j, half] if j < 4 else R.hg.at[j - 4, half, :, :, cols]

    bufs = dict(
        a=lambda j: R.ra.at[j % 2, :, :, :, :, :, pl.ds(0, rounds[j].width)],
        t=pick(R.rt, R.ht),
        x=pick(R.rx, R.hx),
        y=pick(R.ry, R.hy),
        g=corner,
        d=pick(R.rd, R.hd),
        f=lambda j: R.fd.at[j] if j < 2 else R.fs.at[j - 2, :, :, pl.ds(0, rounds[j].width)],
        e=lambda j: R.re.at[j - 2, :, pl.ds(0, rounds[j].width)],
    )
    return Scatter(place, rounds, bufs, sems, R.free)


def mega(*refs):
    names = INS + OUTS + list(SCRATCH)
    r = dict(zip(names, refs))
    n = len(names)
    m = n + 2
    R = Refs()
    R.__dict__.update(r)
    R.g1 = R.w1
    place = coords()
    c = place[3]
    weights = (R.w0, R.w1, R.wd)
    cot_copy = pltpu.make_async_copy(R.cot, R.ups, R.local.at[0])
    cot_copy.start()
    patch_in = pltpu.make_async_copy(R.patches, R.pool, R.local.at[3])
    patch_in.start()
    met = greet(place)
    shards = Shards(place, (R.qkv, R.out, R.up, R.down, R.turn), weights, R.s0, R.r0, R.pair)
    g = Gather(place, gather_rounds(*weights), refs[n:m])
    v = Total(place, R.vec, R.vs, R.vr)

    s = make_scatter(place, R, refs[m:])
    L = Layer(R.__dict__)
    low_copy = pltpu.make_async_copy(R.ups, R.low_out, R.local.at[0])

    out_copies = [
        pltpu.make_async_copy(R.stage, R.layer_out.at[:, :, pl.ds(256 * i, 256)], R.local.at[2]) for i in range(3)
    ]

    def branch(k):
        if k:
            out_copies[k - 1].wait()
        L.branch(k, R.stage)
        out_copies[k].start()

    def start(j):
        g.begin(j)
        g.own(j)

    R.turn[...] = jnp.zeros((EXT, EXT), F32)
    for i, row in enumerate((R.gain_1, R.shift_1, R.gain_2, R.shift_2)):
        R.turn[i : i + 1, 0:24] = row[...].astype(F32)
    R.turn[...] = R.turn[...].T
    for j in range(4):
        shards.stage(j)
    shards.build_down()
    met()
    for j in range(4):
        shards.copy(j).start()
    shards.build(0)
    start(0)
    shards.build(1)
    start(1)
    shards.build(2)
    shards.build(3)
    cot_copy.wait()
    patch_in.wait()
    L.take()

    def over(step, first, last):
        pl.loop(first, last)(step)

    qk, v_only = (0, 1), (2,)

    def close():
        for j in range(9):
            g.sent(j)
        shards.close()

    plan = [
        (g.forward, 0), (g.forward, 1), (g.cross, 0), (start, 2), (g.finish, 0), (g.cross, 1), (start, 3), (g.last, 0),
        (g.forward, 2), (g.finish, 1), (start, 4), (g.arrive, 0), (L.gains,), (L.first,), (L.project, 0, qk),
        (g.forward, 3), (g.cross, 2), (g.last, 1), (start, 5), (g.arrive, 1), (L.project, 0, v_only), (over, L.attend, 0, 2),
        (g.finish, 2), (g.cross, 3), (g.forward, 4), (over, L.attend, 2, 4), (start, 6), (g.last, 2), (g.finish, 3), (over, L.attend, 4, 6),
        (g.arrive, 2), (g.cross, 4), (g.forward, 5), (L.project, 1, qk), (g.last, 3), (g.finish, 4), (start, 7), (start, 8), (g.arrive, 3),
        (L.project, 1, v_only), (over, L.attend, 6, 10), (g.cross, 5), (g.forward, 6), (over, L.attend, 10, 12), (L.mix,), (L.turn_stat,),
        (g.last, 4), (g.finish, 5), (g.forward, 7), (g.arrive, 4), (L.hide, 0), (L.hide, 1), (g.cross, 6), (g.last, 5), (g.forward, 8),
        (L.down_terms, (0, 1)), (g.arrive, 5), (g.cross, 7), (L.hide, 2), (g.finish, 6), (L.hide, 3), (g.cross, 8),
        (L.down_terms, (2, 3)), (g.last, 6), (g.finish, 7), (L.down_terms, (4, 5)), (g.finish, 8), (L.down_terms, (6, 7)),
        (s.begin, 0), (g.last, 7), (g.last, 8), (g.arrive, 6), (g.arrive, 7), (g.arrive, 8), (s.begin, 1), (s.add_a, 0),
        (L.hide_back, 0), (L.hide_back, 1), (s.add_a, 1), (L.hide_back, 2), (L.hide_back, 3),
        (s.add_t, 0), (L.second_back,), (s.add_t, 1), (s.add_g, 0), (close,),
        (L.up_terms, 0), (L.up_terms, 1), (s.begin, 2), (L.up_terms, 2), (s.add_g, 1), (L.up_terms, 3), (s.add_s, 0), (s.add_a, 2), (s.begin, 3),
        (L.mix_back,), (over, L.attend_back, 0, 1), (s.add_s, 1), (s.add_a, 3), (over, L.attend_back, 1, 5), (s.add_t, 2),
        (over, L.attend_back, 5, 7), (s.add_g, 2), (s.add_d, 0), (s.add_d, 1), (s.sent, 0), (s.sent, 1),
        (L.project_terms, 0), (s.add_t, 3), (L.out_terms,), (s.begin, 4), (s.begin, 5), (s.add_s, 2), (over, L.attend_back, 7, 8), (s.add_g, 3), (s.add_a, 4),
        (over, L.attend_back, 8, 9), (s.add_a, 5), (over, L.attend_back, 9, 11), (s.add_t, 4), (s.add_s, 3), (over, L.attend_back, 11, 12), (L.project_terms, 1),
        (s.begin, 6), (s.begin, 7), (s.add_t, 5), (s.add_g, 4), (s.add_d, 2), (branch, 0), (s.add_a, 6), (s.add_a, 7), (s.add_g, 5), (L.first_back, 0),
        (s.add_t, 6), (s.add_s, 4), (L.first_back, 1), (v.begin,), (low_copy.start,), (s.add_t, 7), (s.add_g, 6), (s.add_s, 5), (branch, 1),
        (s.add_g, 7), (v.add, 0), (branch, 2), (s.add_s, 6), (s.add_s, 7), (v.add, 1), (s.add_d, 3), (s.add_d, 4), (s.add_d, 5), (s.add_d, 6), (s.add_d, 7),
    ]
    for step, *at in plan:
        step(*at)
    R.o_side[...] = v.add(2)
    targets = {
        2: (R.o_up, 0, R.o_up, 768),
        3: (R.o_up, 1536, R.o_up, 2304),
        4: (R.o_qkv, 1536, R.o_out, 0),
        5: (R.o_qkv, 0, R.o_qkv, 768),
        6: (R.o_qkv, 1920, R.o_out, 384),
        7: (R.o_qkv, 384, R.o_qkv, 1152),
    }
    for j, (even, even_at, odd, odd_at) in targets.items():
        s.e(j).wait_recv()
        own = s.bufs["f"](j)[c]
        got = s.bufs["e"](j)[...]
        even[:, pl.ds(even_at, s.rounds[j].width)] = jnp.where(c == 0, own, got)
        odd[:, pl.ds(odd_at, s.rounds[j].width)] = jnp.where(c == 0, got, own)
    for k in (0, 1):
        R.o_down[48 * k : 48 * (k + 1), :] = R.fd[k]
    for j in range(2, 8):
        s.sent(j)
    v.sent()
    low_copy.wait()
    out_copies[2].wait()


def finish(count, index, low, side, *refs):
    given, patch_out, small, taken, held, (mid, sems) = refs[:5], refs[5], refs[6:10], refs[10:15], refs[15:20], refs[20:]
    to = [pltpu.make_async_copy(a, b, sems.at[2 + i]) for i, (a, b) in enumerate(zip(given, held))]
    back = [pltpu.make_async_copy(a, b, sems.at[7 + i]) for i, (a, b) in enumerate(zip(held, taken))]
    for copy in to:
        copy.start()
    outs = [pltpu.make_async_copy(mid.at[s], patch_out.at[s, :, 0, :], sems.at[s]) for s in range(2)]
    for s in range(2):
        hot = lax.broadcasted_iota(jnp.int32, (529, 400), 0) == index[s]
        hot = hot & (lax.broadcasted_iota(jnp.int32, (529, 400), 1) < count[s])
        mid[s] = mm(hot.astype(F32).astype(BF16), low[s])
        outs[s].start()
    for first, second in zip(to, back):
        first.wait()
        second.start()
    here = (lax.axis_index(AXES[0]) * 16 + lax.axis_index(AXES[1])) * 24
    own = pltpu.roll(side[...], 768 - here, 1)
    for i in range(4):
        small[i][...] = own[i, :24]
    for copy in outs + back:
        copy.wait()


def one_slice(patches, visible_index, visible_count, qkv_weight, out_weight, up_weight, down_weight, attention_gain, attention_shift, feedforward_gain, feedforward_shift, cotangent):
    small = [row.reshape(1, 24) for row in (attention_gain, attention_shift, feedforward_gain, feedforward_shift)]
    whole = pl.BlockSpec(memory_space=pltpu.VMEM)
    anywhere = pl.BlockSpec(memory_space=pl.ANY)
    smem = pl.BlockSpec(memory_space=pltpu.SMEM)
    shapes = ((2, 400, 768), (2, 400, 768), (24, 2304), (24, 768), (24, 3072), (96, 768), (8, 768))
    types = (F32, BF16, F32, F32, F32, F32, F32)
    counts, index = visible_count.reshape(2), visible_index.reshape(2, 1, 400)
    layer_out, low, *grads, side = pl.pallas_call(
        mega,
        out_shape=[jax.ShapeDtypeStruct(*shape) for shape in zip(shapes, types)],
        in_specs=[smem, whole] + [anywhere] * 2 + [whole] * 8,
        out_specs=[anywhere] * 2 + [whole] * 5,
        scratch_shapes=list(SCRATCH.values()) + sem_shapes(9, 6, 11) + sem_shapes(8, 5, 10),
        compiler_params=pltpu.CompilerParams(collective_id=0, has_side_effects=True, vmem_limit_bytes=62 * 2**20),
        name="layer_step",
    )(
        counts,
        index,
        jnp.transpose(patches.reshape(2, 529, 768), (1, 0, 2)),
        cotangent.reshape(2, 400, 768),
        qkv_weight,
        out_weight,
        up_weight,
        down_weight,
        *small,
    )
    results = [jax.ShapeDtypeStruct(shape, F32) for shape in shapes[:1] + shapes[2:6]]
    patch_out, s0, s1, s2, s3, layer_out, *grads = pl.pallas_call(
        finish,
        out_shape=[jax.ShapeDtypeStruct((2, 529, 1, 768), F32), *[jax.ShapeDtypeStruct((24,), F32)] * 4] + results,
        in_specs=[smem] + [whole] * 3 + [anywhere] * 5,
        out_specs=[anywhere] + [whole] * 4 + [anywhere] * 5,
        scratch_shapes=[pltpu.VMEM(a.shape, F32) for a in results] + [f32(2, 529, 768), pltpu.SemaphoreType.DMA((12,))],
        compiler_params=pltpu.CompilerParams(vmem_limit_bytes=62 * 2**20),
        name="finish",
    )(counts, index, low, side, layer_out, *grads)
    return (layer_out[:, None], jnp.transpose(patch_out, (0, 2, 1, 3)), *grads, s0, s1, s2, s3)


def solution(mesh):
    strips = lambda n: P(None, AXES, *([None] * n))
    rows, row = P(AXES, None), P(AXES)
    body = one_slice if tuple(mesh.shape.values()) == (2, 16) else any_slice
    return jax.shard_map(
        body,
        mesh=mesh,
        in_specs=(strips(2), strips(1), strips(0), rows, rows, rows, rows, row, row, row, row, strips(2)),
        out_specs=(strips(2), strips(2), rows, rows, rows, rows, row, row, row, row),
        check_vma=False,
    )
```

```python
import jax
import jax.numpy as jnp
from jax import lax
from jax.experimental import pallas as pl
from jax.experimental.pallas import tpu as pltpu
from jax.sharding import PartitionSpec as P

HEADS = 12
AXES = ("dp", "fsdp")
MASKED = -1000000000.0
EPSILON = 1e-06
F32 = jnp.float32
BF16 = jnp.bfloat16


def norm_forward(features, scaling, offset):
    center = features - jnp.mean(features, axis=-1, keepdims=True)
    inverse = lax.rsqrt(jnp.mean(center * center, axis=-1, keepdims=True) + EPSILON)
    normed = center * inverse
    return (normed * scaling.astype(F32) + offset.astype(F32), normed, inverse)


def norm_backward(upstream, normed, inverse, scaling):
    through = upstream * scaling.astype(F32)
    inward = inverse * (
        through
        - jnp.mean(through, axis=-1, keepdims=True)
        - normed * jnp.mean(through * normed, axis=-1, keepdims=True)
    )
    return (inward, jnp.sum(upstream * normed, axis=0), jnp.sum(upstream, axis=0))


def sums(equation, left, right):
    return jnp.einsum(equation, left, right, preferred_element_type=F32)


def layer(weights, patches, indices, counts, cotangent):
    qkv_full, out_full, up_full, down_full, first_gain, first_shift, second_gain, second_shift = weights
    strips, visible, patch_count = (indices.shape[0], indices.shape[1], patches.shape[1])
    width = out_full.shape[1]
    rows = strips * visible
    heads = (strips, visible, HEADS, width // HEADS)
    scale = (width // HEADS) ** (-0.5)
    present = jnp.arange(visible)[None, :] < counts[:, None]
    onehot = ((indices[:, :, None] == jnp.arange(patch_count)[None, None, :]) & present[:, :, None]).astype(BF16)
    inputs = sums("bvp,bpd->bvd", onehot, patches).reshape(rows, width)
    first_norm, first_normed, first_inverse = norm_forward(inputs, first_gain, first_shift)
    first_low = first_norm.astype(BF16)
    projected = jnp.dot(first_low, qkv_full, preferred_element_type=F32).astype(BF16)
    queries = projected[:, :width].reshape(heads)
    keys = projected[:, width : 2 * width].reshape(heads)
    values = projected[:, 2 * width :].reshape(heads)
    scores = sums("bqhe,bkhe->bhqk", queries, keys) * scale
    scores = jnp.where(present[:, None, None, :], scores, MASKED)
    attention = jax.nn.softmax(scores, axis=-1)
    attention_low = attention.astype(BF16)
    mixed = sums("bhqk,bkhe->bqhe", attention_low, values).astype(BF16).reshape(rows, width)
    middle = inputs + jnp.dot(mixed, out_full, preferred_element_type=F32)
    second_norm, second_normed, second_inverse = norm_forward(middle, second_gain, second_shift)
    second_low = second_norm.astype(BF16)
    hidden_pre = jnp.dot(second_low, up_full, preferred_element_type=F32)
    hidden, gelu_pull = jax.vjp(lambda v: jax.nn.gelu(v, approximate=False), hidden_pre)
    hidden_low = hidden.astype(BF16)
    branch = jnp.dot(hidden_low, down_full, preferred_element_type=F32)
    live = present.reshape(rows, 1)
    output = ((middle + branch) * live.astype(F32)).reshape(strips, visible, width)

    upstream = cotangent.reshape(rows, width) * live.astype(BF16)
    down_grad = sums("rf,rd->fd", hidden_low, upstream)
    pre_low = gelu_pull(sums("rd,fd->rf", upstream, down_full))[0].astype(BF16)
    up_grad = sums("rf,rd->fd", second_low, pre_low)
    second_back = sums("rd,fd->rf", pre_low, up_full)
    inward, second_gain_grad, second_shift_grad = norm_backward(second_back, second_normed, second_inverse, second_gain)
    middle_grad = upstream.astype(F32) + inward
    middle_low = middle_grad.astype(BF16)
    out_grad = sums("rf,rd->fd", mixed, middle_low)
    mixed_grad = sums("rd,fd->rf", middle_low, out_full).astype(BF16).reshape(heads)
    prob_grad = sums("bqhe,bkhe->bhqk", mixed_grad, values)
    value_grad = sums("bhqk,bqhe->bkhe", attention_low, mixed_grad)
    score_low = (attention * (prob_grad - jnp.sum(attention * prob_grad, axis=-1, keepdims=True))).astype(BF16)
    query_grad = sums("bhqk,bkhe->bqhe", score_low, keys) * scale
    key_grad = sums("bhqk,bqhe->bkhe", score_low, queries) * scale
    projected_grad = jnp.concatenate([g.reshape(rows, width) for g in (query_grad, key_grad, value_grad)], axis=1).astype(BF16)
    qkv_grad = sums("rf,rd->fd", first_low, projected_grad)
    first_back = sums("rd,fd->rf", projected_grad, qkv_full)
    inward, first_gain_grad, first_shift_grad = norm_backward(first_back, first_normed, first_inverse, first_gain)
    input_low = (middle_grad + inward).astype(BF16).reshape(strips, visible, width)
    patch_part = sums("bvp,bvd->bpd", onehot, input_low)
    gradients = (qkv_grad, out_grad, up_grad, down_grad, first_gain_grad, first_shift_grad, second_gain_grad, second_shift_grad)
    return (output, gradients, patch_part)


def any_slice(patches, visible_index, visible_count, *rest):
    weights, cotangent = rest[:-1], rest[-1]
    whole = [lax.all_gather(w, AXES, axis=0, tiled=True) for w in weights]
    micro, strips = patches.shape[:2]
    flat = lambda a: a.reshape((micro * strips,) + a.shape[2:])
    output, gradients, patch_part = layer(whole, flat(patches), flat(visible_index), flat(visible_count), flat(cotangent))
    shares = [lax.psum_scatter(g, AXES, scatter_dimension=0, tiled=True) for g in gradients]
    back = lambda a: a.reshape((micro, strips) + a.shape[1:])
    return (back(output), back(patch_part), *shares)


MESH = pl.DeviceIdType.MESH
EXT = 128
ALL = slice(None)


def coords():
    y = lax.axis_index("dp")
    f = lax.axis_index("fsdp")
    return y, f // 4, (f // 2) % 2, f % 2


def device(y, z, x, c):
    return (y, z * 4 + x * 2 + c)


def other(z, dz):
    if dz == 0:
        return z
    if dz == 1:
        return z + 1 - 2 * (z % 2)
    if dz == 2:
        return (z + 2) % 4
    return 3 - z


def at_z(z):
    return (z // 2, z % 2)


class Round:
    def __init__(self, i, ref, lead, start, width, first):
        self.i, self.ref, self.lead, self.start, self.width = i, ref, lead, start, width
        self.halves = (pl.ds(start, first), pl.ds(start + first, width - first))
        self.cols = pl.ds(start, width)
        self.local = pl.ds(0, first), pl.ds(0, width - first)

    def at(self, par):
        def block(y, z, x, cols=None):
            before, after = self.lead(par)
            return self.ref.at[before + (y,) + z + (x,) + after + (ALL, self.cols if cols is None else cols)]

        return block


def piece(n):
    return lambda par: ((n + par,), ())


def part(n, step=1):
    return lambda par: ((), (n + step * par,))


def gather_rounds(w0, w1, wd):
    return [
        Round(0, w0, piece(0), 0, 384 + EXT, 256),
        Round(1, w1, piece(0), 0, 384, 256),
        Round(2, w0, piece(0), 384 + EXT, 384, 128),
        Round(3, w1, piece(0), 384, 384, 128),
        Round(4, w1, piece(2), 0, 768, 384),
        Round(5, w1, piece(4), 0, 768, 384),
        Round(6, wd, part(0, 2), 0, 768, 384),
        Round(7, wd, part(1, 2), 0, 384, 256),
        Round(8, wd, part(1, 2), 384, 384, 128),
    ]


def scatter_rounds(w1, gd):
    return [
        Round(0, gd, part(0, 2), 0, 768, 384),
        Round(1, gd, part(1, 2), 0, 768, 384),
        Round(2, w1, piece(2), 0, 768, 384),
        Round(3, w1, piece(4), 0, 768, 384),
        Round(4, gd, part(2), 0, 512, 256),
        Round(5, gd, part(0), 0, 512, 256),
        Round(6, gd, part(2), 512, 256, 128),
        Round(7, gd, part(0), 512, 256, 128),
    ]


class Peers:
    def __init__(self, place, rounds, sems):
        y, z, x, c = self.place = place
        self.rounds, self.sems = rounds, sems
        self.all_z, self.pair, self.odd = (ALL, ALL), (ALL, z % 2), (ALL, 1 - z % 2)
        self.x_side, self.y_side = device(y, z, 1 - x, c), device(1 - y, z, x, c)
        self.sibling = device(y, z, x, 1 - c)

    def z_peer(self, dz):
        y, z, x, c = self.place
        return device(y, other(z, dz), x, c)

    def copy(self, send, recv, j, src, dst, to):
        sent, got = self.sems
        return pltpu.make_async_remote_copy(
            src_ref=src, dst_ref=dst, send_sem=sent.at[j, send], recv_sem=got.at[j, recv], device_id=to, device_id_type=MESH
        )


class Gather(Peers):
    def same(self, send, recv, j, ref, to):
        return self.copy(send, recv, j, ref, ref, to)

    def at(self, j, par=None):
        return self.rounds[j].at(self.place[3] if par is None else par)

    def z(self, j, dz, there=0):
        y, z, x, c = self.place
        return self.same(dz - 1, dz - 1, j, self.at(j)(y, at_z(other(z, there)), x), self.z_peer(dz))

    def side(self, j, dz, axis):
        y, z, x, c = self.place
        ref = self.at(j)(y, at_z(other(z, dz)), x)
        if axis == "x":
            return self.same(3, 3 + dz % 2, j, ref, self.x_side)
        return self.same(3, 5 + dz % 2, j, ref, self.y_side)

    def sides_in(self, j, odd, axis):
        y, z, x, c = self.place
        zz = self.odd if odd else self.pair
        if axis == "x":
            return self.same(3, 3 + odd, j, self.at(j)(y, zz, 1 - x), self.x_side)
        return self.same(3, 5 + odd, j, self.at(j)(1 - y, zz, x), self.y_side)

    def diag(self, j, half, there=False):
        y, z, x, c = self.place
        cols = self.rounds[j].halves[half]
        yy = 1 - y if there or half == 1 else y
        xx = 1 - x if there or half == 0 else x
        return self.same(4, 7 + half, j, self.at(j)(yy, self.pair, xx, cols), self.y_side if half == 0 else self.x_side)

    def turn(self, j, there=False):
        y, z, x, c = self.place
        return self.same(4, 9, j, self.at(j)(1 - y, self.odd if there else self.pair, 1 - x), self.z_peer(1))

    def down(self, j, q):
        y, z, x, c = self.place
        yy = y if q < 2 else 1 - y
        xx = x if q in (0, 2) else 1 - x
        zz = self.all_z if q < 3 else self.pair if q == 3 else self.odd
        return self.same(5, 10, j, self.at(j)(yy, zz, xx), self.sibling)

    def downs(self, j, par):
        return self.same(5, 10, j, self.at(j, par)(ALL, self.all_z, ALL), self.sibling)

    def begin(self, j):
        for dz in (1, 2, 3):
            self.z(j, dz).start()

    def own(self, j):
        self.side(j, 0, "x").start()
        self.side(j, 0, "y").start()

    def forward(self, j):
        for dz in (1, 2, 3):
            self.z(j, dz, dz).wait_recv()
            self.side(j, dz, "x").start()
            self.side(j, dz, "y").start()
        self.down(j, 0).start()

    def cross(self, j):
        for half, axis in enumerate(("x", "y")):
            self.sides_in(j, 0, axis).wait_recv()
            self.diag(j, half).start()
        for half, axis in enumerate(("x", "y")):
            self.sides_in(j, 1, axis).wait_recv()
            self.down(j, 1 + half).start()

    def finish(self, j):
        self.diag(j, 0, True).wait_recv()
        self.diag(j, 1, True).wait_recv()
        self.turn(j).start()
        self.down(j, 3).start()

    def last(self, j):
        self.turn(j, True).wait_recv()
        self.down(j, 4).start()

    def arrive(self, j):
        self.downs(j, 1 - self.place[3]).wait_recv()

    def sent(self, j):
        y, z, x, c = self.place
        for dz in (1, 2, 3):
            self.z(j, dz).wait_send()
        self.same(3, 3, j, self.at(j)(y, self.all_z, ALL), self.x_side).wait_send()
        self.same(4, 7, j, self.at(j)(y, self.all_z, x), self.y_side).wait_send()
        self.downs(j, c).wait_send()


def add_to(own, got):
    own[...] = (own[...].astype(F32) + got[...].astype(F32)).astype(BF16)


class Scatter(Peers):
    def __init__(self, place, rounds, bufs, sems, free):
        super().__init__(place, rounds, sems)
        self.bufs, self.free = bufs, free

    def at(self, j, par=None):
        return self.rounds[j].at(self.place[3] if par is None else par)

    def a(self, j):
        return self.copy(0, 0, j, self.at(j, 1 - self.place[3])(ALL, self.all_z, ALL), self.bufs["a"](j), self.sibling)

    def turn(self, j):
        y, z, x, c = self.place
        return self.copy(1, 1, j, self.at(j)(1 - y, self.odd, 1 - x), self.bufs["t"](j), self.z_peer(1))

    def diag(self, j, half):
        y, z, x, c = self.place
        cols = self.rounds[j].halves[half]
        src = self.at(j)(1 - y, self.pair, 1 - x, cols)
        return self.copy(1, 2 + half, j, src, self.bufs["g"](j, half), self.y_side if half == 0 else self.x_side)

    def side(self, j, k, axis):
        y, z, x, c = self.place
        zz = self.pair if k else self.odd
        if axis == "x":
            return self.copy(2, 4 + k, j, self.at(j)(y, zz, 1 - x), self.bufs["x"](j, k), self.x_side)
        return self.copy(2, 6 + k, j, self.at(j)(1 - y, zz, x), self.bufs["y"](j, k), self.y_side)

    def d(self, j, dz):
        y, z, x, c = self.place
        return self.copy(3, 8, j, self.at(j)(y, at_z(other(z, dz)), x), self.bufs["d"](j).at[dz - 1], self.z_peer(dz))

    def ds(self, j):
        return self.copy(3, 8, j, self.bufs["d"](j), self.bufs["d"](j), self.z_peer(1))

    def e(self, j):
        return self.copy(4, 9, j, self.bufs["f"](j).at[1 - self.place[3]], self.bufs["e"](j), self.sibling)

    def begin(self, j):
        if j >= 2:
            pl.semaphore_wait(self.free.at[j % 2], 1)
        self.a(j).start()

    def add_a(self, j):
        self.a(j).wait_recv()
        at, got = self.at(j), self.bufs["a"](j)

        @pl.loop(0, 16)
        def _(i):
            y, z, x = i // 8, at_z((i // 2) % 4), i % 2
            add_to(at(y, z, x), got.at[(y,) + z + (x,)])

        self.turn(j).start()
        self.side(j, 0, "x").start()
        self.side(j, 0, "y").start()
        if j < len(self.rounds) - 2:
            pl.semaphore_signal(self.free.at[j % 2], inc=1, device_id=self.sibling, device_id_type=MESH)

    def add_t(self, j):
        y, z, x, c = self.place
        self.turn(j).wait_recv()
        for h in range(2):
            add_to(self.at(j)(1 - y, (h, z % 2), 1 - x), self.bufs["t"](j).at[h])
        self.diag(j, 0).start()
        self.diag(j, 1).start()

    def add_g(self, j):
        y, z, x, c = self.place
        first, second = self.rounds[j].halves
        self.diag(j, 0).wait_recv()
        for h in range(2):
            add_to(self.at(j)(y, (h, z % 2), 1 - x, first), self.bufs["g"](j, 0).at[h])
        self.side(j, 1, "x").start()
        self.diag(j, 1).wait_recv()
        for h in range(2):
            add_to(self.at(j)(1 - y, (h, z % 2), x, second), self.bufs["g"](j, 1).at[h])
        self.side(j, 1, "y").start()

    def add_s(self, j):
        y, z, x, c = self.place
        for k in range(2):
            self.side(j, k, "x").wait_recv()
            self.side(j, k, "y").wait_recv()
            low = z % 2 if k else 1 - z % 2

            @pl.loop(0, 2)
            def _(h):
                own = self.at(j)(y, (h, low), x)
                both = self.bufs["x"](j, k)[h].astype(F32) + self.bufs["y"](j, k)[h].astype(F32)
                own[...] = (own[...].astype(F32) + both).astype(BF16)

        for dz in (1, 2, 3):
            self.d(j, dz).start()

    def add_d(self, j):
        y, z, x, c = self.place
        self.ds(j).wait_recv()
        total = self.at(j)(y, at_z(z), x)[...].astype(F32)
        for dz in (1, 2, 3):
            total = total + self.bufs["d"](j)[dz - 1].astype(F32)
        out = self.bufs["f"](j)
        if j < 2:
            out[...] = total
        else:
            out[0] = total[:24]
            out[1] = total[24:]
            self.e(j).start()

    def sent(self, j):
        y, z, x, c = self.place
        at = self.at(j)
        self.a(j).wait_send()
        self.copy(1, 1, j, at(y, self.all_z, x), at(y, self.all_z, x), self.z_peer(1)).wait_send()
        self.copy(2, 4, j, at(y, self.all_z, ALL), at(y, self.all_z, ALL), self.x_side).wait_send()
        self.ds(j).wait_send()
        if j > 1:
            self.e(j).wait_send()


class Total(Peers):
    def __init__(self, place, side, send, recv):
        super().__init__(place, None, (send, recv))
        self.side = side

    def step(self, i):
        y, z, x, c = self.place
        if i == 0:
            peers = (self.sibling,)
        elif i == 1:
            peers = tuple(self.z_peer(dz) for dz in (1, 2, 3))
        else:
            peers = (self.x_side, self.y_side, device(1 - y, z, 1 - x, c))
        first = (3, 4, 7)[i]
        return [self.copy(0, 0, i, self.side.at[i], self.side.at[first + n], peer) for n, peer in enumerate(peers)]

    def whole(self, i):
        got = self.side.at[pl.ds((3, 4, 7)[i], 3 if i else 1)]
        return self.copy(0, 0, i, got, got, self.sibling)

    def begin(self):
        self.step(0)[0].start()

    def add(self, i):
        self.whole(i).wait_recv()
        total = self.side[i]
        for n in ((3,), (4, 5, 6), (7, 8, 9))[i]:
            total = total + self.side[n]
        if i < 2:
            self.side[i + 1] = total
            for copy in self.step(i + 1):
                copy.start()
        return total

    def sent(self):
        for i in range(3):
            self.whole(i).wait_send()


def sem_shapes(rounds, sends, receives):
    return [pltpu.SemaphoreType.DMA((rounds, n)) for n in (sends, receives)]


def mm(a, b):
    return lax.dot_general(a, b, (((1,), (0,)), ((), ())), preferred_element_type=F32)


def mt(a, b):
    return lax.dot_general(a, b, (((1,), (1,)), ((), ())), preferred_element_type=F32)


def tm(a, b):
    return lax.dot_general(a, b, (((0,), (0,)), ((), ())), preferred_element_type=F32)


def lanes(i, n):
    return pl.ds(pl.multiple_of(i * n, 128), n)


def rows_at(i, n):
    return pl.ds(pl.multiple_of(i * n, 16), n)


def normal(v):
    center = v - jnp.mean(v, axis=-1, keepdims=True)
    inverse = lax.rsqrt(jnp.mean(center * center, axis=-1, keepdims=True) + EPSILON)
    return center * inverse, inverse


def gelu_parts(v):
    cdf = 0.5 * lax.erf(v * (0.5**0.5)) + 0.5
    return v * cdf, cdf + v * jnp.exp2(v * v * (-0.5 * 1.4426950408889634) - 1.3257480647361593)


class Layer:
    def __init__(self, r):
        self.__dict__.update(r)

    def weight(self, p, start=0, width=768):
        if p < 2:
            return self.w0[p, :, :, :, :, :, pl.ds(EXT + start, width)].reshape(768, width)
        return self.w1[p - 2, :, :, :, :, :, pl.ds(start, width)].reshape(768, width)

    def live(self, s, shape, axis):
        return lax.broadcasted_iota(jnp.int32, shape, axis) < self.count[s]

    def take(self):
        @pl.loop(0, 2)
        def _(s):
            row = lax.broadcasted_iota(jnp.int32, (1058, 400), 0)
            hot = (row == 2 * self.index[s] + s) & self.live(s, (1058, 400), 1)
            got = tm(hot.astype(F32).astype(BF16), self.pool[...].reshape(1058, 768))
            self.inputs[rows_at(s, 400), :] = got.astype(BF16)
            self.ups[s] = jnp.where(self.live(s, (400, 768), 0), self.ups[s], jnp.zeros((), BF16))

    def gains(self):
        side = self.w0[0, :, :, :, :, :, pl.ds(0, EXT)].reshape(768, EXT).astype(F32)
        self.gain[...] = side.T[0:8]

    def first(self):
        @pl.loop(0, 2)
        def _(s):
            normed, _ = normal(self.inputs[rows_at(s, 400), :].astype(F32))
            self.first_low[rows_at(s, 400), :] = (normed * self.gain[0:1] + self.gain[1:2]).astype(BF16)

    def project(self, half, pieces):
        start = 384 * half
        w = jnp.concatenate([self.weight(p, start, 384) for p in pieces], axis=1)

        got = mm(self.first_low[...], w).astype(BF16)
        for i, p in enumerate(pieces):
            self.proj[:, pl.ds(768 * p + start, 384)] = got[:, 384 * i : 384 * (i + 1)]

    def last_keys(self, s, shape, axis):
        return lax.broadcasted_iota(jnp.int32, shape, axis) + 384 < self.count[s]

    def attend(self, i):
        s, t = i % 2, i // 2
        rows = rows_at(s, 400)
        q, k, v = (self.proj[rows, lanes(6 * p + t, 128)] for p in range(3))
        lane = lax.broadcasted_iota(jnp.int32, (400, 128), 1)
        alive = self.last_keys(s, (400, 16), 1)
        halves = (lane < 64, lane >= 64)
        eighth = q * jnp.asarray(0.125, BF16)
        scores = [mt(jnp.where(mine, eighth, jnp.zeros((), BF16)), k) for mine in halves]
        scores = jnp.concatenate([jnp.concatenate([x[:, :384], jnp.where(alive, x[:, 384:], MASKED)], axis=1) for x in scores], axis=0)
        top = jnp.max(scores, axis=1, keepdims=True)
        e = jnp.exp(scores - top)
        total = jnp.sum(e, axis=1, keepdims=True)
        e = e.astype(BF16)
        mixed = jnp.concatenate([mm(e[400 * h : 400 * (h + 1)], v) for h in range(2)], axis=0) * (1.0 / total)
        self.mixed[rows, lanes(t, 128)] = jnp.where(halves[0], mixed[:400], mixed[400:]).astype(BF16)
        logs = top + jnp.log(total)
        stat = self.stat[s, pl.ds(0, 400), :]
        for h in range(2):
            stat = jnp.where(lane == 2 * t + h, logs[400 * h : 400 * (h + 1)], stat)
        self.stat[s, pl.ds(0, 400), :] = stat

    def turn_stat(self):
        for s in range(2):
            self.turned[s] = self.stat[s].T[0:16]

    def mix(self):
        w = self.weight(3)
        @pl.loop(0, 2)
        def _(s):
            rows = rows_at(s, 400)
            middle = self.inputs[rows, :].astype(F32) + mm(self.mixed[rows, :], w)
            self.mid[s, pl.ds(0, 400), :] = middle
            normed, _ = normal(middle)
            self.second_low[rows, :] = (normed * self.gain[2:3] + self.gain[3:4]).astype(BF16)

    def hide(self, p):
        w = self.weight(4 + p)
        cols = pl.ds(768 * p, 768)
        for s in range(2):
            rows = pl.ds(400 * s, 400)
            act, slope = gelu_parts(mm(self.second_low[rows, :], w))
            self.hidden[rows, cols] = act.astype(BF16)
            self.slope[rows, cols] = slope.astype(BF16)

    def down_terms(self, chunks):
        left = jnp.concatenate([self.hidden[:, pl.ds(384 * i, 384)] for i in chunks], axis=1)
        g = tm(left, self.ups[...].reshape(800, 768)).astype(BF16)
        for n, i in enumerate(chunks):
            self.gd[i // 4, (i % 4) // 2, i % 2] = g[384 * n : 384 * (n + 1)].reshape(2, 4, 48, 768)

    def branch(self, n, stage):
        w = self.wd[:, :, :, :, :, :, lanes(n, 256)].reshape(3072, 256)
        for s in range(2):
            got = mm(self.hidden[pl.ds(400 * s, 400), :], w)
            got = (got + self.mid[s, pl.ds(0, 400), lanes(n, 256)]) * self.live(s, (400, 256), 0).astype(F32)
            stage[s] = got

    def hide_back(self, p):
        w = self.wd[p // 2, p % 2].reshape(768, 768)
        cols = pl.ds(768 * p, 768)
        for s in range(2):
            rows = pl.ds(400 * s, 400)
            self.slope[rows, cols] = (mt(self.ups[s], w) * self.slope[rows, cols].astype(F32)).astype(BF16)

    def up_terms(self, p):
        g = tm(self.second_low[...], self.slope[:, pl.ds(768 * p, 768)])
        self.g1[2 + p] = g.astype(BF16).reshape(2, 2, 2, 2, 48, 768)

    def second_back(self):
        self.vec[0] = jnp.zeros((8, 768), F32)

        @pl.loop(0, 2)
        def _(s):
            w = jnp.concatenate([self.weight(4 + p) for p in range(4)], axis=1)
            back = mt(self.slope[rows_at(s, 400), :], w)
            normed, inverse = normal(self.mid[s, pl.ds(0, 400), :])
            inward, dg, db = self.norm_back(back, normed, inverse, self.gain[2:3])
            self.ups[s] = (self.ups[s].astype(F32) + inward).astype(BF16)
            self.vec[0, 2:3] += dg
            self.vec[0, 3:4] += db

    def norm_back(self, back, normed, inverse, gain):
        through = back * gain
        inward = inverse * (
            through
            - jnp.mean(through, axis=-1, keepdims=True)
            - normed * jnp.mean(through * normed, axis=-1, keepdims=True)
        )
        return inward, jnp.sum(back * normed, axis=0, keepdims=True), jnp.sum(back, axis=0, keepdims=True)

    def mix_back(self):
        w = self.weight(3)
        self.second_low[...] = mt(self.ups[...].reshape(800, 768), w).astype(BF16)

    def out_terms(self):
        g = tm(self.mixed[...], self.ups[...].reshape(800, 768))
        self.gd[:, :, :, :, 3] = g.astype(BF16).reshape(2, 2, 2, 2, 48, 768)

    def attend_back(self, i):
        s, t = i % 2, i // 2
        rows = rows_at(s, 400)
        q, k, v = (self.proj[rows, lanes(6 * p + t, 128)] for p in range(3))
        do = self.second_low[rows, lanes(t, 128)]
        first_half = lax.broadcasted_iota(jnp.int32, (400, 128), 1) < 64
        alive = self.last_keys(s, (16, 400), 0)
        zero = jnp.zeros((), BF16)
        halves = (first_half, ~first_half)
        eighth = k * jnp.asarray(0.125, BF16)
        scores = [mt(jnp.where(mine, eighth, zero), q) for mine in halves]
        shares = []
        for h in range(2):
            p = jnp.exp(scores[h] - self.turned[s, pl.ds(2 * t + h, 1), pl.ds(0, 400)])
            shares.append(jnp.concatenate([p[:384], jnp.where(alive, p[384:], 0.0)], axis=0))
        dv = mm(jnp.concatenate([p.astype(BF16) for p in shares], axis=0), do)
        back = [mt(jnp.where(mine, v, zero), do) for mine in halves]
        ds = [(p * (dp - jnp.sum(p * dp, axis=0, keepdims=True))).astype(BF16) for p, dp in zip(shares, back)]
        dk = mm(jnp.concatenate(ds, axis=0), q)
        dq = [tm(x, k) for x in ds]
        for i, (first, second, scale) in enumerate(((dq[0], dq[1], 0.125), (dk[:400], dk[400:], 0.125), (dv[:400], dv[400:], 1.0))):
            g = jnp.where(first_half, first, second) * scale
            self.proj[rows, lanes(6 * i + t, 128)] = g.astype(BF16)

    def project_terms(self, start, width):
        right = jnp.concatenate([self.proj[:, pl.ds(768 * p + start, width)] for p in range(3)], axis=1)
        g = tm(self.first_low[...], right).astype(BF16)
        for p in range(3):
            self.gd[:, :, :, :, p, :, pl.ds(start, width)] = g[:, width * p : width * (p + 1)].reshape(2, 2, 2, 2, 48, width)

    def first_back(self, s):
        rows = pl.ds(400 * s, 400)
        back = mt(self.proj[rows, :], jnp.concatenate([self.weight(p) for p in range(3)], axis=1))
        normed, inverse = normal(self.inputs[rows, :].astype(F32))
        inward, dg, db = self.norm_back(back, normed, inverse, self.gain[0:1])
        self.ups[s] = (self.ups[s].astype(F32) + inward).astype(BF16)
        self.vec[0, 0:1] += dg
        self.vec[0, 1:2] += db


W_SHAPES = ((2, 2, 2, 2, 2, 48, 768 + EXT), (6, 2, 2, 2, 2, 48, 768), (2, 2, 2, 2, 4, 48, 768))


def greet(place):
    y, z, x, c = place
    barrier = pltpu.get_barrier_semaphore()
    peers = [device(y, z, x, 1 - c), device(y, z, 1 - x, c), device(1 - y, z, x, c)]
    peers += [device(y, other(z, dz), x, c) for dz in (1, 2, 3)] + [device(1 - y, z, 1 - x, c)]
    for peer in peers:
        pl.semaphore_signal(barrier, inc=1, device_id=peer, device_id_type=MESH)
    return lambda: pl.semaphore_wait(barrier, len(peers))


class Shards:
    def __init__(self, place, own, weights, sent, got, sems):
        self.place, self.own, self.weights = place, own, weights
        self.sent, self.got, self.sems = sent, got, sems

    def width(self, j):
        return 768 + EXT if j == 0 else 768

    def piece(self, p):
        qkv, out, up, _, ext = self.own
        if p == 3:
            return out[...].astype(F32)
        if p > 3:
            return up[:, 768 * (p - 4) : 768 * (p - 3)].astype(F32)
        v = qkv[:, 768 * p : 768 * (p + 1)].astype(F32)
        return jnp.concatenate([ext[0:24], v], axis=1) if p < 2 else v

    def copy(self, j):
        y, z, x, c = self.place
        cols = pl.ds(0, self.width(j))
        return pltpu.make_async_remote_copy(
            src_ref=self.sent.at[j, :, cols],
            dst_ref=self.got.at[j, :, cols],
            send_sem=self.sems.at[0, j],
            recv_sem=self.sems.at[1, j],
            device_id=device(y, z, x, 1 - c),
            device_id_type=MESH,
        )

    def stage(self, j):
        c = self.place[3]
        self.sent[j, :, pl.ds(0, self.width(j))] = jnp.where(c == 0, self.piece(2 * j + 1), self.piece(2 * j))

    def build(self, j):
        y, z, x, c = self.place
        mine = jnp.where(c == 0, self.piece(2 * j), self.piece(2 * j + 1))
        self.copy(j).wait_recv()
        got = self.got[j, :, pl.ds(0, self.width(j))]
        both = jnp.where(c == 0, jnp.concatenate([mine, got], axis=0), jnp.concatenate([got, mine], axis=0))
        if j == 0:
            self.weights[0][c, y, z // 2, z % 2, x] = both.astype(BF16)
        else:
            self.weights[1][2 * (j - 1) + c, y, z // 2, z % 2, x] = both.astype(BF16)

    def close(self):
        for j in range(4):
            self.copy(j).wait_send()

    def build_down(self):
        y, z, x, c = self.place
        for k in (0, 1):
            self.weights[2][y, z // 2, z % 2, x, 2 * c + k] = self.own[3][48 * k : 48 * (k + 1), :]


class Refs:
    pass


def bf16(*shape):
    return pltpu.VMEM(shape, BF16)


def f32(*shape):
    return pltpu.VMEM(shape, F32)


INS = ["count", "index", "patches", "cot", "qkv", "out", "up", "down", "gain_1", "shift_1", "gain_2", "shift_2"]
OUTS = ["layer_out", "low_out", "o_qkv", "o_out", "o_up", "o_down", "o_side"]
SCRATCH = dict(
    w0=bf16(*W_SHAPES[0]), w1=bf16(*W_SHAPES[1]), wd=bf16(*W_SHAPES[2]), gd=bf16(*W_SHAPES[2]),
    inputs=bf16(800, 768), first_low=bf16(800, 768), proj=bf16(800, 2304), mixed=bf16(800, 768),
    mid=f32(2, 400, 768), second_low=bf16(800, 768), hidden=bf16(800, 3072), slope=bf16(800, 3072),
    ups=bf16(2, 400, 768), gain=f32(8, 768), pool=bf16(529, 2, 768), stage=f32(2, 400, 256),
    stat=f32(2, 512, 128), turn=f32(EXT, EXT), turned=f32(2, 16, 512), vec=f32(10, 8, 768),
    s0=f32(4, 24, 768 + EXT), r0=f32(4, 24, 768 + EXT), ra=bf16(2, 2, 2, 2, 2, 48, 768),
    rt=bf16(4, 2, 48, 768), rx=bf16(4, 2, 2, 48, 768), ry=bf16(4, 2, 2, 48, 768), rg=bf16(4, 2, 2, 48, 384), rd=bf16(4, 3, 48, 768),
    ht=bf16(4, 2, 48, 512), hx=bf16(4, 2, 2, 48, 512), hy=bf16(4, 2, 2, 48, 512), hg=bf16(4, 2, 2, 48, 256), hd=bf16(4, 3, 48, 512),
    fd=f32(2, 48, 768), fs=f32(6, 2, 24, 768), re=f32(6, 24, 768),
    free=pltpu.SemaphoreType.REGULAR((2,)), pair=pltpu.SemaphoreType.DMA((2, 4)), local=pltpu.SemaphoreType.DMA((4,)), vs=pltpu.SemaphoreType.DMA((3, 1)), vr=pltpu.SemaphoreType.DMA((3, 1)),
)


def make_scatter(place, R, sems):
    rounds = scatter_rounds(R.w1, R.gd)

    def pick(full, half):
        return lambda j, *at: full.at[(j,) + at] if j < 4 else half.at[(j - 4,) + at + (ALL, ALL, pl.ds(0, rounds[j].width))]

    def corner(j, half):
        cols = rounds[j].local[half]
        return R.rg.at[j, half] if j < 4 else R.hg.at[j - 4, half, :, :, cols]

    bufs = dict(
        a=lambda j: R.ra.at[j % 2, :, :, :, :, :, pl.ds(0, rounds[j].width)],
        t=pick(R.rt, R.ht),
        x=pick(R.rx, R.hx),
        y=pick(R.ry, R.hy),
        g=corner,
        d=pick(R.rd, R.hd),
        f=lambda j: R.fd.at[j] if j < 2 else R.fs.at[j - 2, :, :, pl.ds(0, rounds[j].width)],
        e=lambda j: R.re.at[j - 2, :, pl.ds(0, rounds[j].width)],
    )
    return Scatter(place, rounds, bufs, sems, R.free)


def mega(*refs):
    names = INS + OUTS + list(SCRATCH)
    r = dict(zip(names, refs))
    n = len(names)
    m = n + 2
    R = Refs()
    R.__dict__.update(r)
    R.g1 = R.w1
    place = coords()
    c = place[3]
    weights = (R.w0, R.w1, R.wd)
    cot_copy = pltpu.make_async_copy(R.cot, R.ups, R.local.at[0])
    cot_copy.start()
    patch_in = pltpu.make_async_copy(R.patches, R.pool, R.local.at[3])
    patch_in.start()
    met = greet(place)
    shards = Shards(place, (R.qkv, R.out, R.up, R.down, R.turn), weights, R.s0, R.r0, R.pair)
    g = Gather(place, gather_rounds(*weights), refs[n:m])
    v = Total(place, R.vec, R.vs, R.vr)

    s = make_scatter(place, R, refs[m:])
    L = Layer(R.__dict__)
    low_copy = pltpu.make_async_copy(R.ups, R.low_out, R.local.at[0])

    out_copies = [
        pltpu.make_async_copy(R.stage, R.layer_out.at[:, :, pl.ds(256 * i, 256)], R.local.at[2]) for i in range(3)
    ]

    def branch(k):
        if k:
            out_copies[k - 1].wait()
        L.branch(k, R.stage)
        out_copies[k].start()

    def start(j):
        g.begin(j)
        g.own(j)

    R.turn[...] = jnp.zeros((EXT, EXT), F32)
    for i, row in enumerate((R.gain_1, R.shift_1, R.gain_2, R.shift_2)):
        R.turn[i : i + 1, 0:24] = row[...].astype(F32)
    R.turn[...] = R.turn[...].T
    for j in range(4):
        shards.stage(j)
    shards.build_down()
    met()
    for j in range(4):
        shards.copy(j).start()
    shards.build(0)
    start(0)
    shards.build(1)
    start(1)
    shards.build(2)
    shards.build(3)
    cot_copy.wait()
    patch_in.wait()
    L.take()

    def over(step, first, last):
        pl.loop(first, last)(step)

    qk, v_only = (0, 1), (2,)

    def close():
        for j in range(9):
            g.sent(j)
        shards.close()

    plan = [
        (g.forward, 0), (g.forward, 1), (g.cross, 0), (start, 2), (g.finish, 0), (g.cross, 1), (start, 3), (g.last, 0),
        (g.forward, 2), (g.finish, 1), (start, 4), (g.arrive, 0), (L.gains,), (L.first,), (L.project, 0, qk),
        (g.forward, 3), (g.cross, 2), (g.last, 1), (start, 5), (g.arrive, 1), (L.project, 0, v_only), (over, L.attend, 0, 2),
        (g.finish, 2), (g.cross, 3), (g.forward, 4), (over, L.attend, 2, 4), (start, 6), (g.last, 2), (g.finish, 3), (over, L.attend, 4, 6),
        (g.arrive, 2), (g.cross, 4), (g.forward, 5), (L.project, 1, qk), (g.last, 3), (g.finish, 4), (start, 7), (start, 8), (g.arrive, 3),
        (L.project, 1, v_only), (over, L.attend, 6, 10), (g.cross, 5), (g.forward, 6), (over, L.attend, 10, 12), (L.mix,), (L.turn_stat,),
        (g.last, 4), (g.finish, 5), (g.forward, 7), (g.arrive, 4), (L.hide, 0), (L.hide, 1), (g.cross, 6), (g.last, 5), (g.forward, 8),
        (L.down_terms, (0, 1)), (g.arrive, 5), (g.cross, 7), (L.hide, 2), (g.finish, 6), (L.hide, 3), (g.cross, 8),
        (L.down_terms, (2, 3)), (g.last, 6), (g.finish, 7), (L.down_terms, (4, 5)), (g.finish, 8), (L.down_terms, (6, 7)),
        (s.begin, 0), (g.last, 7), (g.last, 8), (g.arrive, 6), (g.arrive, 7), (g.arrive, 8), (s.begin, 1), (s.add_a, 0),
        (L.hide_back, 0), (L.hide_back, 1), (s.add_a, 1), (L.hide_back, 2), (L.hide_back, 3),
        (s.add_t, 0), (L.second_back,), (s.add_t, 1), (s.add_g, 0), (close,),
        (L.up_terms, 0), (L.up_terms, 1), (s.begin, 2), (L.up_terms, 2), (s.add_g, 1), (L.up_terms, 3), (s.add_s, 0), (s.add_a, 2), (s.begin, 3),
        (L.mix_back,), (over, L.attend_back, 0, 1), (s.add_s, 1), (s.add_a, 3), (over, L.attend_back, 1, 5), (s.add_t, 2),
        (over, L.attend_back, 5, 8), (s.add_g, 2), (s.add_d, 0), (s.add_d, 1), (s.sent, 0), (s.sent, 1),
        (L.project_terms, 0, 512), (s.add_t, 3), (L.out_terms,), (s.begin, 4), (s.begin, 5), (s.add_s, 2), (over, L.attend_back, 8, 9), (s.add_g, 3), (s.add_a, 4),
        (over, L.attend_back, 9, 10), (s.add_a, 5), (over, L.attend_back, 10, 12), (s.add_t, 4), (s.add_s, 3), (L.project_terms, 512, 256),
        (s.begin, 6), (s.begin, 7), (s.add_t, 5), (s.add_g, 4), (s.add_d, 2), (branch, 0), (s.add_a, 6), (s.add_a, 7), (s.add_g, 5), (L.first_back, 0),
        (s.add_t, 6), (s.add_s, 4), (L.first_back, 1), (v.begin,), (low_copy.start,), (s.add_t, 7), (s.add_g, 6), (s.add_s, 5), (branch, 1),
        (s.add_g, 7), (v.add, 0), (branch, 2), (s.add_s, 6), (s.add_s, 7), (v.add, 1), (s.add_d, 3), (s.add_d, 4), (s.add_d, 5), (s.add_d, 6), (s.add_d, 7),
    ]
    for step, *at in plan:
        step(*at)
    R.o_side[...] = v.add(2)
    targets = {
        2: (R.o_up, 0, R.o_up, 768),
        3: (R.o_up, 1536, R.o_up, 2304),
        4: (R.o_qkv, 1536, R.o_out, 0),
        5: (R.o_qkv, 0, R.o_qkv, 768),
        6: (R.o_qkv, 2048, R.o_out, 512),
        7: (R.o_qkv, 512, R.o_qkv, 1280),
    }
    for j, (even, even_at, odd, odd_at) in targets.items():
        s.e(j).wait_recv()
        own = s.bufs["f"](j)[c]
        got = s.bufs["e"](j)[...]
        even[:, pl.ds(even_at, s.rounds[j].width)] = jnp.where(c == 0, own, got)
        odd[:, pl.ds(odd_at, s.rounds[j].width)] = jnp.where(c == 0, got, own)
    for k in (0, 1):
        R.o_down[48 * k : 48 * (k + 1), :] = R.fd[k]
    for j in range(2, 8):
        s.sent(j)
    v.sent()
    low_copy.wait()
    out_copies[2].wait()


def finish(count, index, low, side, *refs):
    given, patch_out, small, taken, held, (mid, sems) = refs[:5], refs[5], refs[6:10], refs[10:15], refs[15:20], refs[20:]
    to = [pltpu.make_async_copy(a, b, sems.at[2 + i]) for i, (a, b) in enumerate(zip(given, held))]
    back = [pltpu.make_async_copy(a, b, sems.at[7 + i]) for i, (a, b) in enumerate(zip(held, taken))]
    for copy in to:
        copy.start()
    outs = [pltpu.make_async_copy(mid.at[s], patch_out.at[s, :, 0, :], sems.at[s]) for s in range(2)]
    for s in range(2):
        hot = lax.broadcasted_iota(jnp.int32, (529, 400), 0) == index[s]
        hot = hot & (lax.broadcasted_iota(jnp.int32, (529, 400), 1) < count[s])
        mid[s] = mm(hot.astype(F32).astype(BF16), low[s])
        outs[s].start()
    for first, second in zip(to, back):
        first.wait()
        second.start()
    here = (lax.axis_index(AXES[0]) * 16 + lax.axis_index(AXES[1])) * 24
    own = pltpu.roll(side[...], 768 - here, 1)
    for i in range(4):
        small[i][...] = own[i, :24]
    for copy in outs + back:
        copy.wait()


def one_slice(patches, visible_index, visible_count, qkv_weight, out_weight, up_weight, down_weight, attention_gain, attention_shift, feedforward_gain, feedforward_shift, cotangent):
    small = [row.reshape(1, 24) for row in (attention_gain, attention_shift, feedforward_gain, feedforward_shift)]
    whole = pl.BlockSpec(memory_space=pltpu.VMEM)
    anywhere = pl.BlockSpec(memory_space=pl.ANY)
    smem = pl.BlockSpec(memory_space=pltpu.SMEM)
    shapes = ((2, 400, 768), (2, 400, 768), (24, 2304), (24, 768), (24, 3072), (96, 768), (8, 768))
    types = (F32, BF16, F32, F32, F32, F32, F32)
    counts, index = visible_count.reshape(2), visible_index.reshape(2, 1, 400)
    layer_out, low, *grads, side = pl.pallas_call(
        mega,
        out_shape=[jax.ShapeDtypeStruct(*shape) for shape in zip(shapes, types)],
        in_specs=[smem, whole] + [anywhere] * 2 + [whole] * 8,
        out_specs=[anywhere] * 2 + [whole] * 5,
        scratch_shapes=list(SCRATCH.values()) + sem_shapes(9, 6, 11) + sem_shapes(8, 5, 10),
        compiler_params=pltpu.CompilerParams(collective_id=0, has_side_effects=True, vmem_limit_bytes=125 * 2**19),
        name="layer_step",
    )(
        counts,
        index,
        jnp.transpose(patches.reshape(2, 529, 768), (1, 0, 2)),
        cotangent.reshape(2, 400, 768),
        qkv_weight,
        out_weight,
        up_weight,
        down_weight,
        *small,
    )
    results = [jax.ShapeDtypeStruct(shape, F32) for shape in shapes[:1] + shapes[2:6]]
    patch_out, s0, s1, s2, s3, layer_out, *grads = pl.pallas_call(
        finish,
        out_shape=[jax.ShapeDtypeStruct((2, 529, 1, 768), F32), *[jax.ShapeDtypeStruct((24,), F32)] * 4] + results,
        in_specs=[smem] + [whole] * 3 + [anywhere] * 5,
        out_specs=[anywhere] + [whole] * 4 + [anywhere] * 5,
        scratch_shapes=[pltpu.VMEM(a.shape, F32) for a in results] + [f32(2, 529, 768), pltpu.SemaphoreType.DMA((12,))],
        compiler_params=pltpu.CompilerParams(vmem_limit_bytes=62 * 2**20),
        name="finish",
    )(counts, index, low, side, layer_out, *grads)
    return (layer_out[:, None], jnp.transpose(patch_out, (0, 2, 1, 3)), *grads, s0, s1, s2, s3)


def solution(mesh):
    strips = lambda n: P(None, AXES, *([None] * n))
    rows, row = P(AXES, None), P(AXES)
    body = one_slice if tuple(mesh.shape.values()) == (2, 16) else any_slice
    return jax.shard_map(
        body,
        mesh=mesh,
        in_specs=(strips(2), strips(1), strips(0), rows, rows, rows, rows, row, row, row, row, strips(2)),
        out_specs=(strips(2), strips(2), rows, rows, rows, rows, row, row, row, row),
        check_vma=False,
    )
```
